32 devices in a mesh: section: 2 (over core), head: 4 (over z), ctx: 4 (over y, x).
Axes of the slice: x: 2, y: 2, z: 4, core: 2. Of those that a mesh axis runs over, the one named last changes fastest.
Arguments:
- layer_input: bfloat16 [4, 512, 1536], P(None, ('ctx', 'head')), may hold values from -6 to 6
- out_cotangent: bfloat16 [4, 512, 1536], P(None, ('ctx', 'head')), may hold values from -6 to 6
- block_order: int32 [4, 8], replicated, may hold values from 0 to 7, each once within a row
- gain_attn: bfloat16 [2, 1536], P('section', 'ctx'), may hold values from 0.099609375 to 1.8984375
- w_query: bfloat16 [2, 1536, 1536], P('section', 'ctx', 'head'), may hold values from -0.15625 to 0.15625
- w_key: bfloat16 [2, 1536, 768], P('section', 'ctx', 'head'), may hold values from -0.15625 to 0.15625
- w_value: bfloat16 [2, 1536, 768], P('section', 'ctx', 'head'), may hold values from -0.15625 to 0.15625
- w_out: bfloat16 [2, 1536, 1536], P('section', 'head', 'ctx'), may hold values from -0.625 to 0.625
- gain_ffn: bfloat16 [2, 1536], P('section', 'ctx'), may hold values from 0.099609375 to 1.8984375
- w_gate: bfloat16 [2, 1536, 4096], P('section', 'ctx', 'head'), may hold values from -0.15625 to 0.15625
- w_up: bfloat16 [2, 1536, 4096], P('section', 'ctx', 'head'), may hold values from -0.15625 to 0.15625
- w_down: bfloat16 [2, 4096, 1536], P('section', 'head', 'ctx'), may hold values from -0.125 to 0.125
Outputs:
- layer_out: bfloat16 [2, 4, 512, 1536], P('section', None, ('ctx', 'head'))
- in_grad: float32 [2, 4, 512, 1536], P('section', None, ('ctx', 'head'))
- grad_gain_attn: float32 [2, 1536], P('section', 'ctx')
- grad_w_query: float32 [2, 1536, 1536], P('section', 'ctx', 'head')
- grad_w_key: float32 [2, 1536, 768], P('section', 'ctx', 'head')
- grad_w_value: float32 [2, 1536, 768], P('section', 'ctx', 'head')
- grad_w_out: float32 [2, 1536, 1536], P('section', 'head', 'ctx')
- grad_gain_ffn: float32 [2, 1536], P('section', 'ctx')
- grad_w_gate: float32 [2, 1536, 4096], P('section', 'ctx', 'head')
- grad_w_up: float32 [2, 1536, 4096], P('section', 'ctx', 'head')
- grad_w_down: float32 [2, 4096, 1536], P('section', 'head', 'ctx')
The draws below stay inside these ranges and needn't reach their ends.
Inputs may be any that keep to these rules, and one draw needn't show every extreme that they name: `block_order`: row m gives, for each of the 8 stored blocks of sequence m, its block of positions; each row is a permutation.
All inputs are finite; a program needn't handle non-finite values.
Results may differ from the reference program's by a relative error of at most 0.035.
Values may be sent and summed in bfloat16 or wider, within the bound.
No kernel may reach another device: no remote copies, remote signals or barrier semaphores. Data moves between devices by JAX's collectives and lax.ppermute only.
A program may use at most 128 MiB of HBM per device.

```python
import jax
import jax.numpy as jnp
from jax import lax

D = 1536
HEADS = 16
KV_HEADS = 8
HEAD_DIM = 96
FF = 4096
SEQ_DEV = 128
MICRO = 4
SEQ = 512
BLOCKS = 8
QW = 1536
KW = 768


def steps_of(stream_key, shape, split, least, top_value):
    def one(axis_at, blocks):
        heights = jax.random.uniform(jax.random.fold_in(jax.random.fold_in(stream_key, 6), axis_at), (blocks,), jnp.float32, least / len(split), top_value / len(split))
        return jnp.repeat(jnp.exp(heights), shape[axis_at] // blocks).reshape((-1,) + (1,) * (len(shape) - axis_at - 1))

    level = one(*split[0])
    for cut in split[1:]:
        level = level * one(*cut)
    return level


def normal_values(rng, extent, spread, reach, shards=(), held_as=jnp.bfloat16):
    drawn = spread * jax.random.normal(rng, extent, jnp.float32)
    if shards:
        drawn = drawn * steps_of(rng, extent, shards, -0.22, 0.18)
    return jnp.clip(drawn, -reach, reach).astype(held_as)


def setup_inputs(seed: int = 0) -> dict:
    splits = jax.random.split(jax.random.key(seed), 13)
    layer_input = normal_values(splits[0], (MICRO, SEQ, D), 1.0, 6.0, ((1, 16),))
    out_cotangent = normal_values(splits[1], (MICRO, SEQ, D), 1.0, 6.0, ((1, 16),))
    block_order = jax.vmap(lambda own: jax.random.permutation(own, BLOCKS))(jax.random.split(splits[2], MICRO)).reshape((MICRO, BLOCKS)).astype(jnp.int32)
    gain_attn = jnp.clip(1.0 + 0.18 * jax.random.normal(splits[3], (2, D), jnp.float32), 0.099609375, 1.8984375).astype(jnp.bfloat16)
    w_query = normal_values(splits[4], (2, D, QW), D ** -0.5, 0.15625, ((0, 2), (1, 4), (2, 4)))
    w_key = normal_values(splits[5], (2, D, KW), D ** -0.5, 0.15625, ((0, 2), (1, 4), (2, 4)))
    w_value = normal_values(splits[6], (2, D, KW), D ** -0.5, 0.15625, ((0, 2), (1, 4), (2, 4)))
    w_out = normal_values(splits[7], (2, QW, D), (D // 16) ** -0.5, 0.625, ((0, 2), (1, 4), (2, 4)))
    gain_ffn = jnp.clip(1.0 + 0.18 * jax.random.normal(splits[8], (2, D), jnp.float32), 0.099609375, 1.8984375).astype(jnp.bfloat16)
    w_gate = normal_values(splits[9], (2, D, FF), D ** -0.5, 0.15625, ((0, 2), (1, 4), (2, 4)))
    w_up = normal_values(splits[10], (2, D, FF), D ** -0.5, 0.15625, ((0, 2), (1, 4), (2, 4)))
    w_down = normal_values(splits[11], (2, FF, D), (FF // 2) ** -0.5, 0.125, ((0, 2), (1, 4), (2, 4)))
    return dict(layer_input=layer_input, out_cotangent=out_cotangent, block_order=block_order, gain_attn=gain_attn, w_query=w_query, w_key=w_key, w_value=w_value, w_out=w_out, gain_ffn=gain_ffn, w_gate=w_gate, w_up=w_up, w_down=w_down)


epsilon = 1e-05
rope_base = 100000.0
masked = -1e+30

@jax.custom_vjp
def low(v):
    return lax.optimization_barrier(v.astype(jnp.bfloat16)).astype(jnp.float32)

@jax.custom_vjp
def low_back(v):
    return v

def low_keep(v):
    return (low(v), None)

def low_pass(kept, grad):
    return (grad,)

def back_keep(v):
    return (v, None)

def back_low(kept, grad):
    return (low(grad),)
low.defvjp(low_keep, low_pass)
low_back.defvjp(back_keep, back_low)

def rotation(positions, half_dim):
    steps_f = jnp.arange(half_dim, dtype=jnp.float32)
    frequency = jnp.power(rope_base, steps_f * (-2.0 / (2 * half_dim)))
    angles = positions.astype(jnp.float32)[:, None] * frequency[None, :]
    return (jnp.cos(angles), jnp.sin(angles))

def rotate(values, cosine, sine_tab):
    half_dim = values.shape[-1] // 2
    first_half = values[..., :half_dim]
    second_half = values[..., half_dim:]
    return jnp.concatenate([first_half * cosine - second_half * sine_tab, second_half * cosine + first_half * sine_tab], axis=-1)

def row_places(order_row, offset, amount, block_rows):
    stored = offset + jnp.arange(amount, dtype=jnp.int32)
    owner_block = stored // block_rows
    matches = owner_block[:, None] == jnp.arange(order_row.shape[0], dtype=jnp.int32)[None, :]
    base_block = lax.optimization_barrier(jnp.sum(jnp.where(matches, order_row[None, :], 0), axis=1)).astype(jnp.int32)
    return base_block * block_rows + stored % block_rows

def normalize(residual, gain):
    return residual * lax.rsqrt(lax.optimization_barrier(jnp.mean(residual * residual, axis=-1, keepdims=True)) + epsilon) * gain

def matmul(left_rows, right_mat):
    return jnp.dot(left_rows, right_mat, preferred_element_type=jnp.float32, precision=lax.Precision.HIGHEST)

def attention(query_rows, key_rows, value_rows, places):
    seq_len = query_rows.shape[0]
    query_block = min(512, seq_len)
    grouped = query_rows.reshape(seq_len // query_block, query_block, KV_HEADS, HEADS // KV_HEADS, HEAD_DIM)
    place_blocks = places.reshape(seq_len // query_block, query_block)

    @jax.checkpoint
    def one_block(inputs):
        query_part, place_part = inputs
        scores = jnp.einsum('sagd,kad->agsk', query_part, key_rows, precision=lax.Precision.HIGHEST) * HEAD_DIM ** (-0.5)
        scores = low_back(scores)
        allowed = places[None, None, None, :] <= place_part[None, None, :, None]
        scores = jnp.where(allowed, scores, masked)
        row_max = lax.optimization_barrier(jnp.max(scores, axis=-1, keepdims=True))
        log_total = row_max + jnp.log(lax.optimization_barrier(jnp.sum(jnp.exp(scores - row_max), axis=-1, keepdims=True)))
        attn_prob = low(jnp.exp(scores - log_total))
        return jnp.einsum('agsk,kad->sagd', attn_prob, value_rows, precision=lax.Precision.HIGHEST)
    outputs = lax.map(one_block, (grouped, place_blocks))
    return outputs.reshape(seq_len, HEADS * HEAD_DIM)

def layer(layer_in, params, order_row):
    gain_attn, w_query, w_key, w_value, w_out, gain_ffn, w_gate, w_up, w_down = params
    seq_len = layer_in.shape[0]
    places = row_places(order_row, 0, seq_len, SEQ_DEV // 2)
    cosine, sine_tab = rotation(places, HEAD_DIM // 2)
    cosine = cosine[:, None, :]
    sine_tab = sine_tab[:, None, :]
    normed_a = low(normalize(layer_in, gain_attn))
    q_lin = low_back(matmul(normed_a, w_query)).reshape(seq_len, HEADS, HEAD_DIM)
    k_lin = low_back(matmul(normed_a, w_key)).reshape(seq_len, KV_HEADS, HEAD_DIM)
    value_rows = low(low_back(matmul(normed_a, w_value))).reshape(seq_len, KV_HEADS, HEAD_DIM)
    query_rows = low(rotate(q_lin, cosine, sine_tab))
    key_rows = low(rotate(k_lin, cosine, sine_tab))
    attn_mix = low(low_back(attention(query_rows, key_rows, value_rows, places)))
    mid_stream = layer_in + low_back(matmul(attn_mix, w_out))
    normed_b = low(normalize(mid_stream, gain_ffn))
    gate_pre = low_back(matmul(normed_b, w_gate))
    up_pre = low_back(matmul(normed_b, w_up))
    hidden = low(jax.nn.silu(gate_pre) * up_pre)
    return mid_stream + low_back(matmul(hidden, w_down))

def reference(layer_input, out_cotangent, block_order, gain_attn, w_query, w_key, w_value, w_out, gain_ffn, w_gate, w_up, w_down):
    params = tuple((item.astype(jnp.float32) for item in (gain_attn, w_query, w_key, w_value, w_out, gain_ffn, w_gate, w_up, w_down)))

    def one_micro(totals, inputs):
        x_in, cotangent, order_row = inputs
        x_in = x_in.astype(jnp.float32)
        probe = jnp.zeros_like(x_in)

        def both_layers(first_in, weights, probe_in):
            lower_w = tuple((item[0] for item in weights))
            upper_w = tuple((item[1] for item in weights))
            section_out = low(low_back(layer(first_in, lower_w, order_row)))
            final_out = low(layer(section_out + probe_in, upper_w, order_row))
            return (section_out, final_out)
        outputs, pullback = jax.vjp(both_layers, x_in, params, probe)
        d_input, d_params, d_probe = pullback((jnp.zeros_like(outputs[0]), cotangent.astype(jnp.float32)))
        totals = tuple((older + newer for older, newer in zip(totals, d_params)))
        return (totals, (outputs[0], outputs[1], d_input, low(d_probe)))
    start_totals = tuple((jnp.zeros_like(item) for item in params))
    totals, (section_outs, final_outs, d_inputs, d_probes) = lax.scan(one_micro, start_totals, (layer_input, out_cotangent, block_order))
    layer_out = jnp.stack([section_outs, final_outs]).astype(jnp.bfloat16)
    in_grad = jnp.stack([d_inputs, d_probes]).astype(jnp.float32)
    return (layer_out, in_grad, totals[0], totals[1], totals[2], totals[3], totals[4], totals[5], totals[6], totals[7], totals[8])
```

```python
import jax
import jax.numpy as jnp
import numpy as np
from jax import lax
from jax.experimental import pallas as pl
from jax.experimental.pallas import tpu as pltpu
from jax.sharding import PartitionSpec as P

HEAD_DIM = 96
HALF = HEAD_DIM // 2
INV_ROOT = HEAD_DIM ** (-0.5)
EPSILON = 1e-05
ROPE_BASE = 100000.0
MASKED = -1e30
LANES = 128
UNIT_BLOCK = 256
F32 = jnp.float32
BF16 = jnp.bfloat16
GROUPS = 1
VMEM_LIMIT = 48 * 1024 * 1024


def swap(value, axis, step):
    count = lax.axis_size(axis)
    return lax.ppermute(value, axis, [(i, i ^ step) for i in range(count)])


def swap_from(value, source):
    return lax.ppermute(value, "section", [(source, 1 - source)])


def after(value, earlier):
    return lax.optimization_barrier((value, earlier))[0]


def dot(left, right):
    return jnp.dot(left, right, preferred_element_type=F32)


def dot_nt(left, right):
    return lax.dot_general(left, right, (((1,), (1,)), ((), ())), preferred_element_type=F32)


def dot_tn(left, right):
    return lax.dot_general(left, right, (((0,), (0,)), ((), ())), preferred_element_type=F32)


def split_terms(value):
    high = value.astype(BF16)
    return high, (value - high.astype(F32)).astype(BF16)


def shape(dims, dtype=BF16):
    return jax.ShapeDtypeStruct(dims, dtype)


def kept(dims, dtype=BF16):
    return pltpu.HBM(dims, dtype)


class View:
    def __init__(self, array, width=None, block=0):
        self.array = array
        self.width = array.shape[-1] if width is None else width
        self.block = block


def call(kernel, name, args, outs, scratch=(), flops=0):
    specs, arrays = [], []
    size = 0
    for arg in args:
        if isinstance(arg, View):
            block = arg.block
            specs.append(
                pl.BlockSpec((arg.array.shape[0], arg.width), lambda i, block=block: (0, block))
            )
            arrays.append(arg.array)
            size += arg.array.shape[0] * arg.width * arg.array.dtype.itemsize
        else:
            zeros = (0,) * arg.ndim
            specs.append(pl.BlockSpec(arg.shape, lambda i, zeros=zeros: zeros))
            arrays.append(arg)
            size += arg.size * arg.dtype.itemsize
    out_specs = [
        pl.BlockSpec(out.shape, lambda i, zeros=(0,) * len(out.shape): zeros) for out in outs
    ]
    size += sum(int(np.prod(out.shape)) * jnp.dtype(out.dtype).itemsize for out in outs)
    return pl.pallas_call(
        kernel,
        grid=(1,),
        in_specs=specs,
        out_specs=out_specs,
        out_shape=outs,
        scratch_shapes=list(scratch),
        compiler_params=pltpu.CompilerParams(vmem_limit_bytes=VMEM_LIMIT),
        cost_estimate=pl.CostEstimate(flops=flops, bytes_accessed=size, transcendentals=0),
        name=name,
    )(*arrays)


def place(pieces, ctx):
    count = len(pieces)
    size, width = pieces[0].shape

    def kernel(*refs):
        whole = refs[count]
        mine = lax.axis_index("ctx")
        for k in range(count):
            at = pl.multiple_of((mine ^ k) * size, size)
            whole[pl.ds(at, size), :] = refs[k][...]

    return call(kernel, "place", pieces, [shape((count * size, width))])[0]


def write_pieces(outs, value, micros, start=0, width=None):
    heads = len(outs)
    piece = outs[0].shape[1]
    for m in range(micros):
        for k in range(heads):
            at = (m * heads + k) * piece
            outs[k][m] = value[at : at + piece].astype(BF16)


def read_pieces(whole, pieces, micros):
    heads = len(pieces)
    piece = pieces[0].shape[1]
    for m in range(micros):
        for k in range(heads):
            at = (m * heads + k) * piece
            whole[at : at + piece, :] = pieces[k][m]


def project(pieces, queries, kvs, gain_views, cosine, sine, turn):
    heads = len(pieces)
    micros, piece, d_model = pieces[0].shape
    rows = micros * heads * piece
    half = d_model // 2
    width = queries[0].width

    def kernel(*refs):
        xs = refs[:heads]
        q_own, q_other, kv_own, kv_other, g_own, g_other, cos, sin, turns, eye = refs[heads : heads + 10]
        na, q_out, kv_out, gains = refs[heads + 10 :]
        gains[:, :half] = dot_nt(eye[...], g_own[...])
        gains[:, half:] = dot_nt(eye[...], g_other[...])
        gain = gains[0:1, :]
        for m in range(micros):
            for k in range(heads):
                x = xs[k][m].astype(F32)
                scale = lax.rsqrt(jnp.mean(x * x, axis=-1, keepdims=True) + EPSILON)
                at = (m * heads + k) * piece
                na[at : at + piece, :] = (x * scale * gain).astype(BF16)
        low, high = na[:, :half], na[:, half:]
        for part, (own, other, out) in enumerate(
            ((q_own, q_other, q_out), (kv_own, kv_other, kv_out))
        ):
            lin = dot(low, own[...]) + dot(high, other[...])
            a, b = split_terms(lin)
            turned = dot(a, turns[part]) + dot(b, turns[part])
            at = part * width
            out[...] = (
                lin * cos[:, at : at + width] + turned * sin[:, at : at + width]
            ).astype(BF16)

    eye = jnp.asarray(np.eye(8, LANES), BF16)
    return call(
        kernel,
        "project",
        [*pieces, *queries, *kvs, *gain_views, cosine, sine, turn, eye],
        [kept((rows, d_model)), kept((rows, width)), shape((rows, width)), shape((8, d_model), F32)],
        flops=4 * rows * d_model * width,
    )


def attend(query, pieces, place_q, place_k, pad, outs_w, heads, piece, group):
    ctxs = len(pieces)
    micros, span, width = pieces[0].shape
    keys = ctxs * span
    rows = micros * span
    half = outs_w[0].array.shape[0]
    kv_heads = pad.shape[1] // LANES // 2

    def kernel(*refs):
        q_ref = refs[0]
        kvs = refs[1 : 1 + ctxs]
        pq, pk, pads, w_own, w_other = refs[1 + ctxs : 6 + ctxs]
        prob, mix = refs[6 + ctxs : 8 + ctxs]
        outs = refs[8 + ctxs : 8 + ctxs + heads]
        kv_rows, mixed = refs[8 + ctxs + heads :]
        for m in range(micros):
            for j in range(ctxs):
                kv_rows[j * span : (j + 1) * span, :] = kvs[j][m]
            kv = dot(kv_rows[...], pads[...]).astype(BF16)
            q = dot(q_ref[m * span : (m + 1) * span, :], pads[...]).astype(BF16)
            allowed = pk[m] <= pq[m]
            allowed = jnp.concatenate([allowed] * group, axis=0)
            for a in range(kv_heads):
                q2 = jnp.concatenate(
                    [q[:, (a * group + g) * LANES : (a * group + g + 1) * LANES] for g in range(group)],
                    axis=0,
                )
                key = kv[:, a * LANES : (a + 1) * LANES]
                value = kv[:, (kv_heads + a) * LANES : (kv_heads + a + 1) * LANES]
                scores = jnp.where(allowed, dot_nt(q2, key) * INV_ROOT, MASKED)
                top = jnp.max(scores, axis=-1, keepdims=True)
                weight = jnp.exp(scores - top)
                share = (weight / jnp.sum(weight, axis=-1, keepdims=True)).astype(BF16)
                prob[m * kv_heads + a] = share
                got = dot(share, value).astype(BF16)
                for g in range(group):
                    at = (a * group + g) * LANES
                    mixed[:, at : at + LANES] = got[g * span : (g + 1) * span]
            mix[m * span : (m + 1) * span, :] = dot_nt(mixed[...], pads[...]).astype(BF16)
        for t, w in enumerate((w_own, w_other)):
            branch = dot_nt(mix[...], w[...]).astype(BF16)
            for m in range(micros):
                for k in range(heads):
                    at = (m * heads + k) * piece
                    outs[k][m, :, t * half : (t + 1) * half] = branch[at : at + piece]

    return call(
        kernel,
        "attend",
        [query, *pieces, place_q, place_k, pad, *outs_w],
        [
            kept((micros * kv_heads, group * span, keys)),
            kept((rows, width)),
            *[shape((micros, piece, 2 * half)) for _ in range(heads)],
        ],
        [pltpu.VMEM((keys, width), BF16), pltpu.VMEM((span, pad.shape[1]), BF16)],
        flops=4 * rows * width * (keys + half),
    )


def add_mid(x, terms, gains):
    def kernel(*refs):
        x_ref, gain = refs[0], refs[1]
        parts = refs[2 : 2 + len(terms)]
        mid, nb = refs[2 + len(terms) :]
        total = x_ref[...].astype(F32)
        for part in parts:
            total = total + part[...].astype(F32)
        mid[...] = total
        scale = lax.rsqrt(jnp.mean(total * total, axis=-1, keepdims=True) + EPSILON)
        nb[...] = (total * scale * gain[1:2, :]).astype(BF16)

    return call(
        kernel, "add_mid", [x, gains, *terms], [shape(x.shape, F32), shape(x.shape)]
    )


def add_out(mid, terms):
    def kernel(*refs):
        total = refs[0][...]
        for part in refs[1:-1]:
            total = total + part[...].astype(F32)
        refs[-1][...] = total.astype(BF16)

    return call(kernel, "add_out", [mid, *terms], [shape(mid.shape)])[0]


def blocks_of(pair, units):
    specs, arrays = [], []
    count = units // UNIT_BLOCK
    for part in range(3):
        for array in pair:
            specs.append(
                pl.BlockSpec(
                    (array.shape[0], UNIT_BLOCK), lambda j, part=part: (0, part * count + j)
                )
            )
            arrays.append(array)
    return specs, arrays


def pack_places(half, units, width):
    hidden_at = 2 * half
    mix_at = -(-(hidden_at + units) // width) * width
    return hidden_at, mix_at


def feed(pieces, pair, units, na, mix):
    heads = len(pieces)
    micros, piece, d_model = pieces[0].shape
    rows = micros * heads * piece
    half = d_model // 2
    count = units // UNIT_BLOCK
    width = mix.shape[1]
    hidden_at, mix_at = pack_places(half, units, width)

    def kernel(*refs):
        xs = refs[:heads]
        gate_w = refs[heads : heads + 2]
        up_w = refs[heads + 2 : heads + 4]
        down_w = refs[heads + 4 : heads + 6]
        na_in, mix_in = refs[heads + 6 : heads + 8]
        gate_out, up_out, hidden_out, nb, packed = refs[heads + 8 : heads + 13]
        outs = refs[heads + 13 : 2 * heads + 13]
        total = refs[-1]
        j = pl.program_id(0)

        @pl.when(j == 0)
        def _():
            read_pieces(nb, xs, micros)
            total[...] = jnp.zeros_like(total)
            packed[:, :half] = na_in[...]
            packed[:, half : 2 * half] = nb[:, half:]
            packed[:, mix_at : mix_at + width] = mix_in[...]

        low, high = nb[:, :half], nb[:, half:]
        gate = dot(low, gate_w[0][...]) + dot(high, gate_w[1][...])
        up = dot(low, up_w[0][...]) + dot(high, up_w[1][...])
        gate_out[...] = gate
        up_out[...] = up
        hidden = (gate * jax.nn.sigmoid(gate) * up).astype(BF16)
        hidden_out[...] = hidden
        at = pl.multiple_of(hidden_at + j * UNIT_BLOCK, UNIT_BLOCK)
        packed[:, pl.ds(at, UNIT_BLOCK)] = hidden
        total[:, :half] += dot_nt(hidden, down_w[0][...])
        total[:, half:] += dot_nt(hidden, down_w[1][...])

        @pl.when(j == count - 1)
        def _():
            write_pieces(outs, total, micros)

    specs, arrays = blocks_of(pair, units)
    whole = pl.BlockSpec((rows, d_model), lambda j: (0, 0))
    block = pl.BlockSpec((rows, UNIT_BLOCK), lambda j: (0, j))
    rows_spec = pl.BlockSpec((micros, piece, d_model), lambda j: (0, 0, 0))
    return pl.pallas_call(
        kernel,
        grid=(count,),
        in_specs=[rows_spec] * heads
        + specs
        + [pl.BlockSpec((rows, half), lambda j: (0, 1)), pl.BlockSpec(mix.shape, lambda j: (0, 0))],
        out_specs=[block, block, block, whole]
        + [pl.BlockSpec((rows, mix_at + width), lambda j: (0, 0))]
        + [rows_spec] * heads,
        out_shape=[
            kept((rows, units), F32),
            kept((rows, units), F32),
            kept((rows, units)),
            kept((rows, d_model)),
            kept((rows, mix_at + width)),
            *[shape((micros, piece, d_model)) for _ in range(heads)],
        ],
        scratch_shapes=[pltpu.VMEM((rows, d_model), F32)],
        compiler_params=pltpu.CompilerParams(vmem_limit_bytes=VMEM_LIMIT),
        cost_estimate=pl.CostEstimate(
            flops=6 * rows * d_model * units, bytes_accessed=6 * d_model * units, transcendentals=0
        ),
        name="feed",
    )(*pieces, *arrays, na, mix)


def feed_back(pieces, pair, gate, up):
    heads = len(pieces)
    micros, piece, d_model = pieces[0].shape
    rows, units = gate.shape
    half = d_model // 2
    count = units // UNIT_BLOCK

    def kernel(*refs):
        xs = refs[:heads]
        gate_w = refs[heads : heads + 2]
        up_w = refs[heads + 2 : heads + 4]
        down_w = refs[heads + 4 : heads + 6]
        gate_in, up_in = refs[heads + 6 : heads + 8]
        d_gate_out, d_up_out, gf, packed = refs[heads + 8 : heads + 12]
        outs = refs[heads + 12 : 2 * heads + 12]
        total = refs[-1]
        j = pl.program_id(0)

        @pl.when(j == 0)
        def _():
            read_pieces(gf, xs, micros)
            total[...] = jnp.zeros_like(total)
            packed[:, :half] = gf[:, half:]

        d_hidden = dot(gf[:, :half], down_w[0][...]) + dot(gf[:, half:], down_w[1][...])
        gate_v, up_v = gate_in[...], up_in[...]
        sigma = jax.nn.sigmoid(gate_v)
        d_gate = (d_hidden * up_v * sigma * (1.0 + gate_v * (1.0 - sigma))).astype(BF16)
        d_up = (d_hidden * gate_v * sigma).astype(BF16)
        d_gate_out[...] = d_gate
        d_up_out[...] = d_up
        at = pl.multiple_of(half + j * UNIT_BLOCK, UNIT_BLOCK)
        packed[:, pl.ds(at, UNIT_BLOCK)] = d_gate
        at = pl.multiple_of(half + units + j * UNIT_BLOCK, UNIT_BLOCK)
        packed[:, pl.ds(at, UNIT_BLOCK)] = d_up
        total[:, :half] += dot_nt(d_gate, gate_w[0][...]) + dot_nt(d_up, up_w[0][...])
        total[:, half:] += dot_nt(d_gate, gate_w[1][...]) + dot_nt(d_up, up_w[1][...])

        @pl.when(j == count - 1)
        def _():
            write_pieces(outs, total, micros)

    specs, arrays = blocks_of(pair, units)
    whole = pl.BlockSpec((rows, d_model), lambda j: (0, 0))
    block = pl.BlockSpec((rows, UNIT_BLOCK), lambda j: (0, j))
    rows_spec = pl.BlockSpec((micros, piece, d_model), lambda j: (0, 0, 0))
    return pl.pallas_call(
        kernel,
        grid=(count,),
        in_specs=[rows_spec] * heads + specs + [block, block],
        out_specs=[block, block, whole]
        + [pl.BlockSpec((rows, half + 2 * units), lambda j: (0, 0))]
        + [rows_spec] * heads,
        out_shape=[
            kept((rows, units)),
            kept((rows, units)),
            kept((rows, d_model)),
            kept((rows, half + 2 * units)),
            *[shape((micros, piece, d_model)) for _ in range(heads)],
        ],
        scratch_shapes=[pltpu.VMEM((rows, d_model), F32)],
        compiler_params=pltpu.CompilerParams(vmem_limit_bytes=VMEM_LIMIT),
        cost_estimate=pl.CostEstimate(
            flops=6 * rows * d_model * units, bytes_accessed=6 * d_model * units, transcendentals=0
        ),
        name="feed_back",
    )(*pieces, *arrays, gate, up)


def norm_back(terms, residual, gains, row, carried):
    d_model = residual.shape[-1]

    def kernel(*refs):
        res, gain, carry = refs[:3]
        parts = refs[3 : 3 + len(terms)]
        d_out, d_low, d_gain = refs[3 + len(terms) :]
        d_normed = parts[0][...].astype(F32)
        for part in parts[1:]:
            d_normed = d_normed + part[...].astype(F32)
        rows = res[...].astype(F32)
        scale = lax.rsqrt(jnp.mean(rows * rows, axis=-1, keepdims=True) + EPSILON)
        unit = rows * scale
        d_gain[...] = jnp.sum(jnp.sum(d_normed * unit, axis=0), axis=0, keepdims=True)
        d_unit = d_normed * gain[row : row + 1, :]
        total = carry[...].astype(F32) + scale * (
            d_unit - unit * jnp.mean(d_unit * unit, axis=-1, keepdims=True)
        )
        d_out[...] = total
        d_low[...] = total.astype(BF16)

    return call(
        kernel,
        "norm_back",
        [residual, gains, carried, *terms],
        [shape(residual.shape, F32), shape(residual.shape), shape((1, d_model), F32)],
    )


def attend_back(pieces, outs_w, mix, prob, query, kv_pieces, pad, turn, cosine, sine, group):
    heads = len(pieces)
    micros, piece, d_model = pieces[0].shape
    span = heads * piece
    rows = micros * span
    half = d_model // 2
    ctxs = len(kv_pieces)
    width = query.shape[1]
    keys = ctxs * span
    kv_heads = pad.shape[1] // LANES // 2

    def kernel(*refs):
        xs = refs[:heads]
        w_own, w_other, mix_in, prob_in, q_ref = refs[heads : heads + 5]
        kvs = refs[heads + 5 : heads + 5 + ctxs]
        pads, turns, cos, sin = refs[heads + 5 + ctxs : heads + 9 + ctxs]
        ga, ga_other, dq_out = refs[heads + 9 + ctxs : heads + 12 + ctxs]
        outs = refs[heads + 12 + ctxs : heads + 12 + 2 * ctxs]
        kv_rows, d_kv, d_q = refs[heads + 12 + 2 * ctxs :]
        read_pieces(ga, xs, micros)
        ga_other[...] = ga[:, half:]
        d_mix = (dot(ga[:, :half], w_own[...]) + dot(ga[:, half:], w_other[...])).astype(BF16)
        for m in range(micros):
            for j in range(ctxs):
                kv_rows[j * span : (j + 1) * span, :] = kvs[j][m]
            here = slice(m * span, (m + 1) * span)
            kv = dot(kv_rows[...], pads[...]).astype(BF16)
            q = dot(q_ref[here, :], pads[...]).astype(BF16)
            d = dot(d_mix[here], pads[...])
            product = d * dot(mix_in[here, :], pads[...])
            d = d.astype(BF16)
            for a in range(kv_heads):
                cuts = [slice((a * group + g) * LANES, (a * group + g + 1) * LANES) for g in range(group)]
                q2 = jnp.concatenate([q[:, cut] for cut in cuts], axis=0)
                d2 = jnp.concatenate([d[:, cut] for cut in cuts], axis=0)
                delta = jnp.concatenate(
                    [jnp.sum(product[:, cut], axis=-1, keepdims=True) for cut in cuts], axis=0
                )
                key = kv[:, a * LANES : (a + 1) * LANES]
                value = kv[:, (kv_heads + a) * LANES : (kv_heads + a + 1) * LANES]
                share = prob_in[m * kv_heads + a]
                d_prob = dot_nt(d2, value)
                d_score = (share.astype(F32) * (d_prob - delta)).astype(BF16)
                back = dot(d_score, key)
                for g, cut in enumerate(cuts):
                    d_q[:, cut] = back[g * span : (g + 1) * span]
                d_kv[:, a * LANES : (a + 1) * LANES] = dot_tn(d_score, q2).astype(BF16)
                d_kv[:, (kv_heads + a) * LANES : (kv_heads + a + 1) * LANES] = dot_tn(
                    share, d2
                ).astype(BF16)
            packed = dot_nt(d_kv[...], pads[...]).astype(BF16)
            for j in range(ctxs):
                outs[j][m] = packed[j * span : (j + 1) * span]
            high, low = split_terms(d_q[...])
            line = (dot_nt(high, pads[...]) + dot_nt(low, pads[...])) * INV_ROOT
            high, low = split_terms(line)
            turned = dot_nt(high, turns[0]) + dot_nt(low, turns[0])
            dq_out[here, :] = (line * cos[here, :width] + turned * sin[here, :width]).astype(BF16)

    return call(
        kernel,
        "attend_back",
        [*pieces, *outs_w, mix, prob, query, *kv_pieces, pad, turn, cosine, sine],
        [
            kept((rows, d_model)),
            shape((rows, half)),
            shape((rows, width)),
            *[shape((micros, span, width)) for _ in range(ctxs)],
        ],
        [
            pltpu.VMEM((keys, width), BF16),
            pltpu.VMEM((keys, pad.shape[1]), BF16),
            pltpu.VMEM((span, pad.shape[1]), F32),
        ],
        flops=10 * rows * width * keys,
    )


def project_back(terms, dq, queries, kvs, turn, cosine, sine, row_pieces):
    heads = len(row_pieces)
    micros, span, width = terms[0].shape
    rows = micros * span
    piece = span // heads
    half = queries[0].array.shape[0]
    count = len(terms)

    def kernel(*refs):
        parts = refs[:count]
        dq_in, q_own, q_other, kv_own, kv_other, turns, cos, sin = refs[count : count + 8]
        xs = refs[count + 8 : count + 8 + heads]
        d_line, d_gain = refs[count + 8 + heads : count + 10 + heads]
        outs = refs[count + 10 + heads : count + 10 + 2 * heads]
        unit = refs[-1]
        for m in range(micros):
            for k in range(heads):
                x = xs[k][m].astype(F32)
                scale = lax.rsqrt(jnp.mean(x * x, axis=-1, keepdims=True) + EPSILON)
                at = (m * heads + k) * piece
                unit[at : at + piece, :] = x * scale
        d_line[:, :width] = dq_in[...]
        lanes = lax.broadcasted_iota(jnp.int32, (span, width), 1)
        scaled = jnp.where(lanes < width // 2, INV_ROOT, 1.0)
        for m in range(micros):
            here = slice(m * span, (m + 1) * span)
            total = parts[0][m].astype(F32)
            for part in parts[1:]:
                total = total + part[m].astype(F32)
            total = total * scaled
            high, low = split_terms(total)
            turned = dot_nt(high, turns[1]) + dot_nt(low, turns[1])
            d_line[here, width:] = (
                total * cos[here, width:] + turned * sin[here, width:]
            ).astype(BF16)
        for t, (wq, wkv) in enumerate(((q_own, kv_own), (q_other, kv_other))):
            branch = dot_nt(d_line[:, :width], wq[...]) + dot_nt(d_line[:, width:], wkv[...])
            side = slice(t * half, (t + 1) * half)
            d_gain[:, side] = jnp.sum(branch * unit[:, side], axis=0, keepdims=True)
            branch = branch.astype(BF16)
            for m in range(micros):
                for k in range(heads):
                    at = (m * heads + k) * piece
                    outs[k][m, :, t * half : (t + 1) * half] = branch[at : at + piece]

    return call(
        kernel,
        "project_back",
        [*terms, dq, *queries, *kvs, turn, cosine, sine, *row_pieces],
        [
            kept((rows, 2 * width)),
            shape((1, 2 * half), F32),
            *[shape((micros, piece, 2 * half)) for _ in range(heads)],
        ],
        [pltpu.VMEM((rows, 2 * half), F32)],
        flops=8 * rows * half * width,
    )


def weight_grad(groups):
    half = groups[0][0][0].width
    total = sum(group[0][1].width for group in groups)
    args = [view for group in groups for pair in group for view in pair]

    def kernel(*refs):
        out = refs[-1]
        at = 0
        for g, group in enumerate(groups):
            n = group[0][1].width
            a, b, c, d = refs[4 * g : 4 * g + 4]
            out[:, at : at + n] = (dot_tn(a[...], b[...]) + dot_tn(c[...], d[...])).astype(BF16)
            at += n

    rows = groups[0][0][0].array.shape[0]
    return call(
        kernel, "weight_grad", args, [shape((half, total))], flops=4 * half * rows * total
    )[0]


def late_grad(nb, gf, d_gate, d_up, hidden, packed, packed_back):
    rows, d_model = nb.shape
    units = hidden.shape[1]
    half = d_model // 2
    count = units // UNIT_BLOCK
    hidden_at, _ = pack_places(half, units, LANES)

    def kernel(*refs):
        sides = refs[:4]
        lines = refs[4:10]
        out = refs[10]
        turned = refs[11:]
        j = pl.program_id(0)

        @pl.when(j == 0)
        def _():
            for side, flat in zip(sides, turned):
                flat[...] = side[...].T

        for part in range(3):

            @pl.when(j // count == part)
            def _(part=part):
                which = (0, 0, 1)[part]
                out[...] = (
                    dot(turned[which][...], lines[part][...])
                    + dot(turned[2 + which][...], lines[3 + part][...])
                ).astype(BF16)

    def side(block):
        return pl.BlockSpec((rows, half), lambda j: (0, block))

    def line(part, first):
        return pl.BlockSpec(
            (rows, UNIT_BLOCK),
            lambda j: (0, first // UNIT_BLOCK + jnp.clip(j - part * count, 0, count - 1)),
        )

    return pl.pallas_call(
        kernel,
        grid=(3 * count,),
        in_specs=[side(0), side(0), side(1), side(0)]
        + [line(part, 0) for part in range(3)]
        + [line(0, half), line(1, half + units), line(2, hidden_at)],
        out_specs=pl.BlockSpec((half, UNIT_BLOCK), lambda j: (0, j)),
        out_shape=kept((half, 3 * units)),
        scratch_shapes=[pltpu.VMEM((half, rows), BF16)] * 4,
        compiler_params=pltpu.CompilerParams(vmem_limit_bytes=VMEM_LIMIT),
        cost_estimate=pl.CostEstimate(
            flops=12 * half * rows * units, bytes_accessed=6 * half * units, transcendentals=0
        ),
        name="late_grad",
    )(nb, gf, packed, packed_back, d_gate, d_up, hidden, packed_back, packed_back, packed)


def relative_columns(value, section, ctxs):
    width = value.shape[-1] // (2 * ctxs)
    return jnp.concatenate(
        [
            lax.dynamic_slice_in_dim(
                value, (k * 2 + (section ^ t)) * width, width, axis=value.ndim - 1
            )
            for t in range(2)
            for k in range(ctxs)
        ],
        axis=-1,
    )


def stored_columns(value, section, ctxs):
    width = value.shape[-1] // (2 * ctxs)
    return jnp.concatenate(
        [
            lax.dynamic_slice_in_dim(
                value, ((section ^ t) * ctxs + k) * width, width, axis=value.ndim - 1
            )
            for k in range(ctxs)
            for t in range(2)
        ],
        axis=-1,
    )


def send_all(pieces, axis):
    return [pieces[0]] + [swap(piece, axis, k) for k, piece in enumerate(pieces[1:], 1)]


def send_rows(rows):
    return send_all([rows] * lax.axis_size("head"), "head")


def send_blocks(rows):
    return send_all([rows] * lax.axis_size("ctx"), "ctx")


class Fetch:
    def __init__(self, shard):
        self.shard = shard

    def send(self, gate):
        self.pieces = send_blocks(after(self.shard, gate))

    def settle(self, gate=None):
        own = place(after(self.pieces, gate), lax.axis_index("ctx"))
        self.pair = (own, swap(own, "section", 1))
        return self.pair

    def direct(self, gate=None, with_rows=None):
        shard = self.shard if gate is None else after(self.shard, gate)
        pieces = send_blocks(shard)
        if with_rows is not None:
            pieces = after(pieces, with_rows)
        own = place(pieces, lax.axis_index("ctx"))
        self.pair = (own, swap(own, "section", 1))
        return pieces[1:]

    def first(self, gate=None):
        shard = self.shard if gate is None else after(self.shard, gate)
        self.own = lax.all_gather(shard, "ctx", axis=0, tiled=True)
        return self.own

    def second(self, gate=None):
        own = self.own if gate is None else after(self.own, gate)
        self.pair = (own, swap(own, "section", 1))
        return self.pair[1]


class Settle:
    def __init__(self, source):
        self.source = source

    def first(self, whole):
        self.kept = lax.psum_scatter(whole, "ctx", scatter_dimension=0, tiled=True)
        return whole

    def direct(self, whole):
        ctxs = lax.axis_size("ctx")
        ctx = lax.axis_index("ctx")
        size = whole.shape[0] // ctxs
        parts = [
            lax.dynamic_slice_in_dim(whole, (ctx ^ k) * size, size, axis=0) for k in range(ctxs)
        ]
        total = None
        for term in send_all(parts, "ctx"):
            term = term.astype(F32)
            total = term if total is None else total + term
        self.kept = total.astype(BF16)
        return whole

    def second(self, gate=None):
        kept = self.kept if gate is None else after(self.kept, gate)
        self.kept = kept
        sent = swap_from(kept, self.source)
        self.halves = (kept, sent) if self.source == 1 else (sent, kept)
        return sent


class Chain:
    def __init__(self):
        self.tasks = {}
        self.due = {}

    def plan(self, start, end, task):
        self.tasks.setdefault(start, []).append((end, task))

    def enter(self, name, value):
        done = self.due.pop(name, [])
        return after(value, done) if done else value

    def leave(self, name, value):
        for end, task in self.tasks.pop(name, []):
            result = task(value)
            if end is not None:
                self.due.setdefault(end, []).append(result)


class Plan:
    pass


def pick(first, a, b):
    return jnp.where(first, a, b)


def turning(heads_turned, heads):
    turn = np.zeros((heads * HEAD_DIM, heads * HEAD_DIM), np.float32)
    for h in range(heads_turned):
        for i in range(HALF):
            turn[h * HEAD_DIM + HALF + i, h * HEAD_DIM + i] = -1.0
            turn[h * HEAD_DIM + i, h * HEAD_DIM + HALF + i] = 1.0
    return turn


def padding(heads):
    pad = np.zeros((heads * HEAD_DIM, heads * LANES), np.float32)
    for h in range(heads):
        for i in range(HEAD_DIM):
            pad[h * HEAD_DIM + i, h * LANES + i] = 1.0
    return pad


def local(
    layer_input,
    out_cotangent,
    block_order,
    gain_attn,
    w_query,
    w_key,
    w_value,
    w_out,
    gain_ffn,
    w_gate,
    w_up,
    w_down,
):
    section = lax.axis_index("section")
    head = lax.axis_index("head")
    ctx = lax.axis_index("ctx")
    heads = lax.axis_size("head")
    ctxs = lax.axis_size("ctx")
    first = section == 0
    micros_all = layer_input.shape[0] // 2
    micros = micros_all // GROUPS
    rows_dev = layer_input.shape[1]
    d_model = layer_input.shape[2]
    span = heads * rows_dev
    rows = micros * span
    block_rows = ctxs * span // block_order.shape[1]
    d_half = d_model // ctxs // 2
    width = w_query.shape[2]
    k_width = w_key.shape[2]
    units = w_gate.shape[2]
    group_size = width // k_width
    line_heads = width // HEAD_DIM
    chain = Chain()

    turn = jnp.asarray(
        np.stack([turning(line_heads, line_heads), turning(k_width // HEAD_DIM, line_heads)]), BF16
    )
    pad = jnp.asarray(padding(line_heads), BF16)

    def places_of(order, ctx_index):
        piece = jnp.arange(span, dtype=jnp.int32)
        stored = (ctx_index * heads + (head ^ (piece // rows_dev))) * rows_dev + piece % rows_dev
        block = stored // block_rows
        match = block[:, None] == jnp.arange(order.shape[1], dtype=jnp.int32)[None, :]
        base = jnp.sum(jnp.where(match[None], order[:, None, :], 0), axis=2)
        return base * block_rows + (stored % block_rows)[None]

    frequency = jnp.power(ROPE_BASE, jnp.arange(HALF, dtype=F32) * (-2.0 / HEAD_DIM))

    def group_of(index):
        group = Plan()
        at = section * micros_all + index * micros
        group.name = "ab"[index]
        order = lax.dynamic_slice_in_dim(block_order, at, micros, axis=0)
        places_q = places_of(order, ctx)
        places_k = jnp.concatenate([places_of(order, ctx ^ k) for k in range(ctxs)], axis=1)
        group.place_q = places_q[:, :, None]
        group.place_k = places_k[:, None, :]
        angles = places_q.reshape(rows, 1).astype(F32) * frequency
        cosine, sine = jnp.cos(angles), jnp.sin(angles)
        turned = 2 * (line_heads + k_width // HEAD_DIM)
        fixed = width - k_width
        group.cosine = jnp.concatenate(
            [cosine] * turned + [jnp.ones((rows, fixed), F32)], axis=1
        )
        group.sine = jnp.concatenate([sine] * turned + [jnp.zeros((rows, fixed), F32)], axis=1)

        def mine(value):
            part = lax.dynamic_slice_in_dim(value, at, micros, axis=0)
            return relative_columns(part, section, ctxs)

        group.x = mine(layer_input)
        group.cot = mine(out_cotangent)
        group.keep, group.d_in = {}, {}
        return group

    members = [group_of(index) for index in range(GROUPS)]
    tail = members[-1].name
    for group in members:
        group.x_pieces = send_rows(group.x)

    def exchange(shard, gate=None):
        def cut(which):
            return lax.dynamic_slice_in_dim(shard, which * d_half, d_half, axis=0)

        kept, given = cut(section), cut(1 - section)
        if gate is not None:
            given = after(given, gate)
        taken = swap(given, "section", 1)
        return pick(first, kept, taken), pick(first, taken, kept)

    gains = jnp.stack([gain_attn[0], gain_ffn[0]], axis=1)
    gains = jnp.pad(gains, ((0, 0), (0, LANES - 2)))
    early_shards = exchange(
        jnp.concatenate([w_query[0], w_key[0], w_value[0], gains], axis=1)
    )
    early0 = Fetch(early_shards[0])
    out_shards = exchange(w_out[0].T)
    late_shards = exchange(jnp.concatenate([w_gate[0], w_up[0], w_down[0].T], axis=1))
    late0, late1 = Fetch(late_shards[0]), Fetch(late_shards[1])
    out0 = Fetch(out_shards[0])
    both1 = Fetch(jnp.concatenate([out_shards[1], early_shards[1]], axis=1))
    prepared = [group.x_pieces for group in members], [
        (group.cosine, group.sine, group.place_q, group.place_k) for group in members
    ]
    landed = early0.direct(None, (prepared, late_shards, out_shards, both1.shard))
    late0.first(landed)
    out0.send(landed[:1])

    def views0(name):
        if name == "o":
            return [View(part, width, 0) for part in out0.pair]
        at = {"q": (width, 0), "kv": (width, 1), "g": (LANES, 2 * width // LANES)}[name]
        return [View(part, *at) for part in early0.pair]

    def views1(name):
        at = {
            "o": (width, 0),
            "q": (width, 1),
            "kv": (width, 2),
            "g": (LANES, 3 * width // LANES),
        }[name]
        return [View(part, *at) for part in both1.pair]

    token = [None]

    def enter(name, group, value):
        if token[0] is not None and GROUPS > 1:
            value = after(value, token[0])
        return chain.enter(name + group.name, value)

    def leave(name, group, value):
        token[0] = value
        chain.leave(name + group.name, value)

    def forward(label, group, layer_in, views, late_fetch):
        keep = Plan()
        keep.x = layer_in
        pieces = group.x_pieces if label == "0" else send_rows(layer_in)
        leave(label + "F0", group, layer_in)
        yield
        pieces = enter(label + "F1", group, pieces)
        keep.x_pieces = pieces
        keep.na, keep.query, kv, keep.gains = project(
            pieces, views("q"), views("kv"), views("g"), group.cosine, group.sine, turn
        )
        kv = kv.reshape(micros, span, width)
        pieces = send_blocks(kv)
        leave(label + "F1", group, kv)
        yield
        keep.kv = enter(label + "F2", group, pieces)
        keep.prob, keep.mix, *parts = attend(
            keep.query, keep.kv, group.place_q, group.place_k, pad, views("o"),
            heads, rows_dev, group_size,
        )
        terms = send_all(parts, "head")
        leave(label + "F2", group, parts[0])
        yield
        terms = enter(label + "F3", group, terms)
        keep.mid, own_nb = add_mid(layer_in, terms, keep.gains)
        pieces = send_rows(own_nb)
        leave(label + "F3", group, own_nb)
        yield
        pieces = enter(label + "F4", group, pieces)
        keep.late = late_fetch.pair
        keep.gate, keep.up, keep.hidden, keep.nb, packed, *parts = feed(
            pieces, keep.late, units, keep.na, keep.mix
        )
        keep.packed = swap(packed, "section", 1)
        group.parts = parts
        group.keep[label] = keep
        leave(label + "F4", group, parts[0])
        if label == "0":
            terms = send_all(parts, "head")
            yield
            terms = enter(label + "F5", group, terms)
            group.out = add_out(keep.mid, terms)

    def backward(label, group, pieces, grad, views):
        keep = group.keep[label]
        pieces = enter(label + "B1", group, pieces)
        keep.d_gate, keep.d_up, keep.gf, packed, *parts = feed_back(
            pieces, keep.late, keep.gate, keep.up
        )
        keep.packed_back = swap(packed, "section", 1)
        terms = send_all(parts, "head")
        leave(label + "B1", group, parts[0])
        yield
        terms = enter(label + "B2", group, terms)
        d_mid, own_ga, keep.gain_b = norm_back(terms, keep.mid, keep.gains, 1, grad)
        pieces = send_rows(own_ga)
        leave(label + "B2", group, own_ga)
        yield
        pieces = enter(label + "B3", group, pieces)
        keep.ga, ga_other, dq, *parts = attend_back(
            pieces, views("o"), keep.mix, keep.prob, keep.query, keep.kv, pad, turn,
            group.cosine, group.sine, group_size,
        )
        terms = send_all(parts, "ctx")
        keep.ga_other = swap(ga_other, "section", 1)
        leave(label + "B3", group, parts[0])
        yield
        terms = enter(label + "B4", group, terms)
        keep.d_line, keep.gain_a, *parts = project_back(
            terms, dq, views("q"), views("kv"), turn, group.cosine, group.sine, keep.x_pieces
        )
        terms = send_all(parts, "head")
        keep.d_line_other = swap(keep.d_line, "section", 1)
        leave(label + "B4", group, parts[0])
        yield
        terms = enter(label + "B5", group, terms)
        d_input, d_low, _ = norm_back(terms, keep.x, keep.gains, 0, d_mid)
        if label == "1":
            group.d_in[label] = d_low
            group.pieces = send_rows(d_low)
        else:
            group.d_in[label] = d_input
        leave(label + "B5", group, group.d_in[label])
        yield

    def drive(*stages):
        waiting = list(stages)
        while waiting:
            waiting = [stage for stage in waiting if next(stage, stage) is not stage]

    def gather_cot(group):
        def task(gate):
            group.cot_pieces = send_rows(after(group.cot, gate))
            return group.cot_pieces

        return task

    def on_last(start, end, task):
        chain.plan(start + tail, end + tail if end else None, task)

    on_last("0F1", "0F2", out0.settle)
    for group in members:
        chain.plan("0F1" + group.name, "0F2" + group.name, gather_cot(group))
    on_last("0F3", None, late0.second)
    on_last("0F3", None, lambda gate: both1.first(late0.pair[0]))
    on_last("1F0", None, both1.second)
    on_last("1F0", None, lambda gate: late1.first(both1.pair[0]))
    on_last("1F3", None, late1.second)
    drive(*(forward("0", group, group.x, views0, late0) for group in members))

    def scatter_out(group):
        def task(gate):
            parts = after(group.parts, gate)
            group.final = add_out(group.keep["1"].mid, send_all(parts, "head"))
            return group.final

        return task

    for group in members:
        chain.plan("1B3" + group.name, "1B4" + group.name, scatter_out(group))
    drive(*(forward("1", group, group.out, views1, late1) for group in members))

    _, mix_at = pack_places(d_model // 2, units, width)

    def rows_of(label, *names):
        def joined(name):
            parts = [getattr(group.keep[label], name) for group in members]
            return parts[0] if len(parts) == 1 else jnp.concatenate(parts, axis=0)

        return [joined(name) for name in names]

    def late_of(label, gate):
        names = ("nb", "gf", "d_gate", "d_up", "hidden", "packed", "packed_back")
        return late_grad(*after(rows_of(label, *names), gate))

    def out_group(ga, mix, ga_other, packed):
        return (
            (View(ga, d_model // 2, 0), View(mix)),
            (View(ga_other), View(packed, width, mix_at // width)),
        )

    def early_group(na, d_line, packed, d_line_other):
        return (
            (View(na, d_model // 2, 0), View(d_line)),
            (View(packed, d_model // 2, 0), View(d_line_other)),
        )

    out_names = ("ga", "mix", "ga_other", "packed")
    early_names = ("na", "d_line", "packed", "d_line_other")

    def out_of(label, gate):
        return weight_grad([out_group(*after(rows_of(label, *out_names), gate))])

    def early_of(label, gate):
        return weight_grad([early_group(*after(rows_of(label, *early_names), gate))])

    def both_of(label, gate):
        values = after(rows_of(label, *out_names, *early_names), gate)
        return weight_grad([out_group(*values[:4]), early_group(*values[4:])])

    late_1, both_1, late_0, out_0, early_0 = (Settle(s) for s in (0, 0, 1, 1, 1))
    on_last("1B2", "1B3", lambda gate: late_1.first(late_of("1", gate)))
    on_last("1B5", "0B1", late_1.second)
    on_last("1B5", "0B1", lambda gate: both_1.first(both_of("1", (gate, late_1.kept))))
    on_last("0B2", "0B3", both_1.second)
    on_last("0B2", "0B3", lambda gate: late_0.first(late_of("0", (gate, both_1.kept))))
    on_last("0B3", "0B4", lambda gate: out_0.direct(out_of("0", gate)))
    on_last("0B4", None, late_0.second)
    on_last("0B4", None, lambda gate: early_0.direct(early_of("0", (gate, late_0.kept))))
    gain_mine = []

    def sum_gains(gate):
        def gain_of(label, name):
            total = getattr(members[0].keep[label], name)
            for group in members[1:]:
                total = total + getattr(group.keep[label], name)
            return total[0]

        gain_rows = after(
            jnp.stack([gain_of(label, name) for label in "01" for name in ("gain_a", "gain_b")]),
            gate,
        ).reshape(4, 2, ctxs, d_half)
        at = lambda k: lax.dynamic_index_in_dim(gain_rows, ctx ^ k, 2, keepdims=False)
        gain_sum = at(0)
        for k in range(1, ctxs):
            gain_sum = gain_sum + swap(at(k), "ctx", k)
        gain_total = gain_sum
        for k in range(1, heads):
            gain_total = gain_total + swap(gain_sum, "head", k)
        own, other = gain_total[:, 0], gain_total[:, 1]
        low, high = pick(first, own, other), pick(first, other, own)
        gain_total = jnp.concatenate([low, high], axis=1)
        gain_total = gain_total + swap(gain_total, "section", 1)
        gain_mine.append(pick(first, gain_total[:2], gain_total[2:]))
        return gain_mine[0]

    def by_layer(lower, upper):
        lower = stored_columns(lower, section, ctxs)
        upper = stored_columns(upper, section, ctxs)
        kept_rows = pick(first, lower, upper)
        got_rows = swap(pick(first, upper, lower).astype(BF16), "section", 1).astype(lower.dtype)
        return jnp.concatenate(
            [pick(first, kept_rows, got_rows), pick(first, got_rows, kept_rows)], axis=0
        )[None]

    def all_rows(name):
        parts = [name(group) for group in members]
        return parts[0] if len(parts) == 1 else jnp.concatenate(parts, axis=0)

    layer_outs = []

    def out_rows(gate):
        lower, upper = after((all_rows(lambda g: g.out), all_rows(lambda g: g.final)), gate)
        layer_outs.append(by_layer(lower, upper))
        return layer_outs[0]

    on_last("0B2", "0B4", out_rows)
    on_last("0B5", None, sum_gains)
    drive(*(backward("1", group, group.cot_pieces, group.cot, views1) for group in members))
    drive(*(backward("0", group, group.pieces, group.d_in["1"], views0) for group in members))
    out_0.second()
    early_0.second()

    def shard_of(lower, upper):
        return jnp.concatenate([pick(first, a, b) for a, b in zip(lower, upper)], axis=0)

    out_grad = shard_of(out_0.halves, [part[:, :width] for part in both_1.halves]).astype(F32)
    early_grad = shard_of(early_0.halves, [part[:, width:] for part in both_1.halves]).astype(F32)
    late = shard_of(late_0.halves, late_1.halves).astype(F32)
    g_query = early_grad[:, :width]
    g_key = early_grad[:, width : width + k_width]
    g_value = early_grad[:, width + k_width :]
    g_out = out_grad.T
    g_gate = late[:, :units]
    g_up = late[:, units : 2 * units]
    g_down = late[:, 2 * units :].T

    in_grad = by_layer(
        all_rows(lambda g: g.d_in["0"]), all_rows(lambda g: g.d_in["1"]).astype(F32)
    )
    return (
        layer_outs[0],
        in_grad,
        gain_mine[0][0][None],
        g_query[None],
        g_key[None],
        g_value[None],
        g_out[None],
        gain_mine[0][1][None],
        g_gate[None],
        g_up[None],
        g_down[None],
    )


def solution(mesh):
    row_spec = P(None, ("ctx", "head"), None)
    vector = P("section", "ctx")
    tall = P("section", "ctx", "head")
    wide = P("section", "head", "ctx")
    kept_rows = P("section", None, ("ctx", "head"), None)
    return jax.shard_map(
        local,
        mesh=mesh,
        in_specs=(row_spec, row_spec, P(), vector, tall, tall, tall, wide, vector, tall, tall, wide),
        out_specs=(kept_rows, kept_rows, vector, tall, tall, tall, wide, vector, tall, tall, wide),
        check_vma=False,
    )
```

```python
import jax
import jax.numpy as jnp
import numpy as np
from jax import lax
from jax.experimental import pallas as pl
from jax.experimental.pallas import tpu as pltpu
from jax.sharding import PartitionSpec as P

HEAD_DIM = 96
HALF = HEAD_DIM // 2
INV_ROOT = HEAD_DIM ** (-0.5)
EPSILON = 1e-05
ROPE_BASE = 100000.0
MASKED = -1e30
LANES = 128
UNIT_BLOCK = 256
F32 = jnp.float32
BF16 = jnp.bfloat16
GROUPS = 1
VMEM_LARGE = 60 * 1024 * 1024
VMEM_SMALL = 12 * 1024 * 1024


def swap(value, axis, step):
    count = lax.axis_size(axis)
    return lax.ppermute(value, axis, [(i, i ^ step) for i in range(count)])


def swap_from(value, source):
    return lax.ppermute(value, "section", [(source, 1 - source)])


def after(value, earlier):
    return lax.optimization_barrier((value, earlier))[0]


def dot(left, right):
    return jnp.dot(left, right, preferred_element_type=F32)


def dot_nt(left, right):
    return lax.dot_general(left, right, (((1,), (1,)), ((), ())), preferred_element_type=F32)


def dot_tn(left, right):
    return lax.dot_general(left, right, (((0,), (0,)), ((), ())), preferred_element_type=F32)


def split_terms(value):
    high = value.astype(BF16)
    return high, (value - high.astype(F32)).astype(BF16)


def shape(dims, dtype=BF16):
    return jax.ShapeDtypeStruct(dims, dtype)


def kept(dims, dtype=BF16):
    return pltpu.HBM(dims, dtype)


class View:
    def __init__(self, array, width=None, block=0):
        self.array = array
        self.width = array.shape[-1] if width is None else width
        self.block = block


def call(kernel, name, args, outs, scratch=(), flops=0, limit=VMEM_LARGE):
    specs, arrays = [], []
    size = 0
    for arg in args:
        if isinstance(arg, View):
            block = arg.block
            specs.append(
                pl.BlockSpec((arg.array.shape[0], arg.width), lambda i, block=block: (0, block))
            )
            arrays.append(arg.array)
            size += arg.array.shape[0] * arg.width * arg.array.dtype.itemsize
        else:
            zeros = (0,) * arg.ndim
            specs.append(pl.BlockSpec(arg.shape, lambda i, zeros=zeros: zeros))
            arrays.append(arg)
            size += arg.size * arg.dtype.itemsize
    out_specs = [
        pl.BlockSpec(out.shape, lambda i, zeros=(0,) * len(out.shape): zeros) for out in outs
    ]
    size += sum(int(np.prod(out.shape)) * jnp.dtype(out.dtype).itemsize for out in outs)
    return pl.pallas_call(
        kernel,
        grid=(1,),
        in_specs=specs,
        out_specs=out_specs,
        out_shape=outs,
        scratch_shapes=list(scratch),
        compiler_params=pltpu.CompilerParams(vmem_limit_bytes=limit),
        cost_estimate=pl.CostEstimate(flops=flops, bytes_accessed=size, transcendentals=0),
        name=name,
    )(*arrays)


def place(pieces, ctx):
    count = len(pieces)
    size, width = pieces[0].shape

    def kernel(*refs):
        whole = refs[count]
        mine = lax.axis_index("ctx")
        for k in range(count):
            at = pl.multiple_of((mine ^ k) * size, size)
            whole[pl.ds(at, size), :] = refs[k][...]

    return call(kernel, "place", pieces, [shape((count * size, width))])[0]


def write_pieces(outs, value, micros, start=0, width=None):
    heads = len(outs)
    piece = outs[0].shape[1]
    for m in range(micros):
        for k in range(heads):
            at = (m * heads + k) * piece
            outs[k][m] = value[at : at + piece].astype(BF16)


def read_pieces(whole, pieces, micros):
    heads = len(pieces)
    piece = pieces[0].shape[1]
    for m in range(micros):
        for k in range(heads):
            at = (m * heads + k) * piece
            whole[at : at + piece, :] = pieces[k][m]


def project(pieces, queries, kvs, gain_views, cosine, sine, turn):
    heads = len(pieces)
    micros, piece, d_model = pieces[0].shape
    rows = micros * heads * piece
    half = d_model // 2
    width = queries[0].width

    def kernel(*refs):
        xs = refs[:heads]
        q_own, q_other, kv_own, kv_other, g_own, g_other, cos, sin, turns, eye = refs[heads : heads + 10]
        na, q_out, kv_out, gains = refs[heads + 10 :]
        gains[:, :half] = dot_nt(eye[...], g_own[...])
        gains[:, half:] = dot_nt(eye[...], g_other[...])
        gain = gains[0:1, :]
        for m in range(micros):
            for k in range(heads):
                x = xs[k][m].astype(F32)
                scale = lax.rsqrt(jnp.mean(x * x, axis=-1, keepdims=True) + EPSILON)
                at = (m * heads + k) * piece
                na[at : at + piece, :] = (x * scale * gain).astype(BF16)
        low, high = na[:, :half], na[:, half:]
        for part, (own, other, out) in enumerate(
            ((q_own, q_other, q_out), (kv_own, kv_other, kv_out))
        ):
            lin = dot(low, own[...]) + dot(high, other[...])
            a, b = split_terms(lin)
            turned = dot(a, turns[part]) + dot(b, turns[part])
            at = part * width
            out[...] = (
                lin * cos[:, at : at + width] + turned * sin[:, at : at + width]
            ).astype(BF16)

    eye = jnp.asarray(np.eye(8, LANES), BF16)
    return call(
        kernel,
        "project",
        [*pieces, *queries, *kvs, *gain_views, cosine, sine, turn, eye],
        [kept((rows, d_model)), kept((rows, width)), shape((rows, width)), shape((8, d_model), F32)],
        flops=4 * rows * d_model * width,
    )


def attend(query, pieces, place_q, place_k, pad, outs_w, heads, piece, group):
    ctxs = len(pieces)
    micros, span, width = pieces[0].shape
    keys = ctxs * span
    rows = micros * span
    half = outs_w[0].array.shape[0]
    kv_heads = pad.shape[1] // LANES // 2

    def kernel(*refs):
        q_ref = refs[0]
        kvs = refs[1 : 1 + ctxs]
        pq, pk, pads, w_own, w_other = refs[1 + ctxs : 6 + ctxs]
        prob, mix = refs[6 + ctxs : 8 + ctxs]
        outs = refs[8 + ctxs : 8 + ctxs + heads]
        kv_rows, mixed = refs[8 + ctxs + heads :]
        for m in range(micros):
            for j in range(ctxs):
                kv_rows[j * span : (j + 1) * span, :] = kvs[j][m]
            kv = dot(kv_rows[...], pads[...]).astype(BF16)
            q = dot(q_ref[m * span : (m + 1) * span, :], pads[...]).astype(BF16)
            allowed = pk[m] <= pq[m]
            allowed = jnp.concatenate([allowed] * group, axis=0)
            for a in range(kv_heads):
                q2 = jnp.concatenate(
                    [q[:, (a * group + g) * LANES : (a * group + g + 1) * LANES] for g in range(group)],
                    axis=0,
                )
                key = kv[:, a * LANES : (a + 1) * LANES]
                value = kv[:, (kv_heads + a) * LANES : (kv_heads + a + 1) * LANES]
                scores = jnp.where(allowed, dot_nt(q2, key) * INV_ROOT, MASKED)
                top = jnp.max(scores, axis=-1, keepdims=True)
                weight = jnp.exp(scores - top)
                share = (weight / jnp.sum(weight, axis=-1, keepdims=True)).astype(BF16)
                prob[m * kv_heads + a] = share
                got = dot(share, value).astype(BF16)
                for g in range(group):
                    at = (a * group + g) * LANES
                    mixed[:, at : at + LANES] = got[g * span : (g + 1) * span]
            mix[m * span : (m + 1) * span, :] = dot_nt(mixed[...], pads[...]).astype(BF16)
        for t, w in enumerate((w_own, w_other)):
            branch = dot_nt(mix[...], w[...]).astype(BF16)
            for m in range(micros):
                for k in range(heads):
                    at = (m * heads + k) * piece
                    outs[k][m, :, t * half : (t + 1) * half] = branch[at : at + piece]

    return call(
        kernel,
        "attend",
        [query, *pieces, place_q, place_k, pad, *outs_w],
        [
            kept((micros * kv_heads, group * span, keys)),
            kept((rows, width)),
            *[shape((micros, piece, 2 * half)) for _ in range(heads)],
        ],
        [pltpu.VMEM((keys, width), BF16), pltpu.VMEM((span, pad.shape[1]), BF16)],
        flops=4 * rows * width * (keys + half),
    )


def add_mid(x, terms, gains):
    def kernel(*refs):
        x_ref, gain = refs[0], refs[1]
        parts = refs[2 : 2 + len(terms)]
        mid, nb = refs[2 + len(terms) :]
        total = x_ref[...].astype(F32)
        for part in parts:
            total = total + part[...].astype(F32)
        mid[...] = total
        scale = lax.rsqrt(jnp.mean(total * total, axis=-1, keepdims=True) + EPSILON)
        nb[...] = (total * scale * gain[1:2, :]).astype(BF16)

    return call(
        kernel,
        "add_mid",
        [x, gains, *terms],
        [shape(x.shape, F32), shape(x.shape)],
        limit=VMEM_SMALL,
    )


def add_out(mid, terms):
    def kernel(*refs):
        total = refs[0][...]
        for part in refs[1:-1]:
            total = total + part[...].astype(F32)
        refs[-1][...] = total.astype(BF16)

    return call(kernel, "add_out", [mid, *terms], [shape(mid.shape)], limit=VMEM_SMALL)[0]


def blocks_of(pair, units):
    specs, arrays = [], []
    count = units // UNIT_BLOCK
    for part in range(3):
        for array in pair:
            specs.append(
                pl.BlockSpec(
                    (array.shape[0], UNIT_BLOCK), lambda j, part=part: (0, part * count + j)
                )
            )
            arrays.append(array)
    return specs, arrays


def pack_places(half, units, width):
    hidden_at = 2 * half
    mix_at = -(-(hidden_at + units) // width) * width
    return hidden_at, mix_at


def feed(pieces, pair, units, na, mix):
    heads = len(pieces)
    micros, piece, d_model = pieces[0].shape
    rows = micros * heads * piece
    half = d_model // 2
    count = units // UNIT_BLOCK
    width = mix.shape[1]
    hidden_at, mix_at = pack_places(half, units, width)

    def kernel(*refs):
        xs = refs[:heads]
        gate_w = refs[heads : heads + 2]
        up_w = refs[heads + 2 : heads + 4]
        down_w = refs[heads + 4 : heads + 6]
        na_in, mix_in = refs[heads + 6 : heads + 8]
        gate_out, up_out, hidden_out, nb, packed = refs[heads + 8 : heads + 13]
        outs = refs[heads + 13 : 2 * heads + 13]
        total = refs[-1]
        j = pl.program_id(0)

        @pl.when(j == 0)
        def _():
            read_pieces(nb, xs, micros)
            total[...] = jnp.zeros_like(total)
            packed[:, :half] = na_in[...]
            packed[:, half : 2 * half] = nb[:, half:]
            packed[:, mix_at : mix_at + width] = mix_in[...]

        low, high = nb[:, :half], nb[:, half:]
        gate = dot(low, gate_w[0][...]) + dot(high, gate_w[1][...])
        up = dot(low, up_w[0][...]) + dot(high, up_w[1][...])
        gate_out[...] = gate.astype(BF16)
        up_out[...] = up.astype(BF16)
        hidden = (gate * jax.nn.sigmoid(gate) * up).astype(BF16)
        hidden_out[...] = hidden
        at = pl.multiple_of(hidden_at + j * UNIT_BLOCK, UNIT_BLOCK)
        packed[:, pl.ds(at, UNIT_BLOCK)] = hidden
        total[:, :half] += dot_nt(hidden, down_w[0][...])
        total[:, half:] += dot_nt(hidden, down_w[1][...])

        @pl.when(j == count - 1)
        def _():
            write_pieces(outs, total, micros)

    specs, arrays = blocks_of(pair, units)
    whole = pl.BlockSpec((rows, d_model), lambda j: (0, 0))
    block = pl.BlockSpec((rows, UNIT_BLOCK), lambda j: (0, j))
    rows_spec = pl.BlockSpec((micros, piece, d_model), lambda j: (0, 0, 0))
    return pl.pallas_call(
        kernel,
        grid=(count,),
        in_specs=[rows_spec] * heads
        + specs
        + [pl.BlockSpec((rows, half), lambda j: (0, 1)), pl.BlockSpec(mix.shape, lambda j: (0, 0))],
        out_specs=[block, block, block, whole]
        + [pl.BlockSpec((rows, mix_at + width), lambda j: (0, 0))]
        + [rows_spec] * heads,
        out_shape=[
            kept((rows, units)),
            kept((rows, units)),
            kept((rows, units)),
            kept((rows, d_model)),
            kept((rows, mix_at + width)),
            *[shape((micros, piece, d_model)) for _ in range(heads)],
        ],
        scratch_shapes=[pltpu.VMEM((rows, d_model), F32)],
        compiler_params=pltpu.CompilerParams(vmem_limit_bytes=VMEM_LARGE),
        cost_estimate=pl.CostEstimate(
            flops=6 * rows * d_model * units, bytes_accessed=6 * d_model * units, transcendentals=0
        ),
        name="feed",
    )(*pieces, *arrays, na, mix)


def feed_back(pieces, pair, gate, up):
    heads = len(pieces)
    micros, piece, d_model = pieces[0].shape
    rows, units = gate.shape
    half = d_model // 2
    count = units // UNIT_BLOCK

    def kernel(*refs):
        xs = refs[:heads]
        gate_w = refs[heads : heads + 2]
        up_w = refs[heads + 2 : heads + 4]
        down_w = refs[heads + 4 : heads + 6]
        gate_in, up_in = refs[heads + 6 : heads + 8]
        d_gate_out, d_up_out, gf, packed = refs[heads + 8 : heads + 12]
        outs = refs[heads + 12 : 2 * heads + 12]
        total = refs[-1]
        j = pl.program_id(0)

        @pl.when(j == 0)
        def _():
            read_pieces(gf, xs, micros)
            total[...] = jnp.zeros_like(total)
            packed[:, :half] = gf[:, half:]

        d_hidden = dot(gf[:, :half], down_w[0][...]) + dot(gf[:, half:], down_w[1][...])
        gate_v, up_v = gate_in[...].astype(F32), up_in[...].astype(F32)
        sigma = jax.nn.sigmoid(gate_v)
        d_gate = (d_hidden * up_v * sigma * (1.0 + gate_v * (1.0 - sigma))).astype(BF16)
        d_up = (d_hidden * gate_v * sigma).astype(BF16)
        d_gate_out[...] = d_gate
        d_up_out[...] = d_up
        at = pl.multiple_of(half + j * UNIT_BLOCK, UNIT_BLOCK)
        packed[:, pl.ds(at, UNIT_BLOCK)] = d_gate
        at = pl.multiple_of(half + units + j * UNIT_BLOCK, UNIT_BLOCK)
        packed[:, pl.ds(at, UNIT_BLOCK)] = d_up
        total[:, :half] += dot_nt(d_gate, gate_w[0][...]) + dot_nt(d_up, up_w[0][...])
        total[:, half:] += dot_nt(d_gate, gate_w[1][...]) + dot_nt(d_up, up_w[1][...])

        @pl.when(j == count - 1)
        def _():
            write_pieces(outs, total, micros)

    specs, arrays = blocks_of(pair, units)
    whole = pl.BlockSpec((rows, d_model), lambda j: (0, 0))
    block = pl.BlockSpec((rows, UNIT_BLOCK), lambda j: (0, j))
    rows_spec = pl.BlockSpec((micros, piece, d_model), lambda j: (0, 0, 0))
    return pl.pallas_call(
        kernel,
        grid=(count,),
        in_specs=[rows_spec] * heads + specs + [block, block],
        out_specs=[block, block, whole]
        + [pl.BlockSpec((rows, half + 2 * units), lambda j: (0, 0))]
        + [rows_spec] * heads,
        out_shape=[
            kept((rows, units)),
            kept((rows, units)),
            kept((rows, d_model)),
            kept((rows, half + 2 * units)),
            *[shape((micros, piece, d_model)) for _ in range(heads)],
        ],
        scratch_shapes=[pltpu.VMEM((rows, d_model), F32)],
        compiler_params=pltpu.CompilerParams(vmem_limit_bytes=VMEM_LARGE),
        cost_estimate=pl.CostEstimate(
            flops=6 * rows * d_model * units, bytes_accessed=6 * d_model * units, transcendentals=0
        ),
        name="feed_back",
    )(*pieces, *arrays, gate, up)


def norm_back(terms, residual, gains, row, carried):
    d_model = residual.shape[-1]

    def kernel(*refs):
        res, gain, carry = refs[:3]
        parts = refs[3 : 3 + len(terms)]
        d_out, d_low, d_gain = refs[3 + len(terms) :]
        d_normed = parts[0][...].astype(F32)
        for part in parts[1:]:
            d_normed = d_normed + part[...].astype(F32)
        rows = res[...].astype(F32)
        scale = lax.rsqrt(jnp.mean(rows * rows, axis=-1, keepdims=True) + EPSILON)
        unit = rows * scale
        d_gain[...] = jnp.sum(jnp.sum(d_normed * unit, axis=0), axis=0, keepdims=True)
        d_unit = d_normed * gain[row : row + 1, :]
        total = carry[...].astype(F32) + scale * (
            d_unit - unit * jnp.mean(d_unit * unit, axis=-1, keepdims=True)
        )
        d_out[...] = total
        d_low[...] = total.astype(BF16)

    return call(
        kernel,
        "norm_back",
        [residual, gains, carried, *terms],
        [shape(residual.shape, F32), shape(residual.shape), shape((1, d_model), F32)],
        limit=VMEM_SMALL,
    )


def attend_back(pieces, outs_w, mix, prob, query, kv_pieces, pad, turn, cosine, sine, group):
    heads = len(pieces)
    micros, piece, d_model = pieces[0].shape
    span = heads * piece
    rows = micros * span
    half = d_model // 2
    ctxs = len(kv_pieces)
    width = query.shape[1]
    keys = ctxs * span
    kv_heads = pad.shape[1] // LANES // 2

    def kernel(*refs):
        xs = refs[:heads]
        w_own, w_other, mix_in, prob_in, q_ref = refs[heads : heads + 5]
        kvs = refs[heads + 5 : heads + 5 + ctxs]
        pads, turns, cos, sin = refs[heads + 5 + ctxs : heads + 9 + ctxs]
        ga, ga_other, dq_out = refs[heads + 9 + ctxs : heads + 12 + ctxs]
        outs = refs[heads + 12 + ctxs : heads + 12 + 2 * ctxs]
        kv_rows, d_kv, d_q = refs[heads + 12 + 2 * ctxs :]
        read_pieces(ga, xs, micros)
        ga_other[...] = ga[:, half:]
        d_mix = (dot(ga[:, :half], w_own[...]) + dot(ga[:, half:], w_other[...])).astype(BF16)
        for m in range(micros):
            for j in range(ctxs):
                kv_rows[j * span : (j + 1) * span, :] = kvs[j][m]
            here = slice(m * span, (m + 1) * span)
            kv = dot(kv_rows[...], pads[...]).astype(BF16)
            q = dot(q_ref[here, :], pads[...]).astype(BF16)
            d = dot(d_mix[here], pads[...])
            product = d * dot(mix_in[here, :], pads[...])
            d = d.astype(BF16)
            for a in range(kv_heads):
                cuts = [slice((a * group + g) * LANES, (a * group + g + 1) * LANES) for g in range(group)]
                q2 = jnp.concatenate([q[:, cut] for cut in cuts], axis=0)
                d2 = jnp.concatenate([d[:, cut] for cut in cuts], axis=0)
                delta = jnp.concatenate(
                    [jnp.sum(product[:, cut], axis=-1, keepdims=True) for cut in cuts], axis=0
                )
                key = kv[:, a * LANES : (a + 1) * LANES]
                value = kv[:, (kv_heads + a) * LANES : (kv_heads + a + 1) * LANES]
                share = prob_in[m * kv_heads + a]
                d_prob = dot_nt(d2, value)
                d_score = (share.astype(F32) * (d_prob - delta)).astype(BF16)
                back = dot(d_score, key)
                for g, cut in enumerate(cuts):
                    d_q[:, cut] = back[g * span : (g + 1) * span]
                d_kv[:, a * LANES : (a + 1) * LANES] = dot_tn(d_score, q2).astype(BF16)
                d_kv[:, (kv_heads + a) * LANES : (kv_heads + a + 1) * LANES] = dot_tn(
                    share, d2
                ).astype(BF16)
            packed = dot_nt(d_kv[...], pads[...]).astype(BF16)
            for j in range(ctxs):
                outs[j][m] = packed[j * span : (j + 1) * span]
            high, low = split_terms(d_q[...])
            line = (dot_nt(high, pads[...]) + dot_nt(low, pads[...])) * INV_ROOT
            high, low = split_terms(line)
            turned = dot_nt(high, turns[0]) + dot_nt(low, turns[0])
            dq_out[here, :] = (line * cos[here, :width] + turned * sin[here, :width]).astype(BF16)

    return call(
        kernel,
        "attend_back",
        [*pieces, *outs_w, mix, prob, query, *kv_pieces, pad, turn, cosine, sine],
        [
            kept((rows, d_model)),
            shape((rows, half)),
            shape((rows, width)),
            *[shape((micros, span, width)) for _ in range(ctxs)],
        ],
        [
            pltpu.VMEM((keys, width), BF16),
            pltpu.VMEM((keys, pad.shape[1]), BF16),
            pltpu.VMEM((span, pad.shape[1]), F32),
        ],
        flops=10 * rows * width * keys,
    )


def project_back(terms, dq, queries, kvs, turn, cosine, sine, row_pieces):
    heads = len(row_pieces)
    micros, span, width = terms[0].shape
    rows = micros * span
    piece = span // heads
    half = queries[0].array.shape[0]
    count = len(terms)

    def kernel(*refs):
        parts = refs[:count]
        dq_in, q_own, q_other, kv_own, kv_other, turns, cos, sin = refs[count : count + 8]
        xs = refs[count + 8 : count + 8 + heads]
        d_line, d_gain = refs[count + 8 + heads : count + 10 + heads]
        outs = refs[count + 10 + heads : count + 10 + 2 * heads]
        unit = refs[-1]
        for m in range(micros):
            for k in range(heads):
                x = xs[k][m].astype(F32)
                scale = lax.rsqrt(jnp.mean(x * x, axis=-1, keepdims=True) + EPSILON)
                at = (m * heads + k) * piece
                unit[at : at + piece, :] = x * scale
        d_line[:, :width] = dq_in[...]
        lanes = lax.broadcasted_iota(jnp.int32, (span, width), 1)
        scaled = jnp.where(lanes < width // 2, INV_ROOT, 1.0)
        for m in range(micros):
            here = slice(m * span, (m + 1) * span)
            total = parts[0][m].astype(F32)
            for part in parts[1:]:
                total = total + part[m].astype(F32)
            total = total * scaled
            high, low = split_terms(total)
            turned = dot_nt(high, turns[1]) + dot_nt(low, turns[1])
            d_line[here, width:] = (
                total * cos[here, width:] + turned * sin[here, width:]
            ).astype(BF16)
        for t, (wq, wkv) in enumerate(((q_own, kv_own), (q_other, kv_other))):
            branch = dot_nt(d_line[:, :width], wq[...]) + dot_nt(d_line[:, width:], wkv[...])
            side = slice(t * half, (t + 1) * half)
            d_gain[:, side] = jnp.sum(branch * unit[:, side], axis=0, keepdims=True)
            branch = branch.astype(BF16)
            for m in range(micros):
                for k in range(heads):
                    at = (m * heads + k) * piece
                    outs[k][m, :, t * half : (t + 1) * half] = branch[at : at + piece]

    return call(
        kernel,
        "project_back",
        [*terms, dq, *queries, *kvs, turn, cosine, sine, *row_pieces],
        [
            kept((rows, 2 * width)),
            shape((1, 2 * half), F32),
            *[shape((micros, piece, 2 * half)) for _ in range(heads)],
        ],
        [pltpu.VMEM((rows, 2 * half), F32)],
        flops=8 * rows * half * width,
    )


def weight_grad(groups):
    half = groups[0][0][0].width
    total = sum(group[0][1].width for group in groups)
    args = [view for group in groups for pair in group for view in pair]

    def kernel(*refs):
        out = refs[-1]
        at = 0
        for g, group in enumerate(groups):
            n = group[0][1].width
            a, b, c, d = refs[4 * g : 4 * g + 4]
            out[:, at : at + n] = (dot_tn(a[...], b[...]) + dot_tn(c[...], d[...])).astype(BF16)
            at += n

    rows = groups[0][0][0].array.shape[0]
    return call(
        kernel, "weight_grad", args, [shape((half, total))], flops=4 * half * rows * total
    )[0]


def late_grad(nb, gf, d_gate, d_up, hidden, packed, packed_back):
    rows, d_model = nb.shape
    units = hidden.shape[1]
    half = d_model // 2
    count = units // UNIT_BLOCK
    hidden_at, _ = pack_places(half, units, LANES)

    def kernel(*refs):
        sides = refs[:4]
        lines = refs[4:10]
        out = refs[10]
        turned = refs[11:]
        j = pl.program_id(0)

        @pl.when(j == 0)
        def _():
            for side, flat in zip(sides, turned):
                flat[...] = side[...].T

        for part in range(3):

            @pl.when(j // count == part)
            def _(part=part):
                which = (0, 0, 1)[part]
                out[...] = (
                    dot(turned[which][...], lines[part][...])
                    + dot(turned[2 + which][...], lines[3 + part][...])
                ).astype(BF16)

    def side(block):
        return pl.BlockSpec((rows, half), lambda j: (0, block))

    def line(part, first):
        return pl.BlockSpec(
            (rows, UNIT_BLOCK),
            lambda j: (0, first // UNIT_BLOCK + jnp.clip(j - part * count, 0, count - 1)),
        )

    return pl.pallas_call(
        kernel,
        grid=(3 * count,),
        in_specs=[side(0), side(0), side(1), side(0)]
        + [line(part, 0) for part in range(3)]
        + [line(0, half), line(1, half + units), line(2, hidden_at)],
        out_specs=pl.BlockSpec((half, UNIT_BLOCK), lambda j: (0, j)),
        out_shape=kept((half, 3 * units)),
        scratch_shapes=[pltpu.VMEM((half, rows), BF16)] * 4,
        compiler_params=pltpu.CompilerParams(vmem_limit_bytes=VMEM_LARGE),
        cost_estimate=pl.CostEstimate(
            flops=12 * half * rows * units, bytes_accessed=6 * half * units, transcendentals=0
        ),
        name="late_grad",
    )(nb, gf, packed, packed_back, d_gate, d_up, hidden, packed_back, packed_back, packed)


def relative_columns(value, section, ctxs):
    width = value.shape[-1] // (2 * ctxs)
    return jnp.concatenate(
        [
            lax.dynamic_slice_in_dim(
                value, (k * 2 + (section ^ t)) * width, width, axis=value.ndim - 1
            )
            for t in range(2)
            for k in range(ctxs)
        ],
        axis=-1,
    )


def stored_columns(value, section, ctxs):
    width = value.shape[-1] // (2 * ctxs)
    return jnp.concatenate(
        [
            lax.dynamic_slice_in_dim(
                value, ((section ^ t) * ctxs + k) * width, width, axis=value.ndim - 1
            )
            for k in range(ctxs)
            for t in range(2)
        ],
        axis=-1,
    )


def send_all(pieces, axis):
    return [pieces[0]] + [swap(piece, axis, k) for k, piece in enumerate(pieces[1:], 1)]


def send_rows(rows):
    return send_all([rows] * lax.axis_size("head"), "head")


def send_blocks(rows):
    return send_all([rows] * lax.axis_size("ctx"), "ctx")


class Fetch:
    def __init__(self, shard):
        self.shard = shard

    def send(self, gate=None):
        self.pieces = send_blocks(self.shard if gate is None else after(self.shard, gate))

    def settle(self, gate=None):
        own = place(after(self.pieces, gate), lax.axis_index("ctx"))
        self.pair = (own, swap(own, "section", 1))
        return self.pair

    def direct(self, gate=None, with_rows=None):
        shard = self.shard if gate is None else after(self.shard, gate)
        pieces = send_blocks(shard)
        if with_rows is not None:
            pieces = after(pieces, with_rows)
        own = place(pieces, lax.axis_index("ctx"))
        self.pair = (own, swap(own, "section", 1))
        return pieces[1:]

    def first(self, gate=None):
        shard = self.shard if gate is None else after(self.shard, gate)
        self.own = lax.all_gather(shard, "ctx", axis=0, tiled=True)
        return self.own

    def second(self, gate=None):
        own = self.own if gate is None else after(self.own, gate)
        self.pair = (own, swap(own, "section", 1))
        return self.pair[1]


class Settle:
    def __init__(self, source):
        self.source = source

    def first(self, whole):
        self.kept = lax.psum_scatter(whole, "ctx", scatter_dimension=0, tiled=True)
        return whole

    def direct(self, whole, gate=None):
        if gate is not None:
            whole = after(whole, gate)
        ctxs = lax.axis_size("ctx")
        ctx = lax.axis_index("ctx")
        size = whole.shape[0] // ctxs
        parts = [
            lax.dynamic_slice_in_dim(whole, (ctx ^ k) * size, size, axis=0) for k in range(ctxs)
        ]
        total = None
        for term in send_all(parts, "ctx"):
            term = term.astype(F32)
            total = term if total is None else total + term
        self.kept = total.astype(BF16)
        return whole

    def second(self, gate=None):
        kept = self.kept if gate is None else after(self.kept, gate)
        self.kept = kept
        sent = swap_from(kept, self.source)
        self.halves = (kept, sent) if self.source == 1 else (sent, kept)
        return sent


class Chain:
    def __init__(self):
        self.tasks = {}
        self.due = {}

    def plan(self, start, end, task):
        self.tasks.setdefault(start, []).append((end, task))

    def enter(self, name, value):
        done = self.due.pop(name, [])
        return after(value, done) if done else value

    def leave(self, name, value):
        for end, task in self.tasks.pop(name, []):
            result = task(value)
            if end is not None:
                self.due.setdefault(end, []).append(result)


class Plan:
    pass


def pick(first, a, b):
    return jnp.where(first, a, b)


def turning(heads_turned, heads):
    turn = np.zeros((heads * HEAD_DIM, heads * HEAD_DIM), np.float32)
    for h in range(heads_turned):
        for i in range(HALF):
            turn[h * HEAD_DIM + HALF + i, h * HEAD_DIM + i] = -1.0
            turn[h * HEAD_DIM + i, h * HEAD_DIM + HALF + i] = 1.0
    return turn


def padding(heads):
    pad = np.zeros((heads * HEAD_DIM, heads * LANES), np.float32)
    for h in range(heads):
        for i in range(HEAD_DIM):
            pad[h * HEAD_DIM + i, h * LANES + i] = 1.0
    return pad


def local(
    layer_input,
    out_cotangent,
    block_order,
    gain_attn,
    w_query,
    w_key,
    w_value,
    w_out,
    gain_ffn,
    w_gate,
    w_up,
    w_down,
):
    section = lax.axis_index("section")
    head = lax.axis_index("head")
    ctx = lax.axis_index("ctx")
    heads = lax.axis_size("head")
    ctxs = lax.axis_size("ctx")
    first = section == 0
    micros_all = layer_input.shape[0] // 2
    micros = micros_all // GROUPS
    rows_dev = layer_input.shape[1]
    d_model = layer_input.shape[2]
    span = heads * rows_dev
    rows = micros * span
    block_rows = ctxs * span // block_order.shape[1]
    d_half = d_model // ctxs // 2
    width = w_query.shape[2]
    k_width = w_key.shape[2]
    units = w_gate.shape[2]
    group_size = width // k_width
    line_heads = width // HEAD_DIM
    chain = Chain()

    turn = jnp.asarray(
        np.stack([turning(line_heads, line_heads), turning(k_width // HEAD_DIM, line_heads)]), BF16
    )
    pad = jnp.asarray(padding(line_heads), BF16)

    def places_of(order, ctx_index):
        piece = jnp.arange(span, dtype=jnp.int32)
        stored = (ctx_index * heads + (head ^ (piece // rows_dev))) * rows_dev + piece % rows_dev
        block = stored // block_rows
        match = block[:, None] == jnp.arange(order.shape[1], dtype=jnp.int32)[None, :]
        base = jnp.sum(jnp.where(match[None], order[:, None, :], 0), axis=2)
        return base * block_rows + (stored % block_rows)[None]

    frequency = jnp.power(ROPE_BASE, jnp.arange(HALF, dtype=F32) * (-2.0 / HEAD_DIM))

    def group_of(index):
        group = Plan()
        at = section * micros_all + index * micros
        group.name = "ab"[index]
        order = lax.dynamic_slice_in_dim(block_order, at, micros, axis=0)
        places_q = places_of(order, ctx)
        places_k = jnp.concatenate([places_of(order, ctx ^ k) for k in range(ctxs)], axis=1)
        group.place_q = places_q[:, :, None]
        group.place_k = places_k[:, None, :]
        group.places = places_q

        def make_tables(places):
            angles = places.reshape(rows, 1).astype(F32) * frequency
            cosine, sine = jnp.cos(angles), jnp.sin(angles)
            turned = 2 * (line_heads + k_width // HEAD_DIM)
            fixed = width - k_width
            group.cosine = jnp.concatenate(
                [cosine] * turned + [jnp.ones((rows, fixed), F32)], axis=1
            )
            group.sine = jnp.concatenate(
                [sine] * turned + [jnp.zeros((rows, fixed), F32)], axis=1
            )

        group.make_tables = make_tables

        def mine(value):
            part = lax.dynamic_slice_in_dim(value, at, micros, axis=0)
            return relative_columns(part, section, ctxs)

        group.x = mine(layer_input)
        group.cot = mine(out_cotangent)
        group.keep, group.d_in = {}, {}
        return group

    members = [group_of(index) for index in range(GROUPS)]
    tail = members[-1].name
    for group in members:
        group.firsts = send_rows(group.x)
        group.cot_pieces = [group.cot] * heads

    def exchange(shard, gate=None):
        def cut(which):
            return lax.dynamic_slice_in_dim(shard, which * d_half, d_half, axis=0)

        kept, given = cut(section), cut(1 - section)
        if gate is not None:
            given = after(given, gate)
        taken = swap(given, "section", 1)
        return pick(first, kept, taken), pick(first, taken, kept)

    gains = jnp.stack([gain_attn[0], gain_ffn[0]], axis=1)
    gains = jnp.pad(gains, ((0, 0), (0, LANES - 2)))
    early_shards = exchange(
        jnp.concatenate([w_query[0], w_key[0], w_value[0], gains], axis=1)
    )
    early0 = Fetch(early_shards[0])
    early0.send([group.firsts[1] for group in members])
    tables = after([group.places for group in members], early0.pieces[1])
    for group, places in zip(members, tables):
        group.make_tables(places)
    early0.settle([(group.cosine, group.sine, group.firsts) for group in members])
    landed = early0.pair[:1]
    w_late, w_o = after(((w_gate[0], w_up[0], w_down[0]), w_out[0]), landed)
    out_shards = exchange(w_o.T)
    late_shards = exchange(jnp.concatenate([w_late[0], w_late[1], w_late[2].T], axis=1))
    late0, late1 = Fetch(late_shards[0]), Fetch(late_shards[1])
    out0 = Fetch(out_shards[0])
    both1 = Fetch(jnp.concatenate([out_shards[1], early_shards[1]], axis=1))
    late0.first(landed)
    out0.send(landed)

    def views0(name):
        if name == "o":
            return [View(part, width, 0) for part in out0.pair]
        at = {"q": (width, 0), "kv": (width, 1), "g": (LANES, 2 * width // LANES)}[name]
        return [View(part, *at) for part in early0.pair]

    def views1(name):
        at = {
            "o": (width, 0),
            "q": (width, 1),
            "kv": (width, 2),
            "g": (LANES, 3 * width // LANES),
        }[name]
        return [View(part, *at) for part in both1.pair]

    token = [None]

    def enter(name, group, value):
        if token[0] is not None and GROUPS > 1:
            value = after(value, token[0])
        return chain.enter(name + group.name, value)

    def leave(name, group, value):
        token[0] = value
        chain.leave(name + group.name, value)

    def forward(label, group, layer_in, views, late_fetch):
        keep = Plan()
        keep.x = layer_in
        pieces = group.firsts if label == "0" else send_rows(layer_in)
        leave(label + "F0", group, layer_in)
        yield
        pieces = enter(label + "F1", group, pieces)
        keep.x_pieces = pieces
        keep.na, keep.query, kv, keep.gains = project(
            pieces, views("q"), views("kv"), views("g"), group.cosine, group.sine, turn
        )
        kv = kv.reshape(micros, span, width)
        pieces = send_blocks(kv)
        leave(label + "F1", group, kv)
        yield
        keep.kv = enter(label + "F2", group, pieces)
        keep.prob, keep.mix, *parts = attend(
            keep.query, keep.kv, group.place_q, group.place_k, pad, views("o"),
            heads, rows_dev, group_size,
        )
        terms = send_all(parts, "head")
        leave(label + "F2", group, parts[0])
        yield
        terms = enter(label + "F3", group, terms)
        keep.mid, own_nb = add_mid(layer_in, terms, keep.gains)
        pieces = send_rows(own_nb)
        leave(label + "F3", group, own_nb)
        yield
        pieces = enter(label + "F4", group, pieces)
        keep.late = late_fetch.pair
        keep.gate, keep.up, keep.hidden, keep.nb, packed, *parts = feed(
            pieces, keep.late, units, keep.na, keep.mix
        )
        keep.packed = swap(packed, "section", 1)
        group.parts = parts
        group.keep[label] = keep
        leave(label + "F4", group, parts[0])
        if label == "0":
            terms = send_all(parts, "head")
            yield
            terms = enter(label + "F5", group, terms)
            group.out = add_out(keep.mid, terms)

    def backward(label, group, pieces, grad, views):
        keep = group.keep[label]
        if label == "0":
            pieces = enter(label + "B1", group, pieces)
        keep.d_gate, keep.d_up, keep.gf, packed, *parts = feed_back(
            pieces, keep.late, keep.gate, keep.up
        )
        keep.packed_back = swap(packed, "section", 1)
        terms = send_all(parts, "head")
        leave(label + "B1", group, parts[0])
        yield
        terms = enter(label + "B2", group, terms)
        d_mid, own_ga, keep.gain_b = norm_back(terms, keep.mid, keep.gains, 1, grad)
        pieces = send_rows(own_ga)
        leave(label + "B2", group, own_ga)
        yield
        pieces = enter(label + "B3", group, pieces)
        keep.ga, ga_other, dq, *parts = attend_back(
            pieces, views("o"), keep.mix, keep.prob, keep.query, keep.kv, pad, turn,
            group.cosine, group.sine, group_size,
        )
        terms = send_all(parts, "ctx")
        keep.ga_other = swap(ga_other, "section", 1)
        leave(label + "B3", group, parts[0])
        yield
        terms = enter(label + "B4", group, terms)
        keep.d_line, keep.gain_a, *parts = project_back(
            terms, dq, views("q"), views("kv"), turn, group.cosine, group.sine, keep.x_pieces
        )
        terms = send_all(parts, "head")
        keep.d_line_other = swap(keep.d_line, "section", 1)
        leave(label + "B4", group, parts[0])
        yield
        terms = enter(label + "B5", group, terms)
        d_input, d_low, _ = norm_back(terms, keep.x, keep.gains, 0, d_mid)
        if label == "1":
            group.d_in[label] = d_low
            group.pieces = send_rows(d_low)
        else:
            group.d_in[label] = d_input
        leave(label + "B5", group, group.d_in[label])
        yield

    def drive(*stages):
        waiting = list(stages)
        while waiting:
            waiting = [stage for stage in waiting if next(stage, stage) is not stage]

    def gather_cot(group, which):
        def task(gate):
            for k in which:
                if k < heads:
                    group.cot_pieces[k] = swap(after(group.cot, gate), "head", k)
            return group.cot_pieces[1:]

        return task

    for group in members:
        chain.plan("0F1" + group.name, "0F2" + group.name, gather_cot(group, [2, 1]))
        chain.plan("1F1" + group.name, "1F2" + group.name, gather_cot(group, range(3, heads)))

    def on_last(start, end, task):
        chain.plan(start + tail, end + tail if end else None, task)

    on_last("0F1", "0F2", out0.settle)
    on_last("0F3", None, late0.second)
    on_last("0F3", None, lambda gate: both1.first(late0.pair[0]))
    on_last("1F0", None, both1.second)
    on_last("1F0", None, lambda gate: late1.first(both1.pair[0]))
    on_last("1F3", None, late1.second)
    drive(*(forward("0", group, group.x, views0, late0) for group in members))

    def scatter_out(group, which):
        def task(gate):
            group.terms += [
                swap(after(group.parts[k], gate), "head", k) for k in which if k < heads
            ]
            return group.terms[1:]

        return task

    def finish_out(group):
        def task(gate):
            group.final = add_out(group.keep["1"].mid, group.terms)
            return group.final

        return task

    drive(*(forward("1", group, group.out, views1, late1) for group in members))
    for group in members:
        group.terms = [group.parts[0]]
        chain.plan("1B3" + group.name, "1B4" + group.name, scatter_out(group, [2, 1]))
        chain.plan("0B3" + group.name, "0B4" + group.name, scatter_out(group, range(3, heads)))
        chain.plan("0B4" + group.name, "0B5" + group.name, finish_out(group))

    _, mix_at = pack_places(d_model // 2, units, width)

    def rows_of(label, *names):
        def joined(name):
            parts = [getattr(group.keep[label], name) for group in members]
            return parts[0] if len(parts) == 1 else jnp.concatenate(parts, axis=0)

        return [joined(name) for name in names]

    def late_of(label, gate):
        names = ("nb", "gf", "d_gate", "d_up", "hidden", "packed", "packed_back")
        return late_grad(*after(rows_of(label, *names), gate))

    def out_group(ga, mix, ga_other, packed):
        return (
            (View(ga, d_model // 2, 0), View(mix)),
            (View(ga_other), View(packed, width, mix_at // width)),
        )

    def early_group(na, d_line, packed, d_line_other):
        return (
            (View(na, d_model // 2, 0), View(d_line)),
            (View(packed, d_model // 2, 0), View(d_line_other)),
        )

    out_names = ("ga", "mix", "ga_other", "packed")
    early_names = ("na", "d_line", "packed", "d_line_other")

    def out_of(label, gate):
        return weight_grad([out_group(*after(rows_of(label, *out_names), gate))])

    def early_of(label, gate):
        return weight_grad([early_group(*after(rows_of(label, *early_names), gate))])

    def both_of(label, gate):
        values = after(rows_of(label, *out_names, *early_names), gate)
        return weight_grad([out_group(*values[:4]), early_group(*values[4:])])

    late_1, both_1, late_0, out_0, early_0 = (Settle(s) for s in (0, 0, 1, 1, 1))
    on_last("1B2", "1B3", lambda gate: late_1.first(late_of("1", gate)))
    on_last("1B5", "0B1", late_1.second)
    on_last("1B5", "0B1", lambda gate: both_1.first(both_of("1", (gate, late_1.kept))))
    on_last("0B2", "0B3", both_1.second)
    on_last("0B2", "0B3", lambda gate: late_0.first(late_of("0", (gate, both_1.kept))))
    on_last("0B3", "0B4", lambda gate: out_0.direct(out_of("0", gate)))
    on_last("0B4", "0B5", late_0.second)
    last = []

    def last_grad(gate):
        last.append(early_of("0", gate))
        return last[0]

    on_last("0B4", "0B5", last_grad)
    on_last("0B5", None, lambda gate: early_0.direct(last[0], gate))
    gain_mine = []

    def sum_gains(gate):
        def gain_of(label, name):
            total = getattr(members[0].keep[label], name)
            for group in members[1:]:
                total = total + getattr(group.keep[label], name)
            return total[0]

        gain_rows = jnp.stack(
            [gain_of(label, name) for label in "01" for name in ("gain_a", "gain_b")]
        )
        gain_rows = stored_columns(gain_rows, section, ctxs)
        total = lax.psum(gain_rows, ("section", "head", "ctx"))
        two = lax.dynamic_slice_in_dim(total, section * 2, 2, axis=0)
        gain_mine.append(
            lax.dynamic_slice_in_dim(two, ctx * 2 * d_half, 2 * d_half, axis=1)
        )
        return gain_mine[0]

    def by_layer(lower, upper):
        lower = stored_columns(lower, section, ctxs)
        upper = stored_columns(upper, section, ctxs)
        kept_rows = pick(first, lower, upper)
        got_rows = swap(pick(first, upper, lower).astype(BF16), "section", 1).astype(lower.dtype)
        return jnp.concatenate(
            [pick(first, kept_rows, got_rows), pick(first, got_rows, kept_rows)], axis=0
        )[None]

    def all_rows(name):
        parts = [name(group) for group in members]
        return parts[0] if len(parts) == 1 else jnp.concatenate(parts, axis=0)

    layer_outs = []

    def out_rows(gate):
        lower, upper = after((all_rows(lambda g: g.out), all_rows(lambda g: g.final)), gate)
        layer_outs.append(by_layer(lower, upper))
        return layer_outs[0]

    on_last("0B5", None, out_rows)
    on_last("0B4", None, sum_gains)
    drive(*(backward("1", group, group.cot_pieces, group.cot, views1) for group in members))
    drive(*(backward("0", group, group.pieces, group.d_in["1"], views0) for group in members))
    out_0.second()
    early_0.second()

    def shard_of(lower, upper):
        return jnp.concatenate([pick(first, a, b) for a, b in zip(lower, upper)], axis=0)

    out_grad = shard_of(out_0.halves, [part[:, :width] for part in both_1.halves]).astype(F32)
    early_grad = shard_of(early_0.halves, [part[:, width:] for part in both_1.halves]).astype(F32)
    late = shard_of(late_0.halves, late_1.halves).astype(F32)
    g_query = early_grad[:, :width]
    g_key = early_grad[:, width : width + k_width]
    g_value = early_grad[:, width + k_width :]
    g_out = out_grad.T
    g_gate = late[:, :units]
    g_up = late[:, units : 2 * units]
    g_down = late[:, 2 * units :].T

    in_grad = by_layer(
        all_rows(lambda g: g.d_in["0"]), all_rows(lambda g: g.d_in["1"]).astype(F32)
    )
    return (
        layer_outs[0],
        in_grad,
        gain_mine[0][0][None],
        g_query[None],
        g_key[None],
        g_value[None],
        g_out[None],
        gain_mine[0][1][None],
        g_gate[None],
        g_up[None],
        g_down[None],
    )


def solution(mesh):
    row_spec = P(None, ("ctx", "head"), None)
    vector = P("section", "ctx")
    tall = P("section", "ctx", "head")
    wide = P("section", "head", "ctx")
    kept_rows = P("section", None, ("ctx", "head"), None)
    return jax.shard_map(
        local,
        mesh=mesh,
        in_specs=(row_spec, row_spec, P(), vector, tall, tall, tall, wide, vector, tall, tall, wide),
        out_specs=(kept_rows, kept_rows, vector, tall, tall, tall, wide, vector, tall, tall, wide),
        check_vma=False,
    )
```

```python
import jax
import jax.numpy as jnp
import numpy as np
from jax import lax
from jax.experimental import pallas as pl
from jax.experimental.pallas import tpu as pltpu
from jax.sharding import PartitionSpec as P

HEAD_DIM = 96
HALF = HEAD_DIM // 2
INV_ROOT = HEAD_DIM ** (-0.5)
EPSILON = 1e-05
ROPE_BASE = 100000.0
MASKED = -1e30
LANES = 128
UNIT_BLOCK = 512
F32 = jnp.float32
BF16 = jnp.bfloat16
GROUPS = 1
VMEM_LARGE = 60 * 1024 * 1024
VMEM_SMALL = 12 * 1024 * 1024


def swap(value, axis, step):
    count = lax.axis_size(axis)
    return lax.ppermute(value, axis, [(i, i ^ step) for i in range(count)])


def swap_from(value, source):
    return lax.ppermute(value, "section", [(source, 1 - source)])


def after(value, earlier):
    return lax.optimization_barrier((value, earlier))[0]


def dot(left, right):
    return jnp.dot(left, right, preferred_element_type=F32)


def dot_nt(left, right):
    return lax.dot_general(left, right, (((1,), (1,)), ((), ())), preferred_element_type=F32)


def dot_tn(left, right):
    return lax.dot_general(left, right, (((0,), (0,)), ((), ())), preferred_element_type=F32)


def split_terms(value):
    high = value.astype(BF16)
    return high, (value - high.astype(F32)).astype(BF16)


def shape(dims, dtype=BF16):
    return jax.ShapeDtypeStruct(dims, dtype)


def kept(dims, dtype=BF16):
    return pltpu.HBM(dims, dtype)


class View:
    def __init__(self, array, width=None, block=0):
        self.array = array
        self.width = array.shape[-1] if width is None else width
        self.block = block


def call(kernel, name, args, outs, scratch=(), flops=0, limit=VMEM_LARGE):
    specs, arrays = [], []
    size = 0
    for arg in args:
        if isinstance(arg, View):
            block = arg.block
            specs.append(
                pl.BlockSpec((arg.array.shape[0], arg.width), lambda i, block=block: (0, block))
            )
            arrays.append(arg.array)
            size += arg.array.shape[0] * arg.width * arg.array.dtype.itemsize
        else:
            zeros = (0,) * arg.ndim
            specs.append(pl.BlockSpec(arg.shape, lambda i, zeros=zeros: zeros))
            arrays.append(arg)
            size += arg.size * arg.dtype.itemsize
    out_specs = [
        pl.BlockSpec(out.shape, lambda i, zeros=(0,) * len(out.shape): zeros) for out in outs
    ]
    size += sum(int(np.prod(out.shape)) * jnp.dtype(out.dtype).itemsize for out in outs)
    return pl.pallas_call(
        kernel,
        grid=(1,),
        in_specs=specs,
        out_specs=out_specs,
        out_shape=outs,
        scratch_shapes=list(scratch),
        compiler_params=pltpu.CompilerParams(vmem_limit_bytes=limit),
        cost_estimate=pl.CostEstimate(flops=flops, bytes_accessed=size, transcendentals=0),
        name=name,
    )(*arrays)


def place(pieces, ctx):
    count = len(pieces)
    size, width = pieces[0].shape

    def kernel(*refs):
        whole = refs[count]
        mine = lax.axis_index("ctx")
        for k in range(count):
            at = pl.multiple_of((mine ^ k) * size, size)
            whole[pl.ds(at, size), :] = refs[k][...]

    return call(kernel, "place", pieces, [shape((count * size, width))])[0]


def write_pieces(outs, value, micros, start=0, width=None):
    heads = len(outs)
    piece = outs[0].shape[1]
    for m in range(micros):
        for k in range(heads):
            at = (m * heads + k) * piece
            outs[k][m] = value[at : at + piece].astype(BF16)


def read_pieces(whole, pieces, micros):
    heads = len(pieces)
    piece = pieces[0].shape[1]
    for m in range(micros):
        for k in range(heads):
            at = (m * heads + k) * piece
            whole[at : at + piece, :] = pieces[k][m]


def project(pieces, queries, kvs, gain_views, cosine, sine, turn):
    heads = len(pieces)
    micros, piece, d_model = pieces[0].shape
    rows = micros * heads * piece
    half = d_model // 2
    width = queries[0].width

    def kernel(*refs):
        xs = refs[:heads]
        q_own, q_other, kv_own, kv_other, g_own, g_other, cos, sin, turns, eye = refs[heads : heads + 10]
        na, q_out, kv_out, gains = refs[heads + 10 :]
        gains[:, :half] = dot_nt(eye[...], g_own[...])
        gains[:, half:] = dot_nt(eye[...], g_other[...])
        gain = gains[0:1, :]
        for m in range(micros):
            for k in range(heads):
                x = xs[k][m].astype(F32)
                scale = lax.rsqrt(jnp.mean(x * x, axis=-1, keepdims=True) + EPSILON)
                at = (m * heads + k) * piece
                na[at : at + piece, :] = (x * scale * gain).astype(BF16)
        low, high = na[:, :half], na[:, half:]
        for part, (own, other, out) in enumerate(
            ((q_own, q_other, q_out), (kv_own, kv_other, kv_out))
        ):
            lin = dot(low, own[...]) + dot(high, other[...])
            a, b = split_terms(lin)
            turned = dot(a, turns[part]) + dot(b, turns[part])
            at = part * width
            out[...] = (
                lin * cos[:, at : at + width] + turned * sin[:, at : at + width]
            ).astype(BF16)

    eye = jnp.asarray(np.eye(8, LANES), BF16)
    return call(
        kernel,
        "project",
        [*pieces, *queries, *kvs, *gain_views, cosine, sine, turn, eye],
        [kept((rows, d_model)), kept((rows, width)), shape((rows, width)), shape((8, d_model), F32)],
        flops=4 * rows * d_model * width,
    )


def attend(query, pieces, place_q, place_k, pad, outs_w, heads, piece, group):
    ctxs = len(pieces)
    micros, span, width = pieces[0].shape
    keys = ctxs * span
    rows = micros * span
    half = outs_w[0].array.shape[0]
    kv_heads = pad.shape[1] // LANES // 2

    def kernel(*refs):
        q_ref = refs[0]
        kvs = refs[1 : 1 + ctxs]
        pq, pk, pads, w_own, w_other = refs[1 + ctxs : 6 + ctxs]
        prob, mix = refs[6 + ctxs : 8 + ctxs]
        outs = refs[8 + ctxs : 8 + ctxs + heads]
        kv_rows, mixed = refs[8 + ctxs + heads :]
        for m in range(micros):
            for j in range(ctxs):
                kv_rows[j * span : (j + 1) * span, :] = kvs[j][m]
            kv = dot(kv_rows[...], pads[...]).astype(BF16)
            q = dot(q_ref[m * span : (m + 1) * span, :], pads[...]).astype(BF16)
            allowed = pk[m] <= pq[m]
            allowed = jnp.concatenate([allowed] * group, axis=0)
            for a in range(kv_heads):
                q2 = jnp.concatenate(
                    [q[:, (a * group + g) * LANES : (a * group + g + 1) * LANES] for g in range(group)],
                    axis=0,
                )
                key = kv[:, a * LANES : (a + 1) * LANES]
                value = kv[:, (kv_heads + a) * LANES : (kv_heads + a + 1) * LANES]
                scores = jnp.where(allowed, dot_nt(q2, key) * INV_ROOT, MASKED)
                top = jnp.max(scores, axis=-1, keepdims=True)
                weight = jnp.exp(scores - top)
                share = (weight / jnp.sum(weight, axis=-1, keepdims=True)).astype(BF16)
                prob[m * kv_heads + a] = share
                got = dot(share, value).astype(BF16)
                for g in range(group):
                    at = (a * group + g) * LANES
                    mixed[:, at : at + LANES] = got[g * span : (g + 1) * span]
            mix[m * span : (m + 1) * span, :] = dot_nt(mixed[...], pads[...]).astype(BF16)
        for t, w in enumerate((w_own, w_other)):
            branch = dot_nt(mix[...], w[...]).astype(BF16)
            for m in range(micros):
                for k in range(heads):
                    at = (m * heads + k) * piece
                    outs[k][m, :, t * half : (t + 1) * half] = branch[at : at + piece]

    return call(
        kernel,
        "attend",
        [query, *pieces, place_q, place_k, pad, *outs_w],
        [
            kept((micros * kv_heads, group * span, keys)),
            kept((rows, width)),
            *[shape((micros, piece, 2 * half)) for _ in range(heads)],
        ],
        [pltpu.VMEM((keys, width), BF16), pltpu.VMEM((span, pad.shape[1]), BF16)],
        flops=4 * rows * width * (keys + half),
    )


def add_mid(x, terms, gains):
    def kernel(*refs):
        x_ref, gain = refs[0], refs[1]
        parts = refs[2 : 2 + len(terms)]
        mid, nb = refs[2 + len(terms) :]
        total = x_ref[...].astype(F32)
        for part in parts:
            total = total + part[...].astype(F32)
        mid[...] = total
        scale = lax.rsqrt(jnp.mean(total * total, axis=-1, keepdims=True) + EPSILON)
        nb[...] = (total * scale * gain[1:2, :]).astype(BF16)

    return call(
        kernel,
        "add_mid",
        [x, gains, *terms],
        [shape(x.shape, F32), shape(x.shape)],
        limit=VMEM_SMALL,
    )


def add_out(mid, terms):
    def kernel(*refs):
        total = refs[0][...]
        for part in refs[1:-1]:
            total = total + part[...].astype(F32)
        refs[-1][...] = total.astype(BF16)

    return call(kernel, "add_out", [mid, *terms], [shape(mid.shape)], limit=VMEM_SMALL)[0]


def blocks_of(pair, units):
    specs, arrays = [], []
    count = units // UNIT_BLOCK
    for part in range(3):
        for array in pair:
            specs.append(
                pl.BlockSpec(
                    (array.shape[0], UNIT_BLOCK), lambda j, part=part: (0, part * count + j)
                )
            )
            arrays.append(array)
    return specs, arrays


def pack_places(half, units, width):
    hidden_at = -(-2 * half // UNIT_BLOCK) * UNIT_BLOCK
    mix_at = -(-(hidden_at + units) // width) * width
    return hidden_at, mix_at


def feed(pieces, pair, units, na, mix):
    heads = len(pieces)
    micros, piece, d_model = pieces[0].shape
    rows = micros * heads * piece
    half = d_model // 2
    count = units // UNIT_BLOCK
    width = mix.shape[1]
    hidden_at, mix_at = pack_places(half, units, width)

    def kernel(*refs):
        xs = refs[:heads]
        gate_w = refs[heads : heads + 2]
        up_w = refs[heads + 2 : heads + 4]
        down_w = refs[heads + 4 : heads + 6]
        na_in, mix_in = refs[heads + 6 : heads + 8]
        gate_out, up_out, hidden_out, nb, packed = refs[heads + 8 : heads + 13]
        outs = refs[heads + 13 : 2 * heads + 13]
        total = refs[-1]
        j = pl.program_id(0)

        @pl.when(j == 0)
        def _():
            read_pieces(nb, xs, micros)
            total[...] = jnp.zeros_like(total)
            packed[:, :half] = na_in[...]
            packed[:, half : 2 * half] = nb[:, half:]
            packed[:, mix_at : mix_at + width] = mix_in[...]

        low, high = nb[:, :half], nb[:, half:]
        gate = dot(low, gate_w[0][...]) + dot(high, gate_w[1][...])
        up = dot(low, up_w[0][...]) + dot(high, up_w[1][...])
        gate_out[...] = gate.astype(BF16)
        up_out[...] = up.astype(BF16)
        hidden = (gate * jax.nn.sigmoid(gate) * up).astype(BF16)
        hidden_out[...] = hidden
        at = pl.multiple_of(hidden_at + j * UNIT_BLOCK, UNIT_BLOCK)
        packed[:, pl.ds(at, UNIT_BLOCK)] = hidden
        total[:, :half] += dot_nt(hidden, down_w[0][...])
        total[:, half:] += dot_nt(hidden, down_w[1][...])

        @pl.when(j == count - 1)
        def _():
            write_pieces(outs, total, micros)

    specs, arrays = blocks_of(pair, units)
    whole = pl.BlockSpec((rows, d_model), lambda j: (0, 0))
    block = pl.BlockSpec((rows, UNIT_BLOCK), lambda j: (0, j))
    rows_spec = pl.BlockSpec((micros, piece, d_model), lambda j: (0, 0, 0))
    return pl.pallas_call(
        kernel,
        grid=(count,),
        in_specs=[rows_spec] * heads
        + specs
        + [pl.BlockSpec((rows, half), lambda j: (0, 1)), pl.BlockSpec(mix.shape, lambda j: (0, 0))],
        out_specs=[block, block, block, whole]
        + [pl.BlockSpec((rows, mix_at + width), lambda j: (0, 0))]
        + [rows_spec] * heads,
        out_shape=[
            kept((rows, units)),
            kept((rows, units)),
            kept((rows, units)),
            kept((rows, d_model)),
            kept((rows, mix_at + width)),
            *[shape((micros, piece, d_model)) for _ in range(heads)],
        ],
        scratch_shapes=[pltpu.VMEM((rows, d_model), F32)],
        compiler_params=pltpu.CompilerParams(vmem_limit_bytes=VMEM_LARGE),
        cost_estimate=pl.CostEstimate(
            flops=6 * rows * d_model * units, bytes_accessed=6 * d_model * units, transcendentals=0
        ),
        name="feed",
    )(*pieces, *arrays, na, mix)


def feed_back(pieces, pair, gate, up):
    heads = len(pieces)
    micros, piece, d_model = pieces[0].shape
    rows, units = gate.shape
    half = d_model // 2
    count = units // UNIT_BLOCK
    back_at = -(-half // UNIT_BLOCK) * UNIT_BLOCK

    def kernel(*refs):
        xs = refs[:heads]
        gate_w = refs[heads : heads + 2]
        up_w = refs[heads + 2 : heads + 4]
        down_w = refs[heads + 4 : heads + 6]
        gate_in, up_in = refs[heads + 6 : heads + 8]
        d_gate_out, d_up_out, gf, packed = refs[heads + 8 : heads + 12]
        outs = refs[heads + 12 : 2 * heads + 12]
        total = refs[-1]
        j = pl.program_id(0)

        @pl.when(j == 0)
        def _():
            read_pieces(gf, xs, micros)
            total[...] = jnp.zeros_like(total)
            packed[:, :half] = gf[:, half:]

        d_hidden = dot(gf[:, :half], down_w[0][...]) + dot(gf[:, half:], down_w[1][...])
        gate_v, up_v = gate_in[...].astype(F32), up_in[...].astype(F32)
        sigma = jax.nn.sigmoid(gate_v)
        d_gate = (d_hidden * up_v * sigma * (1.0 + gate_v * (1.0 - sigma))).astype(BF16)
        d_up = (d_hidden * gate_v * sigma).astype(BF16)
        d_gate_out[...] = d_gate
        d_up_out[...] = d_up
        at = pl.multiple_of(back_at + j * UNIT_BLOCK, UNIT_BLOCK)
        packed[:, pl.ds(at, UNIT_BLOCK)] = d_gate
        at = pl.multiple_of(back_at + units + j * UNIT_BLOCK, UNIT_BLOCK)
        packed[:, pl.ds(at, UNIT_BLOCK)] = d_up
        total[:, :half] += dot_nt(d_gate, gate_w[0][...]) + dot_nt(d_up, up_w[0][...])
        total[:, half:] += dot_nt(d_gate, gate_w[1][...]) + dot_nt(d_up, up_w[1][...])

        @pl.when(j == count - 1)
        def _():
            write_pieces(outs, total, micros)

    specs, arrays = blocks_of(pair, units)
    whole = pl.BlockSpec((rows, d_model), lambda j: (0, 0))
    block = pl.BlockSpec((rows, UNIT_BLOCK), lambda j: (0, j))
    rows_spec = pl.BlockSpec((micros, piece, d_model), lambda j: (0, 0, 0))
    return pl.pallas_call(
        kernel,
        grid=(count,),
        in_specs=[rows_spec] * heads + specs + [block, block],
        out_specs=[block, block, whole]
        + [pl.BlockSpec((rows, back_at + 2 * units), lambda j: (0, 0))]
        + [rows_spec] * heads,
        out_shape=[
            kept((rows, units)),
            kept((rows, units)),
            kept((rows, d_model)),
            kept((rows, back_at + 2 * units)),
            *[shape((micros, piece, d_model)) for _ in range(heads)],
        ],
        scratch_shapes=[pltpu.VMEM((rows, d_model), F32)],
        compiler_params=pltpu.CompilerParams(vmem_limit_bytes=VMEM_LARGE),
        cost_estimate=pl.CostEstimate(
            flops=6 * rows * d_model * units, bytes_accessed=6 * d_model * units, transcendentals=0
        ),
        name="feed_back",
    )(*pieces, *arrays, gate, up)


def norm_back(terms, residual, gains, row, carried):
    d_model = residual.shape[-1]

    def kernel(*refs):
        res, gain, carry = refs[:3]
        parts = refs[3 : 3 + len(terms)]
        d_out, d_low, d_gain = refs[3 + len(terms) :]
        d_normed = parts[0][...].astype(F32)
        for part in parts[1:]:
            d_normed = d_normed + part[...].astype(F32)
        rows = res[...].astype(F32)
        scale = lax.rsqrt(jnp.mean(rows * rows, axis=-1, keepdims=True) + EPSILON)
        unit = rows * scale
        d_gain[...] = jnp.sum(jnp.sum(d_normed * unit, axis=0), axis=0, keepdims=True)
        d_unit = d_normed * gain[row : row + 1, :]
        total = carry[...].astype(F32) + scale * (
            d_unit - unit * jnp.mean(d_unit * unit, axis=-1, keepdims=True)
        )
        d_out[...] = total
        d_low[...] = total.astype(BF16)

    return call(
        kernel,
        "norm_back",
        [residual, gains, carried, *terms],
        [shape(residual.shape, F32), shape(residual.shape), shape((1, d_model), F32)],
        limit=VMEM_SMALL,
    )


def attend_back(pieces, outs_w, mix, prob, query, kv_pieces, pad, turn, cosine, sine, group):
    heads = len(pieces)
    micros, piece, d_model = pieces[0].shape
    span = heads * piece
    rows = micros * span
    half = d_model // 2
    ctxs = len(kv_pieces)
    width = query.shape[1]
    keys = ctxs * span
    kv_heads = pad.shape[1] // LANES // 2

    def kernel(*refs):
        xs = refs[:heads]
        w_own, w_other, mix_in, prob_in, q_ref = refs[heads : heads + 5]
        kvs = refs[heads + 5 : heads + 5 + ctxs]
        pads, turns, cos, sin = refs[heads + 5 + ctxs : heads + 9 + ctxs]
        ga, ga_other, dq_out = refs[heads + 9 + ctxs : heads + 12 + ctxs]
        outs = refs[heads + 12 + ctxs : heads + 12 + 2 * ctxs]
        kv_rows, d_kv, d_q = refs[heads + 12 + 2 * ctxs :]
        read_pieces(ga, xs, micros)
        ga_other[...] = ga[:, half:]
        d_mix = (dot(ga[:, :half], w_own[...]) + dot(ga[:, half:], w_other[...])).astype(BF16)
        for m in range(micros):
            for j in range(ctxs):
                kv_rows[j * span : (j + 1) * span, :] = kvs[j][m]
            here = slice(m * span, (m + 1) * span)
            kv = dot(kv_rows[...], pads[...]).astype(BF16)
            q = dot(q_ref[here, :], pads[...]).astype(BF16)
            d = dot(d_mix[here], pads[...])
            product = d * dot(mix_in[here, :], pads[...])
            d = d.astype(BF16)
            for a in range(kv_heads):
                cuts = [slice((a * group + g) * LANES, (a * group + g + 1) * LANES) for g in range(group)]
                q2 = jnp.concatenate([q[:, cut] for cut in cuts], axis=0)
                d2 = jnp.concatenate([d[:, cut] for cut in cuts], axis=0)
                delta = jnp.concatenate(
                    [jnp.sum(product[:, cut], axis=-1, keepdims=True) for cut in cuts], axis=0
                )
                key = kv[:, a * LANES : (a + 1) * LANES]
                value = kv[:, (kv_heads + a) * LANES : (kv_heads + a + 1) * LANES]
                share = prob_in[m * kv_heads + a]
                d_prob = dot_nt(d2, value)
                d_score = (share.astype(F32) * (d_prob - delta)).astype(BF16)
                back = dot(d_score, key)
                for g, cut in enumerate(cuts):
                    d_q[:, cut] = back[g * span : (g + 1) * span]
                d_kv[:, a * LANES : (a + 1) * LANES] = dot_tn(d_score, q2).astype(BF16)
                d_kv[:, (kv_heads + a) * LANES : (kv_heads + a + 1) * LANES] = dot_tn(
                    share, d2
                ).astype(BF16)
            packed = dot_nt(d_kv[...], pads[...]).astype(BF16)
            for j in range(ctxs):
                outs[j][m] = packed[j * span : (j + 1) * span]
            high, low = split_terms(d_q[...])
            line = (dot_nt(high, pads[...]) + dot_nt(low, pads[...])) * INV_ROOT
            high, low = split_terms(line)
            turned = dot_nt(high, turns[0]) + dot_nt(low, turns[0])
            dq_out[here, :] = (line * cos[here, :width] + turned * sin[here, :width]).astype(BF16)

    return call(
        kernel,
        "attend_back",
        [*pieces, *outs_w, mix, prob, query, *kv_pieces, pad, turn, cosine, sine],
        [
            kept((rows, d_model)),
            shape((rows, half)),
            shape((rows, width)),
            *[shape((micros, span, width)) for _ in range(ctxs)],
        ],
        [
            pltpu.VMEM((keys, width), BF16),
            pltpu.VMEM((keys, pad.shape[1]), BF16),
            pltpu.VMEM((span, pad.shape[1]), F32),
        ],
        flops=10 * rows * width * keys,
    )


def project_back(terms, dq, queries, kvs, turn, cosine, sine, row_pieces):
    heads = len(row_pieces)
    micros, span, width = terms[0].shape
    rows = micros * span
    piece = span // heads
    half = queries[0].array.shape[0]
    count = len(terms)

    def kernel(*refs):
        parts = refs[:count]
        dq_in, q_own, q_other, kv_own, kv_other, turns, cos, sin = refs[count : count + 8]
        xs = refs[count + 8 : count + 8 + heads]
        d_line, d_gain = refs[count + 8 + heads : count + 10 + heads]
        outs = refs[count + 10 + heads : count + 10 + 2 * heads]
        unit = refs[-1]
        for m in range(micros):
            for k in range(heads):
                x = xs[k][m].astype(F32)
                scale = lax.rsqrt(jnp.mean(x * x, axis=-1, keepdims=True) + EPSILON)
                at = (m * heads + k) * piece
                unit[at : at + piece, :] = x * scale
        d_line[:, :width] = dq_in[...]
        lanes = lax.broadcasted_iota(jnp.int32, (span, width), 1)
        scaled = jnp.where(lanes < width // 2, INV_ROOT, 1.0)
        for m in range(micros):
            here = slice(m * span, (m + 1) * span)
            total = parts[0][m].astype(F32)
            for part in parts[1:]:
                total = total + part[m].astype(F32)
            total = total * scaled
            high, low = split_terms(total)
            turned = dot_nt(high, turns[1]) + dot_nt(low, turns[1])
            d_line[here, width:] = (
                total * cos[here, width:] + turned * sin[here, width:]
            ).astype(BF16)
        for t, (wq, wkv) in enumerate(((q_own, kv_own), (q_other, kv_other))):
            branch = dot_nt(d_line[:, :width], wq[...]) + dot_nt(d_line[:, width:], wkv[...])
            side = slice(t * half, (t + 1) * half)
            d_gain[:, side] = jnp.sum(branch * unit[:, side], axis=0, keepdims=True)
            branch = branch.astype(BF16)
            for m in range(micros):
                for k in range(heads):
                    at = (m * heads + k) * piece
                    outs[k][m, :, t * half : (t + 1) * half] = branch[at : at + piece]

    return call(
        kernel,
        "project_back",
        [*terms, dq, *queries, *kvs, turn, cosine, sine, *row_pieces],
        [
            kept((rows, 2 * width)),
            shape((1, 2 * half), F32),
            *[shape((micros, piece, 2 * half)) for _ in range(heads)],
        ],
        [pltpu.VMEM((rows, 2 * half), F32)],
        flops=8 * rows * half * width,
    )


def weight_grad(groups):
    half = groups[0][0][0].width
    total = sum(group[0][1].width for group in groups)
    args = [view for group in groups for pair in group for view in pair]

    def kernel(*refs):
        out = refs[-1]
        at = 0
        for g, group in enumerate(groups):
            n = group[0][1].width
            a, b, c, d = refs[4 * g : 4 * g + 4]
            out[:, at : at + n] = (dot_tn(a[...], b[...]) + dot_tn(c[...], d[...])).astype(BF16)
            at += n

    rows = groups[0][0][0].array.shape[0]
    return call(
        kernel, "weight_grad", args, [shape((half, total))], flops=4 * half * rows * total
    )[0]


def late_grad(nb, gf, d_gate, d_up, hidden, packed, packed_back):
    rows, d_model = nb.shape
    units = hidden.shape[1]
    half = d_model // 2
    count = units // UNIT_BLOCK
    hidden_at, _ = pack_places(half, units, LANES)
    back_at = -(-half // UNIT_BLOCK) * UNIT_BLOCK

    def kernel(*refs):
        sides = refs[:4]
        lines = refs[4:10]
        out = refs[10]
        turned, line = refs[11:13], refs[13]
        j = pl.program_id(0)

        @pl.when(j == 0)
        def _():
            for k, side in enumerate(sides):
                turned[k % 2][:, k // 2 * rows : (k // 2 + 1) * rows] = side[...].T

        for part in range(3):

            @pl.when(j // count == part)
            def _(part=part):
                line[:rows, :] = lines[part][...]
                line[rows:, :] = lines[3 + part][...]
                out[...] = dot(turned[(0, 0, 1)[part]][...], line[...]).astype(BF16)

    def side(block):
        return pl.BlockSpec((rows, half), lambda j: (0, block))

    def line(part, first):
        return pl.BlockSpec(
            (rows, UNIT_BLOCK),
            lambda j: (0, first // UNIT_BLOCK + jnp.clip(j - part * count, 0, count - 1)),
        )

    return pl.pallas_call(
        kernel,
        grid=(3 * count,),
        in_specs=[side(0), side(0), side(1), side(0)]
        + [line(part, 0) for part in range(3)]
        + [line(0, back_at), line(1, back_at + units), line(2, hidden_at)],
        out_specs=pl.BlockSpec((half, UNIT_BLOCK), lambda j: (0, j)),
        out_shape=kept((half, 3 * units)),
        scratch_shapes=[pltpu.VMEM((half, 2 * rows), BF16)] * 2
        + [pltpu.VMEM((2 * rows, UNIT_BLOCK), BF16)],
        compiler_params=pltpu.CompilerParams(vmem_limit_bytes=VMEM_LARGE),
        cost_estimate=pl.CostEstimate(
            flops=12 * half * rows * units, bytes_accessed=6 * half * units, transcendentals=0
        ),
        name="late_grad",
    )(nb, gf, packed, packed_back, d_gate, d_up, hidden, packed_back, packed_back, packed)


def finish_late(lower, upper, units):
    size, _ = lower[0].shape
    count = units // UNIT_BLOCK

    def kernel(*refs):
        parts, outs = refs[:12], refs[12:]
        first = lax.axis_index("section") == 0
        for which in range(3):
            a0, a1, b0, b1 = (parts[4 * which + k][...].astype(F32) for k in range(4))
            top, low = jnp.where(first, a0, b0), jnp.where(first, a1, b1)
            if which < 2:
                outs[which][:size, :] = top
                outs[which][size:, :] = low
            else:
                outs[2][:, :size] = top.T
                outs[2][:, size:] = low.T

    specs, arrays = [], []
    for which in range(3):
        for array in (*lower, *upper):
            specs.append(
                pl.BlockSpec((size, UNIT_BLOCK), lambda j, which=which: (0, which * count + j))
            )
            arrays.append(array)
    flat = pl.BlockSpec((2 * size, UNIT_BLOCK), lambda j: (0, j))
    return pl.pallas_call(
        kernel,
        grid=(count,),
        in_specs=specs,
        out_specs=[flat, flat, pl.BlockSpec((UNIT_BLOCK, 2 * size), lambda j: (j, 0))],
        out_shape=[
            kept((2 * size, units), F32),
            kept((2 * size, units), F32),
            kept((units, 2 * size), F32),
        ],
        compiler_params=pltpu.CompilerParams(vmem_limit_bytes=VMEM_LARGE),
        cost_estimate=pl.CostEstimate(
            flops=0, bytes_accessed=48 * size * units, transcendentals=0
        ),
        name="finish_late",
    )(*arrays)


def finish_early(lower, lower_out, upper, k_width):
    size, lines = lower[0].shape
    width = lower_out[0].shape[1]

    def kernel(*refs):
        e0, e1, o0, o1, b0, b1, query, key, value, out = refs
        first = lax.axis_index("section") == 0
        for t, (e, o, b) in enumerate(((e0, o0, b0), (e1, o1, b1))):
            rows = slice(t * size, (t + 1) * size)
            both = b[...].astype(F32)
            line = jnp.where(first, e[...].astype(F32), both[:, width:])
            query[rows, :] = line[:, :width]
            key[:, rows] = line[:, width : width + k_width].T
            value[:, rows] = line[:, width + k_width :].T
            out[:, rows] = jnp.where(first, o[...].astype(F32), both[:, :width]).T

    return call(
        kernel,
        "finish_early",
        [*lower, *lower_out, *upper],
        [
            kept((2 * size, width), F32),
            kept((k_width, 2 * size), F32),
            kept((k_width, 2 * size), F32),
            kept((width, 2 * size), F32),
        ],
    )


def relative_columns(value, section, ctxs):
    width = value.shape[-1] // (2 * ctxs)
    return jnp.concatenate(
        [
            lax.dynamic_slice_in_dim(
                value, (k * 2 + (section ^ t)) * width, width, axis=value.ndim - 1
            )
            for t in range(2)
            for k in range(ctxs)
        ],
        axis=-1,
    )


def stored_columns(value, section, ctxs):
    width = value.shape[-1] // (2 * ctxs)
    return jnp.concatenate(
        [
            lax.dynamic_slice_in_dim(
                value, ((section ^ t) * ctxs + k) * width, width, axis=value.ndim - 1
            )
            for k in range(ctxs)
            for t in range(2)
        ],
        axis=-1,
    )


def send_all(pieces, axis):
    return [pieces[0]] + [swap(piece, axis, k) for k, piece in enumerate(pieces[1:], 1)]


def send_rows(rows):
    return send_all([rows] * lax.axis_size("head"), "head")


def send_blocks(rows):
    return send_all([rows] * lax.axis_size("ctx"), "ctx")


class Fetch:
    def __init__(self, shard):
        self.shard = shard

    def send(self, gate=None):
        self.pieces = send_blocks(self.shard if gate is None else after(self.shard, gate))

    def settle(self, gate=None):
        own = place(after(self.pieces, gate), lax.axis_index("ctx"))
        self.pair = (own, swap(own, "section", 1))
        return self.pair

    def direct(self, gate=None, with_rows=None):
        shard = self.shard if gate is None else after(self.shard, gate)
        pieces = send_blocks(shard)
        if with_rows is not None:
            pieces = after(pieces, with_rows)
        own = place(pieces, lax.axis_index("ctx"))
        self.pair = (own, swap(own, "section", 1))
        return pieces[1:]

    def first(self, gate=None):
        shard = self.shard if gate is None else after(self.shard, gate)
        self.own = lax.all_gather(shard, "ctx", axis=0, tiled=True)
        return self.own

    def second(self, gate=None):
        own = self.own if gate is None else after(self.own, gate)
        self.pair = (own, swap(own, "section", 1))
        return self.pair[1]


class Settle:
    def __init__(self, source):
        self.source = source

    def first(self, whole):
        self.kept = lax.psum_scatter(whole, "ctx", scatter_dimension=0, tiled=True)
        return whole

    def direct(self, whole, gate=None):
        if gate is not None:
            whole = after(whole, gate)
        ctxs = lax.axis_size("ctx")
        ctx = lax.axis_index("ctx")
        size = whole.shape[0] // ctxs
        parts = [
            lax.dynamic_slice_in_dim(whole, (ctx ^ k) * size, size, axis=0) for k in range(ctxs)
        ]
        total = None
        for term in send_all(parts, "ctx"):
            term = term.astype(F32)
            total = term if total is None else total + term
        self.kept = total.astype(BF16)
        return whole

    def second(self, gate=None):
        kept = self.kept if gate is None else after(self.kept, gate)
        self.kept = kept
        sent = swap_from(kept, self.source)
        self.halves = (kept, sent) if self.source == 1 else (sent, kept)
        return sent


class Chain:
    def __init__(self):
        self.tasks = {}
        self.due = {}

    def plan(self, start, end, task):
        self.tasks.setdefault(start, []).append((end, task))

    def enter(self, name, value):
        done = self.due.pop(name, [])
        return after(value, done) if done else value

    def leave(self, name, value):
        for end, task in self.tasks.pop(name, []):
            result = task(value)
            if end is not None:
                self.due.setdefault(end, []).append(result)


class Plan:
    pass


def pick(first, a, b):
    return jnp.where(first, a, b)


def turning(heads_turned, heads):
    turn = np.zeros((heads * HEAD_DIM, heads * HEAD_DIM), np.float32)
    for h in range(heads_turned):
        for i in range(HALF):
            turn[h * HEAD_DIM + HALF + i, h * HEAD_DIM + i] = -1.0
            turn[h * HEAD_DIM + i, h * HEAD_DIM + HALF + i] = 1.0
    return turn


def padding(heads):
    pad = np.zeros((heads * HEAD_DIM, heads * LANES), np.float32)
    for h in range(heads):
        for i in range(HEAD_DIM):
            pad[h * HEAD_DIM + i, h * LANES + i] = 1.0
    return pad


def local(
    layer_input,
    out_cotangent,
    block_order,
    gain_attn,
    w_query,
    w_key,
    w_value,
    w_out,
    gain_ffn,
    w_gate,
    w_up,
    w_down,
):
    section = lax.axis_index("section")
    head = lax.axis_index("head")
    ctx = lax.axis_index("ctx")
    heads = lax.axis_size("head")
    ctxs = lax.axis_size("ctx")
    first = section == 0
    micros_all = layer_input.shape[0] // 2
    micros = micros_all // GROUPS
    rows_dev = layer_input.shape[1]
    d_model = layer_input.shape[2]
    span = heads * rows_dev
    rows = micros * span
    block_rows = ctxs * span // block_order.shape[1]
    d_half = d_model // ctxs // 2
    width = w_query.shape[2]
    k_width = w_key.shape[2]
    units = w_gate.shape[2]
    group_size = width // k_width
    line_heads = width // HEAD_DIM
    chain = Chain()

    turn = jnp.asarray(
        np.stack([turning(line_heads, line_heads), turning(k_width // HEAD_DIM, line_heads)]), BF16
    )
    pad = jnp.asarray(padding(line_heads), BF16)

    def places_of(order, ctx_index):
        piece = jnp.arange(span, dtype=jnp.int32)
        stored = (ctx_index * heads + (head ^ (piece // rows_dev))) * rows_dev + piece % rows_dev
        block = stored // block_rows
        match = block[:, None] == jnp.arange(order.shape[1], dtype=jnp.int32)[None, :]
        base = jnp.sum(jnp.where(match[None], order[:, None, :], 0), axis=2)
        return base * block_rows + (stored % block_rows)[None]

    frequency = jnp.power(ROPE_BASE, jnp.arange(HALF, dtype=F32) * (-2.0 / HEAD_DIM))

    def group_of(index):
        group = Plan()
        at = section * micros_all + index * micros
        group.name = "ab"[index]
        order = lax.dynamic_slice_in_dim(block_order, at, micros, axis=0)
        places_q = places_of(order, ctx)
        places_k = jnp.concatenate([places_of(order, ctx ^ k) for k in range(ctxs)], axis=1)
        group.place_q = places_q[:, :, None]
        group.place_k = places_k[:, None, :]
        group.places = places_q

        def make_tables(places):
            angles = places.reshape(rows, 1).astype(F32) * frequency
            cosine, sine = jnp.cos(angles), jnp.sin(angles)
            turned = 2 * (line_heads + k_width // HEAD_DIM)
            fixed = width - k_width
            group.cosine = jnp.concatenate(
                [cosine] * turned + [jnp.ones((rows, fixed), F32)], axis=1
            )
            group.sine = jnp.concatenate(
                [sine] * turned + [jnp.zeros((rows, fixed), F32)], axis=1
            )

        group.make_tables = make_tables

        def mine(value):
            part = lax.dynamic_slice_in_dim(value, at, micros, axis=0)
            return relative_columns(part, section, ctxs)

        group.x = mine(layer_input)
        group.cot = mine(out_cotangent)
        group.keep, group.d_in = {}, {}
        return group

    members = [group_of(index) for index in range(GROUPS)]
    tail = members[-1].name
    for group in members:
        group.firsts = send_rows(group.x)
        group.cot_pieces = [group.cot] * heads

    def exchange(shard, gate=None):
        def cut(which):
            return lax.dynamic_slice_in_dim(shard, which * d_half, d_half, axis=0)

        kept, given = cut(section), cut(1 - section)
        if gate is not None:
            given = after(given, gate)
        taken = swap(given, "section", 1)
        return pick(first, kept, taken), pick(first, taken, kept)

    gains = jnp.stack([gain_attn[0], gain_ffn[0]], axis=1)
    gains = jnp.pad(gains, ((0, 0), (0, LANES - 2)))
    early_shards = exchange(
        jnp.concatenate([w_query[0], w_key[0], w_value[0], gains], axis=1)
    )
    early0 = Fetch(early_shards[0])
    early0.send([group.firsts[1] for group in members])
    tables = after([group.places for group in members], early0.pieces[1])
    for group, places in zip(members, tables):
        group.make_tables(places)
    early0.settle([(group.cosine, group.sine, group.firsts) for group in members])
    landed = early0.pair[:1]
    w_late, w_o = after(((w_gate[0], w_up[0], w_down[0]), w_out[0]), landed)
    out_shards = exchange(w_o.T)
    late_shards = exchange(jnp.concatenate([w_late[0], w_late[1], w_late[2].T], axis=1))
    late0, late1 = Fetch(late_shards[0]), Fetch(late_shards[1])
    out0 = Fetch(out_shards[0])
    both1 = Fetch(jnp.concatenate([out_shards[1], early_shards[1]], axis=1))
    late0.first(landed)
    out0.send(landed)

    def views0(name):
        if name == "o":
            return [View(part, width, 0) for part in out0.pair]
        at = {"q": (width, 0), "kv": (width, 1), "g": (LANES, 2 * width // LANES)}[name]
        return [View(part, *at) for part in early0.pair]

    def views1(name):
        at = {
            "o": (width, 0),
            "q": (width, 1),
            "kv": (width, 2),
            "g": (LANES, 3 * width // LANES),
        }[name]
        return [View(part, *at) for part in both1.pair]

    token = [None]

    def enter(name, group, value):
        if token[0] is not None and GROUPS > 1:
            value = after(value, token[0])
        return chain.enter(name + group.name, value)

    def leave(name, group, value):
        token[0] = value
        chain.leave(name + group.name, value)

    def forward(label, group, layer_in, views, late_fetch):
        keep = Plan()
        keep.x = layer_in
        pieces = group.firsts if label == "0" else send_rows(layer_in)
        leave(label + "F0", group, layer_in)
        yield
        pieces = enter(label + "F1", group, pieces)
        keep.x_pieces = pieces
        keep.na, keep.query, kv, keep.gains = project(
            pieces, views("q"), views("kv"), views("g"), group.cosine, group.sine, turn
        )
        kv = kv.reshape(micros, span, width)
        pieces = send_blocks(kv)
        leave(label + "F1", group, kv)
        yield
        keep.kv = enter(label + "F2", group, pieces)
        keep.prob, keep.mix, *parts = attend(
            keep.query, keep.kv, group.place_q, group.place_k, pad, views("o"),
            heads, rows_dev, group_size,
        )
        terms = send_all(parts, "head")
        leave(label + "F2", group, parts[0])
        yield
        terms = enter(label + "F3", group, terms)
        keep.mid, own_nb = add_mid(layer_in, terms, keep.gains)
        pieces = send_rows(own_nb)
        leave(label + "F3", group, own_nb)
        yield
        pieces = enter(label + "F4", group, pieces)
        keep.late = late_fetch.pair
        keep.gate, keep.up, keep.hidden, keep.nb, packed, *parts = feed(
            pieces, keep.late, units, keep.na, keep.mix
        )
        keep.packed = swap(packed, "section", 1)
        group.parts = parts
        group.keep[label] = keep
        leave(label + "F4", group, parts[0])
        if label == "0":
            terms = send_all(parts, "head")
            yield
            terms = enter(label + "F5", group, terms)
            group.out = add_out(keep.mid, terms)

    def backward(label, group, pieces, grad, views):
        keep = group.keep[label]
        if label == "0":
            pieces = enter(label + "B1", group, pieces)
        keep.d_gate, keep.d_up, keep.gf, packed, *parts = feed_back(
            pieces, keep.late, keep.gate, keep.up
        )
        keep.packed_back = swap(packed, "section", 1)
        terms = send_all(parts, "head")
        leave(label + "B1", group, parts[0])
        yield
        terms = enter(label + "B2", group, terms)
        d_mid, own_ga, keep.gain_b = norm_back(terms, keep.mid, keep.gains, 1, grad)
        pieces = send_rows(own_ga)
        leave(label + "B2", group, own_ga)
        yield
        pieces = enter(label + "B3", group, pieces)
        keep.ga, ga_other, dq, *parts = attend_back(
            pieces, views("o"), keep.mix, keep.prob, keep.query, keep.kv, pad, turn,
            group.cosine, group.sine, group_size,
        )
        terms = send_all(parts, "ctx")
        keep.ga_other = swap(ga_other, "section", 1)
        leave(label + "B3", group, parts[0])
        yield
        terms = enter(label + "B4", group, terms)
        keep.d_line, keep.gain_a, *parts = project_back(
            terms, dq, views("q"), views("kv"), turn, group.cosine, group.sine, keep.x_pieces
        )
        terms = send_all(parts, "head")
        keep.d_line_other = swap(keep.d_line, "section", 1)
        leave(label + "B4", group, parts[0])
        yield
        terms = enter(label + "B5", group, terms)
        d_input, d_low, _ = norm_back(terms, keep.x, keep.gains, 0, d_mid)
        if label == "1":
            group.d_in[label] = d_low
            group.pieces = send_rows(d_low)
        else:
            group.d_in[label] = d_input
        leave(label + "B5", group, group.d_in[label])
        yield

    def drive(*stages):
        waiting = list(stages)
        while waiting:
            waiting = [stage for stage in waiting if next(stage, stage) is not stage]

    def gather_cot(group, which):
        def task(gate):
            for k in which:
                if k < heads:
                    group.cot_pieces[k] = swap(after(group.cot, gate), "head", k)
            return group.cot_pieces[1:]

        return task

    for group in members:
        chain.plan("0F1" + group.name, "0F2" + group.name, gather_cot(group, [2, 1]))
        chain.plan("1F1" + group.name, "1F2" + group.name, gather_cot(group, range(3, heads)))

    def on_last(start, end, task):
        chain.plan(start + tail, end + tail if end else None, task)

    on_last("0F1", "0F2", out0.settle)
    on_last("0F3", None, late0.second)
    on_last("0F3", None, lambda gate: both1.first(late0.pair[0]))
    on_last("1F0", None, both1.second)
    on_last("1F0", None, lambda gate: late1.first(both1.pair[0]))
    on_last("1F3", None, late1.second)
    drive(*(forward("0", group, group.x, views0, late0) for group in members))

    def scatter_out(group, which):
        def task(gate):
            group.terms += [
                swap(after(group.parts[k], gate), "head", k) for k in which if k < heads
            ]
            return group.terms[1:]

        return task

    def finish_out(group):
        def task(gate):
            group.final = add_out(group.keep["1"].mid, group.terms)
            return group.final

        return task

    drive(*(forward("1", group, group.out, views1, late1) for group in members))
    for group in members:
        group.terms = [group.parts[0]]
        chain.plan("1B3" + group.name, "1B4" + group.name, scatter_out(group, [2, 1]))
        chain.plan("0B3" + group.name, "0B4" + group.name, scatter_out(group, range(3, heads)))
        chain.plan("0B5" + group.name, None, finish_out(group))

    _, mix_at = pack_places(d_model // 2, units, width)

    def rows_of(label, *names):
        def joined(name):
            parts = [getattr(group.keep[label], name) for group in members]
            return parts[0] if len(parts) == 1 else jnp.concatenate(parts, axis=0)

        return [joined(name) for name in names]

    def late_of(label, gate):
        names = ("nb", "gf", "d_gate", "d_up", "hidden", "packed", "packed_back")
        return late_grad(*after(rows_of(label, *names), gate))

    def out_group(ga, mix, ga_other, packed):
        return (
            (View(ga, d_model // 2, 0), View(mix)),
            (View(ga_other), View(packed, width, mix_at // width)),
        )

    def early_group(na, d_line, packed, d_line_other):
        return (
            (View(na, d_model // 2, 0), View(d_line)),
            (View(packed, d_model // 2, 0), View(d_line_other)),
        )

    out_names = ("ga", "mix", "ga_other", "packed")
    early_names = ("na", "d_line", "packed", "d_line_other")

    def out_of(label, gate):
        return weight_grad([out_group(*after(rows_of(label, *out_names), gate))])

    def early_of(label, gate):
        return weight_grad([early_group(*after(rows_of(label, *early_names), gate))])

    def both_of(label, gate):
        values = after(rows_of(label, *out_names, *early_names), gate)
        return weight_grad([out_group(*values[:4]), early_group(*values[4:])])

    late_1, both_1, late_0, out_0, early_0 = (Settle(s) for s in (0, 0, 1, 1, 1))
    on_last("1B2", "1B3", lambda gate: late_1.first(late_of("1", gate)))
    on_last("1B5", "0B1", late_1.second)
    on_last("1B5", "0B1", lambda gate: both_1.first(both_of("1", (gate, late_1.kept))))
    on_last("0B2", "0B3", both_1.second)
    on_last("0B2", "0B3", lambda gate: late_0.first(late_of("0", (gate, both_1.kept))))
    early_out = []

    def out_first(gate):
        early_out.append(out_of("0", gate))
        return early_out[0]

    on_last("0B3", "0B4", out_first)
    on_last("0B5", None, lambda gate: out_0.direct(early_out[0], gate))
    late_done = []

    def finish(gate):
        late_done.append(finish_late(late_0.halves, late_1.halves, units))
        return late_done[0]

    on_last("0B5", None, late_0.second)
    on_last("0B5", None, finish)
    last = []

    def last_grad(gate):
        last.append(early_of("0", gate))
        return last[0]

    on_last("0B5", None, last_grad)
    on_last("0B5", None, lambda gate: early_0.direct(last[0], gate))
    gain_mine = []

    def sum_gains(gate):
        def gain_of(label, name):
            total = getattr(members[0].keep[label], name)
            for group in members[1:]:
                total = total + getattr(group.keep[label], name)
            return total[0]

        gain_rows = jnp.stack(
            [gain_of(label, name) for label in "01" for name in ("gain_a", "gain_b")]
        )
        gain_rows = after(gain_rows, gate)
        half = d_model // 2
        got = swap(pick(first, gain_rows[2:], gain_rows[:2]), "section", 1)
        got = jnp.concatenate([got[:, half:], got[:, :half]], axis=1)
        blocks = (pick(first, gain_rows[:2], gain_rows[2:]) + got).reshape(4, ctxs, d_half)

        def sum_over(values):
            total = values[0]
            for value in values[1:]:
                total = total + value
            return total

        mine = [
            lax.dynamic_index_in_dim(blocks, ctx ^ k, 1, keepdims=False) for k in range(ctxs)
        ]
        part = sum_over(send_all(mine, "ctx"))
        part = sum_over(send_all([part] * heads, "head")).reshape(2, 2, d_half)
        part = pick(first, part, part[:, ::-1])
        gain_mine.append(part.reshape(2, 2 * d_half))
        return gain_mine[0]

    def by_layer(lower, upper):
        lower = stored_columns(lower, section, ctxs)
        upper = stored_columns(upper, section, ctxs)
        kept_rows = pick(first, lower, upper)
        got_rows = swap(pick(first, upper, lower).astype(BF16), "section", 1).astype(lower.dtype)
        return jnp.concatenate(
            [pick(first, kept_rows, got_rows), pick(first, got_rows, kept_rows)], axis=0
        )[None]

    def all_rows(name):
        parts = [name(group) for group in members]
        return parts[0] if len(parts) == 1 else jnp.concatenate(parts, axis=0)

    layer_outs = []

    def out_rows(gate):
        lower, upper = after((all_rows(lambda g: g.out), all_rows(lambda g: g.final)), gate)
        layer_outs.append(by_layer(lower, upper))
        return layer_outs[0]

    on_last("0B5", None, out_rows)
    on_last("0B5", None, lambda gate: sum_gains((gate, early_0.kept)))
    drive(*(backward("1", group, group.cot_pieces, group.cot, views1) for group in members))
    drive(*(backward("0", group, group.pieces, group.d_in["1"], views0) for group in members))
    out_0.second()
    early_0.second()

    g_query, g_key, g_value, g_out = finish_early(
        early_0.halves, out_0.halves, both_1.halves, k_width
    )
    g_key, g_value = g_key.T, g_value.T
    g_gate, g_up, g_down = late_done[0]
    in_grad = by_layer(
        all_rows(lambda g: g.d_in["0"]), all_rows(lambda g: g.d_in["1"]).astype(F32)
    )
    return (
        layer_outs[0],
        in_grad,
        gain_mine[0][0][None],
        g_query[None],
        g_key[None],
        g_value[None],
        g_out[None],
        gain_mine[0][1][None],
        g_gate[None],
        g_up[None],
        g_down[None],
    )


def solution(mesh):
    row_spec = P(None, ("ctx", "head"), None)
    vector = P("section", "ctx")
    tall = P("section", "ctx", "head")
    wide = P("section", "head", "ctx")
    kept_rows = P("section", None, ("ctx", "head"), None)
    return jax.shard_map(
        local,
        mesh=mesh,
        in_specs=(row_spec, row_spec, P(), vector, tall, tall, tall, wide, vector, tall, tall, wide),
        out_specs=(kept_rows, kept_rows, vector, tall, tall, tall, wide, vector, tall, tall, wide),
        check_vma=False,
    )
```

```python
import jax
import jax.numpy as jnp
import numpy as np
from jax import lax
from jax.experimental import pallas as pl
from jax.experimental.pallas import tpu as pltpu
from jax.sharding import PartitionSpec as P

HEAD_DIM = 96
HALF = HEAD_DIM // 2
INV_ROOT = HEAD_DIM ** (-0.5)
EPSILON = 1e-05
ROPE_BASE = 100000.0
MASKED = -1e30
LANES = 128
UNIT_BLOCK = 512
F32 = jnp.float32
BF16 = jnp.bfloat16
GROUPS = 1
VMEM_LARGE = 60 * 1024 * 1024
VMEM_SMALL = 12 * 1024 * 1024


def swap(value, axis, step):
    count = lax.axis_size(axis)
    return lax.ppermute(value, axis, [(i, i ^ step) for i in range(count)])


def swap_from(value, source):
    return lax.ppermute(value, "section", [(source, 1 - source)])


def after(value, earlier):
    return lax.optimization_barrier((value, earlier))[0]


def dot(left, right):
    return jnp.dot(left, right, preferred_element_type=F32)


def dot_nt(left, right):
    return lax.dot_general(left, right, (((1,), (1,)), ((), ())), preferred_element_type=F32)


def dot_tn(left, right):
    return lax.dot_general(left, right, (((0,), (0,)), ((), ())), preferred_element_type=F32)


def split_terms(value):
    high = value.astype(BF16)
    return high, (value - high.astype(F32)).astype(BF16)


def shape(dims, dtype=BF16):
    return jax.ShapeDtypeStruct(dims, dtype)


def kept(dims, dtype=BF16):
    return pltpu.HBM(dims, dtype)


class View:
    def __init__(self, array, width=None, block=0):
        self.array = array
        self.width = array.shape[-1] if width is None else width
        self.block = block


def call(kernel, name, args, outs, scratch=(), flops=0, limit=VMEM_LARGE):
    specs, arrays = [], []
    size = 0
    for arg in args:
        if isinstance(arg, View):
            block = arg.block
            specs.append(
                pl.BlockSpec((arg.array.shape[0], arg.width), lambda i, block=block: (0, block))
            )
            arrays.append(arg.array)
            size += arg.array.shape[0] * arg.width * arg.array.dtype.itemsize
        else:
            zeros = (0,) * arg.ndim
            specs.append(pl.BlockSpec(arg.shape, lambda i, zeros=zeros: zeros))
            arrays.append(arg)
            size += arg.size * arg.dtype.itemsize
    out_specs = [
        pl.BlockSpec(out.shape, lambda i, zeros=(0,) * len(out.shape): zeros) for out in outs
    ]
    size += sum(int(np.prod(out.shape)) * jnp.dtype(out.dtype).itemsize for out in outs)
    return pl.pallas_call(
        kernel,
        grid=(1,),
        in_specs=specs,
        out_specs=out_specs,
        out_shape=outs,
        scratch_shapes=list(scratch),
        compiler_params=pltpu.CompilerParams(vmem_limit_bytes=limit),
        cost_estimate=pl.CostEstimate(flops=flops, bytes_accessed=size, transcendentals=0),
        name=name,
    )(*arrays)


def place(pieces, ctx):
    count = len(pieces)
    size, width = pieces[0].shape

    def kernel(*refs):
        whole = refs[count]
        mine = lax.axis_index("ctx")
        for k in range(count):
            at = pl.multiple_of((mine ^ k) * size, size)
            whole[pl.ds(at, size), :] = refs[k][...]

    return call(kernel, "place", pieces, [shape((count * size, width))])[0]


def write_pieces(outs, value, micros, start=0, width=None):
    heads = len(outs)
    piece = outs[0].shape[1]
    for m in range(micros):
        for k in range(heads):
            at = (m * heads + k) * piece
            outs[k][m] = value[at : at + piece].astype(BF16)


def read_pieces(whole, pieces, micros):
    heads = len(pieces)
    piece = pieces[0].shape[1]
    for m in range(micros):
        for k in range(heads):
            at = (m * heads + k) * piece
            whole[at : at + piece, :] = pieces[k][m]


def project(pieces, queries, kvs, gain_views, cosine, sine, turn):
    heads = len(pieces)
    micros, piece, d_model = pieces[0].shape
    rows = micros * heads * piece
    half = d_model // 2
    width = queries[0].width

    def kernel(*refs):
        xs = refs[:heads]
        q_own, q_other, kv_own, kv_other, g_own, g_other, cos, sin, turns, eye = refs[heads : heads + 10]
        na, q_out, kv_out, gains = refs[heads + 10 :]
        gains[:, :half] = dot_nt(eye[...], g_own[...])
        gains[:, half:] = dot_nt(eye[...], g_other[...])
        gain = gains[0:1, :]
        for m in range(micros):
            for k in range(heads):
                x = xs[k][m].astype(F32)
                scale = lax.rsqrt(jnp.mean(x * x, axis=-1, keepdims=True) + EPSILON)
                at = (m * heads + k) * piece
                na[at : at + piece, :] = (x * scale * gain).astype(BF16)
        low, high = na[:, :half], na[:, half:]
        for part, (own, other, out) in enumerate(
            ((q_own, q_other, q_out), (kv_own, kv_other, kv_out))
        ):
            lin = dot(low, own[...]) + dot(high, other[...])
            a, b = split_terms(lin)
            turned = dot(a, turns[part]) + dot(b, turns[part])
            at = part * width
            out[...] = (
                lin * cos[:, at : at + width] + turned * sin[:, at : at + width]
            ).astype(BF16)

    eye = jnp.asarray(np.eye(8, LANES), BF16)
    return call(
        kernel,
        "project",
        [*pieces, *queries, *kvs, *gain_views, cosine, sine, turn, eye],
        [kept((rows, d_model)), kept((rows, width)), shape((rows, width)), shape((8, d_model), F32)],
        flops=4 * rows * d_model * width,
    )


def attend(query, pieces, place_q, place_k, pad, outs_w, heads, piece, group):
    ctxs = len(pieces)
    micros, span, width = pieces[0].shape
    keys = ctxs * span
    rows = micros * span
    half = outs_w[0].array.shape[0]
    kv_heads = pad.shape[1] // LANES // 2

    def kernel(*refs):
        q_ref = refs[0]
        kvs = refs[1 : 1 + ctxs]
        pq, pk, pads, w_own, w_other = refs[1 + ctxs : 6 + ctxs]
        prob, mix = refs[6 + ctxs : 8 + ctxs]
        outs = refs[8 + ctxs : 8 + ctxs + heads]
        kv_rows, mixed = refs[8 + ctxs + heads :]
        for m in range(micros):
            for j in range(ctxs):
                kv_rows[j * span : (j + 1) * span, :] = kvs[j][m]
            kv = dot(kv_rows[...], pads[...]).astype(BF16)
            q = dot(q_ref[m * span : (m + 1) * span, :], pads[...]).astype(BF16)
            allowed = pk[m] <= pq[m]
            allowed = jnp.concatenate([allowed] * group, axis=0)
            for a in range(kv_heads):
                q2 = jnp.concatenate(
                    [q[:, (a * group + g) * LANES : (a * group + g + 1) * LANES] for g in range(group)],
                    axis=0,
                )
                key = kv[:, a * LANES : (a + 1) * LANES]
                value = kv[:, (kv_heads + a) * LANES : (kv_heads + a + 1) * LANES]
                scores = jnp.where(allowed, dot_nt(q2, key) * INV_ROOT, MASKED)
                top = jnp.max(scores, axis=-1, keepdims=True)
                weight = jnp.exp(scores - top)
                share = (weight / jnp.sum(weight, axis=-1, keepdims=True)).astype(BF16)
                prob[m * kv_heads + a] = share
                got = dot(share, value).astype(BF16)
                for g in range(group):
                    at = (a * group + g) * LANES
                    mixed[:, at : at + LANES] = got[g * span : (g + 1) * span]
            mix[m * span : (m + 1) * span, :] = dot_nt(mixed[...], pads[...]).astype(BF16)
        for t, w in enumerate((w_own, w_other)):
            branch = dot_nt(mix[...], w[...]).astype(BF16)
            for m in range(micros):
                for k in range(heads):
                    at = (m * heads + k) * piece
                    outs[k][m, :, t * half : (t + 1) * half] = branch[at : at + piece]

    return call(
        kernel,
        "attend",
        [query, *pieces, place_q, place_k, pad, *outs_w],
        [
            kept((micros * kv_heads, group * span, keys)),
            kept((rows, width)),
            *[shape((micros, piece, 2 * half)) for _ in range(heads)],
        ],
        [pltpu.VMEM((keys, width), BF16), pltpu.VMEM((span, pad.shape[1]), BF16)],
        flops=4 * rows * width * (keys + half),
    )


def add_mid(x, terms, gains):
    def kernel(*refs):
        x_ref, gain = refs[0], refs[1]
        parts = refs[2 : 2 + len(terms)]
        mid, nb = refs[2 + len(terms) :]
        total = x_ref[...].astype(F32)
        for part in parts:
            total = total + part[...].astype(F32)
        mid[...] = total
        scale = lax.rsqrt(jnp.mean(total * total, axis=-1, keepdims=True) + EPSILON)
        nb[...] = (total * scale * gain[1:2, :]).astype(BF16)

    return call(
        kernel,
        "add_mid",
        [x, gains, *terms],
        [shape(x.shape, F32), shape(x.shape)],
        limit=VMEM_SMALL,
    )


def add_out(mid, terms):
    def kernel(*refs):
        total = refs[0][...]
        for part in refs[1:-1]:
            total = total + part[...].astype(F32)
        refs[-1][...] = total.astype(BF16)

    return call(kernel, "add_out", [mid, *terms], [shape(mid.shape)], limit=VMEM_SMALL)[0]


def blocks_of(pair, units):
    specs, arrays = [], []
    count = units // UNIT_BLOCK
    for part in range(3):
        for array in pair:
            specs.append(
                pl.BlockSpec(
                    (array.shape[0], UNIT_BLOCK), lambda j, part=part: (0, part * count + j)
                )
            )
            arrays.append(array)
    return specs, arrays


def pack_places(half, units, width):
    hidden_at = -(-2 * half // UNIT_BLOCK) * UNIT_BLOCK
    mix_at = -(-(hidden_at + units) // width) * width
    return hidden_at, mix_at


def feed(pieces, pair, units, na, mix):
    heads = len(pieces)
    micros, piece, d_model = pieces[0].shape
    rows = micros * heads * piece
    half = d_model // 2
    count = units // UNIT_BLOCK
    width = mix.shape[1]
    hidden_at, mix_at = pack_places(half, units, width)

    def kernel(*refs):
        xs = refs[:heads]
        gate_w = refs[heads : heads + 2]
        up_w = refs[heads + 2 : heads + 4]
        down_w = refs[heads + 4 : heads + 6]
        na_in, mix_in = refs[heads + 6 : heads + 8]
        gate_out, up_out, hidden_out, nb, packed = refs[heads + 8 : heads + 13]
        outs = refs[heads + 13 : 2 * heads + 13]
        total = refs[-1]
        j = pl.program_id(0)

        @pl.when(j == 0)
        def _():
            read_pieces(nb, xs, micros)
            total[...] = jnp.zeros_like(total)
            packed[:, :half] = na_in[...]
            packed[:, half : 2 * half] = nb[:, half:]
            packed[:, mix_at : mix_at + width] = mix_in[...]

        low, high = nb[:, :half], nb[:, half:]
        gate = dot(low, gate_w[0][...]) + dot(high, gate_w[1][...])
        up = dot(low, up_w[0][...]) + dot(high, up_w[1][...])
        gate_out[...] = gate.astype(BF16)
        up_out[...] = up.astype(BF16)
        hidden = (gate * jax.nn.sigmoid(gate) * up).astype(BF16)
        hidden_out[...] = hidden
        at = pl.multiple_of(hidden_at + j * UNIT_BLOCK, UNIT_BLOCK)
        packed[:, pl.ds(at, UNIT_BLOCK)] = hidden
        total[:, :half] += dot_nt(hidden, down_w[0][...])
        total[:, half:] += dot_nt(hidden, down_w[1][...])

        @pl.when(j == count - 1)
        def _():
            write_pieces(outs, total, micros)

    specs, arrays = blocks_of(pair, units)
    whole = pl.BlockSpec((rows, d_model), lambda j: (0, 0))
    block = pl.BlockSpec((rows, UNIT_BLOCK), lambda j: (0, j))
    rows_spec = pl.BlockSpec((micros, piece, d_model), lambda j: (0, 0, 0))
    return pl.pallas_call(
        kernel,
        grid=(count,),
        in_specs=[rows_spec] * heads
        + specs
        + [pl.BlockSpec((rows, half), lambda j: (0, 1)), pl.BlockSpec(mix.shape, lambda j: (0, 0))],
        out_specs=[block, block, block, whole]
        + [pl.BlockSpec((rows, mix_at + width), lambda j: (0, 0))]
        + [rows_spec] * heads,
        out_shape=[
            kept((rows, units)),
            kept((rows, units)),
            kept((rows, units)),
            kept((rows, d_model)),
            kept((rows, mix_at + width)),
            *[shape((micros, piece, d_model)) for _ in range(heads)],
        ],
        scratch_shapes=[pltpu.VMEM((rows, d_model), F32)],
        compiler_params=pltpu.CompilerParams(vmem_limit_bytes=VMEM_LARGE),
        cost_estimate=pl.CostEstimate(
            flops=6 * rows * d_model * units, bytes_accessed=6 * d_model * units, transcendentals=0
        ),
        name="feed",
    )(*pieces, *arrays, na, mix)


def feed_back(pieces, pair, gate, up):
    heads = len(pieces)
    micros, piece, d_model = pieces[0].shape
    rows, units = gate.shape
    half = d_model // 2
    count = units // UNIT_BLOCK
    back_at = -(-half // UNIT_BLOCK) * UNIT_BLOCK

    def kernel(*refs):
        xs = refs[:heads]
        gate_w = refs[heads : heads + 2]
        up_w = refs[heads + 2 : heads + 4]
        down_w = refs[heads + 4 : heads + 6]
        gate_in, up_in = refs[heads + 6 : heads + 8]
        d_gate_out, d_up_out, gf, packed = refs[heads + 8 : heads + 12]
        outs = refs[heads + 12 : 2 * heads + 12]
        total = refs[-1]
        j = pl.program_id(0)

        @pl.when(j == 0)
        def _():
            read_pieces(gf, xs, micros)
            total[...] = jnp.zeros_like(total)
            packed[:, :half] = gf[:, half:]

        d_hidden = dot(gf[:, :half], down_w[0][...]) + dot(gf[:, half:], down_w[1][...])
        gate_v, up_v = gate_in[...].astype(F32), up_in[...].astype(F32)
        sigma = jax.nn.sigmoid(gate_v)
        d_gate = (d_hidden * up_v * sigma * (1.0 + gate_v * (1.0 - sigma))).astype(BF16)
        d_up = (d_hidden * gate_v * sigma).astype(BF16)
        d_gate_out[...] = d_gate
        d_up_out[...] = d_up
        at = pl.multiple_of(back_at + j * UNIT_BLOCK, UNIT_BLOCK)
        packed[:, pl.ds(at, UNIT_BLOCK)] = d_gate
        at = pl.multiple_of(back_at + units + j * UNIT_BLOCK, UNIT_BLOCK)
        packed[:, pl.ds(at, UNIT_BLOCK)] = d_up
        total[:, :half] += dot_nt(d_gate, gate_w[0][...]) + dot_nt(d_up, up_w[0][...])
        total[:, half:] += dot_nt(d_gate, gate_w[1][...]) + dot_nt(d_up, up_w[1][...])

        @pl.when(j == count - 1)
        def _():
            write_pieces(outs, total, micros)

    specs, arrays = blocks_of(pair, units)
    whole = pl.BlockSpec((rows, d_model), lambda j: (0, 0))
    block = pl.BlockSpec((rows, UNIT_BLOCK), lambda j: (0, j))
    rows_spec = pl.BlockSpec((micros, piece, d_model), lambda j: (0, 0, 0))
    return pl.pallas_call(
        kernel,
        grid=(count,),
        in_specs=[rows_spec] * heads + specs + [block, block],
        out_specs=[block, block, whole]
        + [pl.BlockSpec((rows, back_at + 2 * units), lambda j: (0, 0))]
        + [rows_spec] * heads,
        out_shape=[
            kept((rows, units)),
            kept((rows, units)),
            kept((rows, d_model)),
            kept((rows, back_at + 2 * units)),
            *[shape((micros, piece, d_model)) for _ in range(heads)],
        ],
        scratch_shapes=[pltpu.VMEM((rows, d_model), F32)],
        compiler_params=pltpu.CompilerParams(vmem_limit_bytes=VMEM_LARGE),
        cost_estimate=pl.CostEstimate(
            flops=6 * rows * d_model * units, bytes_accessed=6 * d_model * units, transcendentals=0
        ),
        name="feed_back",
    )(*pieces, *arrays, gate, up)


def norm_back(terms, residual, gains, row, carried):
    d_model = residual.shape[-1]

    def kernel(*refs):
        res, gain, carry = refs[:3]
        parts = refs[3 : 3 + len(terms)]
        d_out, d_low, d_gain = refs[3 + len(terms) :]
        d_normed = parts[0][...].astype(F32)
        for part in parts[1:]:
            d_normed = d_normed + part[...].astype(F32)
        rows = res[...].astype(F32)
        scale = lax.rsqrt(jnp.mean(rows * rows, axis=-1, keepdims=True) + EPSILON)
        unit = rows * scale
        d_gain[...] = jnp.sum(jnp.sum(d_normed * unit, axis=0), axis=0, keepdims=True)
        d_unit = d_normed * gain[row : row + 1, :]
        total = carry[...].astype(F32) + scale * (
            d_unit - unit * jnp.mean(d_unit * unit, axis=-1, keepdims=True)
        )
        d_out[...] = total
        d_low[...] = total.astype(BF16)

    return call(
        kernel,
        "norm_back",
        [residual, gains, carried, *terms],
        [shape(residual.shape, F32), shape(residual.shape), shape((1, d_model), F32)],
        limit=VMEM_SMALL,
    )


def attend_back(pieces, outs_w, mix, prob, query, kv_pieces, pad, turn, cosine, sine, group):
    heads = len(pieces)
    micros, piece, d_model = pieces[0].shape
    span = heads * piece
    rows = micros * span
    half = d_model // 2
    ctxs = len(kv_pieces)
    width = query.shape[1]
    keys = ctxs * span
    kv_heads = pad.shape[1] // LANES // 2

    def kernel(*refs):
        xs = refs[:heads]
        w_own, w_other, mix_in, prob_in, q_ref = refs[heads : heads + 5]
        kvs = refs[heads + 5 : heads + 5 + ctxs]
        pads, turns, cos, sin = refs[heads + 5 + ctxs : heads + 9 + ctxs]
        ga, ga_other, dq_out = refs[heads + 9 + ctxs : heads + 12 + ctxs]
        outs = refs[heads + 12 + ctxs : heads + 12 + 2 * ctxs]
        kv_rows, d_kv, d_q = refs[heads + 12 + 2 * ctxs :]
        read_pieces(ga, xs, micros)
        ga_other[...] = ga[:, half:]
        d_mix = (dot(ga[:, :half], w_own[...]) + dot(ga[:, half:], w_other[...])).astype(BF16)
        for m in range(micros):
            for j in range(ctxs):
                kv_rows[j * span : (j + 1) * span, :] = kvs[j][m]
            here = slice(m * span, (m + 1) * span)
            kv = dot(kv_rows[...], pads[...]).astype(BF16)
            q = dot(q_ref[here, :], pads[...]).astype(BF16)
            d = dot(d_mix[here], pads[...])
            product = d * dot(mix_in[here, :], pads[...])
            d = d.astype(BF16)
            for a in range(kv_heads):
                cuts = [slice((a * group + g) * LANES, (a * group + g + 1) * LANES) for g in range(group)]
                q2 = jnp.concatenate([q[:, cut] for cut in cuts], axis=0)
                d2 = jnp.concatenate([d[:, cut] for cut in cuts], axis=0)
                delta = jnp.concatenate(
                    [jnp.sum(product[:, cut], axis=-1, keepdims=True) for cut in cuts], axis=0
                )
                key = kv[:, a * LANES : (a + 1) * LANES]
                value = kv[:, (kv_heads + a) * LANES : (kv_heads + a + 1) * LANES]
                share = prob_in[m * kv_heads + a]
                d_prob = dot_nt(d2, value)
                d_score = (share.astype(F32) * (d_prob - delta)).astype(BF16)
                back = dot(d_score, key)
                for g, cut in enumerate(cuts):
                    d_q[:, cut] = back[g * span : (g + 1) * span]
                d_kv[:, a * LANES : (a + 1) * LANES] = dot_tn(d_score, q2).astype(BF16)
                d_kv[:, (kv_heads + a) * LANES : (kv_heads + a + 1) * LANES] = dot_tn(
                    share, d2
                ).astype(BF16)
            packed = dot_nt(d_kv[...], pads[...]).astype(BF16)
            for j in range(ctxs):
                outs[j][m] = packed[j * span : (j + 1) * span]
            high, low = split_terms(d_q[...])
            line = (dot_nt(high, pads[...]) + dot_nt(low, pads[...])) * INV_ROOT
            high, low = split_terms(line)
            turned = dot_nt(high, turns[0]) + dot_nt(low, turns[0])
            dq_out[here, :] = (line * cos[here, :width] + turned * sin[here, :width]).astype(BF16)

    return call(
        kernel,
        "attend_back",
        [*pieces, *outs_w, mix, prob, query, *kv_pieces, pad, turn, cosine, sine],
        [
            kept((rows, d_model)),
            shape((rows, half)),
            shape((rows, width)),
            *[shape((micros, span, width)) for _ in range(ctxs)],
        ],
        [
            pltpu.VMEM((keys, width), BF16),
            pltpu.VMEM((keys, pad.shape[1]), BF16),
            pltpu.VMEM((span, pad.shape[1]), F32),
        ],
        flops=10 * rows * width * keys,
    )


def project_back(terms, dq, queries, kvs, turn, cosine, sine, row_pieces):
    heads = len(row_pieces)
    micros, span, width = terms[0].shape
    rows = micros * span
    piece = span // heads
    half = queries[0].array.shape[0]
    count = len(terms)

    def kernel(*refs):
        parts = refs[:count]
        dq_in, q_own, q_other, kv_own, kv_other, turns, cos, sin = refs[count : count + 8]
        xs = refs[count + 8 : count + 8 + heads]
        d_line, d_gain = refs[count + 8 + heads : count + 10 + heads]
        outs = refs[count + 10 + heads : count + 10 + 2 * heads]
        unit = refs[-1]
        for m in range(micros):
            for k in range(heads):
                x = xs[k][m].astype(F32)
                scale = lax.rsqrt(jnp.mean(x * x, axis=-1, keepdims=True) + EPSILON)
                at = (m * heads + k) * piece
                unit[at : at + piece, :] = x * scale
        d_line[:, :width] = dq_in[...]
        lanes = lax.broadcasted_iota(jnp.int32, (span, width), 1)
        scaled = jnp.where(lanes < width // 2, INV_ROOT, 1.0)
        for m in range(micros):
            here = slice(m * span, (m + 1) * span)
            total = parts[0][m].astype(F32)
            for part in parts[1:]:
                total = total + part[m].astype(F32)
            total = total * scaled
            high, low = split_terms(total)
            turned = dot_nt(high, turns[1]) + dot_nt(low, turns[1])
            d_line[here, width:] = (
                total * cos[here, width:] + turned * sin[here, width:]
            ).astype(BF16)
        for t, (wq, wkv) in enumerate(((q_own, kv_own), (q_other, kv_other))):
            branch = dot_nt(d_line[:, :width], wq[...]) + dot_nt(d_line[:, width:], wkv[...])
            side = slice(t * half, (t + 1) * half)
            d_gain[:, side] = jnp.sum(branch * unit[:, side], axis=0, keepdims=True)
            branch = branch.astype(BF16)
            for m in range(micros):
                for k in range(heads):
                    at = (m * heads + k) * piece
                    outs[k][m, :, t * half : (t + 1) * half] = branch[at : at + piece]

    return call(
        kernel,
        "project_back",
        [*terms, dq, *queries, *kvs, turn, cosine, sine, *row_pieces],
        [
            kept((rows, 2 * width)),
            shape((1, 2 * half), F32),
            *[shape((micros, piece, 2 * half)) for _ in range(heads)],
        ],
        [pltpu.VMEM((rows, 2 * half), F32)],
        flops=8 * rows * half * width,
    )


def weight_grad(groups):
    half = groups[0][0][0].width
    total = sum(group[0][1].width for group in groups)
    args = [view for group in groups for pair in group for view in pair]

    def kernel(*refs):
        out = refs[-1]
        at = 0
        for g, group in enumerate(groups):
            n = group[0][1].width
            a, b, c, d = refs[4 * g : 4 * g + 4]
            out[:, at : at + n] = (dot_tn(a[...], b[...]) + dot_tn(c[...], d[...])).astype(BF16)
            at += n

    rows = groups[0][0][0].array.shape[0]
    return call(
        kernel, "weight_grad", args, [shape((half, total))], flops=4 * half * rows * total
    )[0]


def late_grad(nb, gf, d_gate, d_up, hidden, packed, packed_back):
    rows, d_model = nb.shape
    units = hidden.shape[1]
    half = d_model // 2
    count = units // UNIT_BLOCK
    hidden_at, _ = pack_places(half, units, LANES)
    back_at = -(-half // UNIT_BLOCK) * UNIT_BLOCK

    def kernel(*refs):
        sides = refs[:4]
        lines = refs[4:10]
        out = refs[10]
        turned, line = refs[11:13], refs[13]
        j = pl.program_id(0)

        @pl.when(j == 0)
        def _():
            for k, side in enumerate(sides):
                turned[k % 2][:, k // 2 * rows : (k // 2 + 1) * rows] = side[...].T

        for part in range(3):

            @pl.when(j // count == part)
            def _(part=part):
                line[:rows, :] = lines[part][...]
                line[rows:, :] = lines[3 + part][...]
                out[...] = dot(turned[(0, 0, 1)[part]][...], line[...]).astype(BF16)

    def side(block):
        return pl.BlockSpec((rows, half), lambda j: (0, block))

    def line(part, first):
        return pl.BlockSpec(
            (rows, UNIT_BLOCK),
            lambda j: (0, first // UNIT_BLOCK + jnp.clip(j - part * count, 0, count - 1)),
        )

    return pl.pallas_call(
        kernel,
        grid=(3 * count,),
        in_specs=[side(0), side(0), side(1), side(0)]
        + [line(part, 0) for part in range(3)]
        + [line(0, back_at), line(1, back_at + units), line(2, hidden_at)],
        out_specs=pl.BlockSpec((half, UNIT_BLOCK), lambda j: (0, j)),
        out_shape=kept((half, 3 * units)),
        scratch_shapes=[pltpu.VMEM((half, 2 * rows), BF16)] * 2
        + [pltpu.VMEM((2 * rows, UNIT_BLOCK), BF16)],
        compiler_params=pltpu.CompilerParams(vmem_limit_bytes=VMEM_LARGE),
        cost_estimate=pl.CostEstimate(
            flops=12 * half * rows * units, bytes_accessed=6 * half * units, transcendentals=0
        ),
        name="late_grad",
    )(nb, gf, packed, packed_back, d_gate, d_up, hidden, packed_back, packed_back, packed)


def finish_late(lower, upper, units):
    size, _ = lower[0].shape
    count = units // UNIT_BLOCK

    def kernel(*refs):
        parts, outs = refs[:12], refs[12:]
        first = lax.axis_index("section") == 0
        for which in range(3):
            a0, a1, b0, b1 = (parts[4 * which + k][...].astype(F32) for k in range(4))
            top, low = jnp.where(first, a0, b0), jnp.where(first, a1, b1)
            if which < 2:
                outs[which][:size, :] = top
                outs[which][size:, :] = low
            else:
                outs[2][:, :size] = top.T
                outs[2][:, size:] = low.T

    specs, arrays = [], []
    for which in range(3):
        for array in (*lower, *upper):
            specs.append(
                pl.BlockSpec((size, UNIT_BLOCK), lambda j, which=which: (0, which * count + j))
            )
            arrays.append(array)
    flat = pl.BlockSpec((2 * size, UNIT_BLOCK), lambda j: (0, j))
    return pl.pallas_call(
        kernel,
        grid=(count,),
        in_specs=specs,
        out_specs=[flat, flat, pl.BlockSpec((UNIT_BLOCK, 2 * size), lambda j: (j, 0))],
        out_shape=[
            kept((2 * size, units), F32),
            kept((2 * size, units), F32),
            kept((units, 2 * size), F32),
        ],
        compiler_params=pltpu.CompilerParams(vmem_limit_bytes=VMEM_LARGE),
        cost_estimate=pl.CostEstimate(
            flops=0, bytes_accessed=48 * size * units, transcendentals=0
        ),
        name="finish_late",
    )(*arrays)


def finish_early(lower, upper, width, k_width):
    size, lines = lower[0].shape

    def kernel(*refs):
        a0, a1, b0, b1, query, key, value, out = refs
        first = lax.axis_index("section") == 0
        for t, (a, b) in enumerate(((a0, b0), (a1, b1))):
            rows = slice(t * size, (t + 1) * size)
            both = jnp.where(first, a[...].astype(F32), b[...].astype(F32))
            line = both[:, width:]
            query[rows, :] = line[:, :width]
            key[:, rows] = line[:, width : width + k_width].T
            value[:, rows] = line[:, width + k_width :].T
            out[:, rows] = both[:, :width].T

    return call(
        kernel,
        "finish_early",
        [*lower, *upper],
        [
            kept((2 * size, width), F32),
            kept((k_width, 2 * size), F32),
            kept((k_width, 2 * size), F32),
            kept((width, 2 * size), F32),
        ],
    )


def relative_columns(value, section, ctxs):
    width = value.shape[-1] // (2 * ctxs)
    return jnp.concatenate(
        [
            lax.dynamic_slice_in_dim(
                value, (k * 2 + (section ^ t)) * width, width, axis=value.ndim - 1
            )
            for t in range(2)
            for k in range(ctxs)
        ],
        axis=-1,
    )


def stored_columns(value, section, ctxs):
    width = value.shape[-1] // (2 * ctxs)
    return jnp.concatenate(
        [
            lax.dynamic_slice_in_dim(
                value, ((section ^ t) * ctxs + k) * width, width, axis=value.ndim - 1
            )
            for k in range(ctxs)
            for t in range(2)
        ],
        axis=-1,
    )


def send_all(pieces, axis):
    return [pieces[0]] + [swap(piece, axis, k) for k, piece in enumerate(pieces[1:], 1)]


def send_rows(rows):
    return send_all([rows] * lax.axis_size("head"), "head")


def send_blocks(rows):
    return send_all([rows] * lax.axis_size("ctx"), "ctx")


class Fetch:
    def __init__(self, shard):
        self.shard = shard

    def send(self, gate=None):
        self.pieces = send_blocks(self.shard if gate is None else after(self.shard, gate))

    def settle(self, gate=None):
        own = place(after(self.pieces, gate), lax.axis_index("ctx"))
        self.pair = (own, swap(own, "section", 1))
        return self.pair

    def direct(self, gate=None, with_rows=None):
        shard = self.shard if gate is None else after(self.shard, gate)
        pieces = send_blocks(shard)
        if with_rows is not None:
            pieces = after(pieces, with_rows)
        own = place(pieces, lax.axis_index("ctx"))
        self.pair = (own, swap(own, "section", 1))
        return pieces[1:]

    def first(self, gate=None):
        shard = self.shard if gate is None else after(self.shard, gate)
        self.own = lax.all_gather(shard, "ctx", axis=0, tiled=True)
        return self.own

    def second(self, gate=None):
        own = self.own if gate is None else after(self.own, gate)
        self.pair = (own, swap(own, "section", 1))
        return self.pair[1]


class Settle:
    def __init__(self, source):
        self.source = source

    def first(self, whole):
        self.kept = lax.psum_scatter(whole, "ctx", scatter_dimension=0, tiled=True)
        return whole

    def direct(self, whole, gate=None):
        if gate is not None:
            whole = after(whole, gate)
        ctxs = lax.axis_size("ctx")
        ctx = lax.axis_index("ctx")
        size = whole.shape[0] // ctxs
        parts = [
            lax.dynamic_slice_in_dim(whole, (ctx ^ k) * size, size, axis=0) for k in range(ctxs)
        ]
        total = None
        for term in send_all(parts, "ctx"):
            term = term.astype(F32)
            total = term if total is None else total + term
        self.kept = total.astype(BF16)
        return whole

    def second(self, gate=None):
        kept = self.kept if gate is None else after(self.kept, gate)
        self.kept = kept
        sent = swap_from(kept, self.source)
        self.halves = (kept, sent) if self.source == 1 else (sent, kept)
        return sent


class Chain:
    def __init__(self):
        self.tasks = {}
        self.due = {}

    def plan(self, start, end, task):
        self.tasks.setdefault(start, []).append((end, task))

    def enter(self, name, value):
        done = self.due.pop(name, [])
        return after(value, done) if done else value

    def leave(self, name, value):
        for end, task in self.tasks.pop(name, []):
            result = task(value)
            if end is not None:
                self.due.setdefault(end, []).append(result)


class Plan:
    pass


def pick(first, a, b):
    return jnp.where(first, a, b)


def turning(heads_turned, heads):
    turn = np.zeros((heads * HEAD_DIM, heads * HEAD_DIM), np.float32)
    for h in range(heads_turned):
        for i in range(HALF):
            turn[h * HEAD_DIM + HALF + i, h * HEAD_DIM + i] = -1.0
            turn[h * HEAD_DIM + i, h * HEAD_DIM + HALF + i] = 1.0
    return turn


def padding(heads):
    pad = np.zeros((heads * HEAD_DIM, heads * LANES), np.float32)
    for h in range(heads):
        for i in range(HEAD_DIM):
            pad[h * HEAD_DIM + i, h * LANES + i] = 1.0
    return pad


def local(
    layer_input,
    out_cotangent,
    block_order,
    gain_attn,
    w_query,
    w_key,
    w_value,
    w_out,
    gain_ffn,
    w_gate,
    w_up,
    w_down,
):
    section = lax.axis_index("section")
    head = lax.axis_index("head")
    ctx = lax.axis_index("ctx")
    heads = lax.axis_size("head")
    ctxs = lax.axis_size("ctx")
    first = section == 0
    micros_all = layer_input.shape[0] // 2
    micros = micros_all // GROUPS
    rows_dev = layer_input.shape[1]
    d_model = layer_input.shape[2]
    span = heads * rows_dev
    rows = micros * span
    block_rows = ctxs * span // block_order.shape[1]
    d_half = d_model // ctxs // 2
    width = w_query.shape[2]
    k_width = w_key.shape[2]
    units = w_gate.shape[2]
    group_size = width // k_width
    line_heads = width // HEAD_DIM
    chain = Chain()

    turn = jnp.asarray(
        np.stack([turning(line_heads, line_heads), turning(k_width // HEAD_DIM, line_heads)]), BF16
    )
    pad = jnp.asarray(padding(line_heads), BF16)

    def places_of(order, ctx_index):
        piece = jnp.arange(span, dtype=jnp.int32)
        stored = (ctx_index * heads + (head ^ (piece // rows_dev))) * rows_dev + piece % rows_dev
        block = stored // block_rows
        match = block[:, None] == jnp.arange(order.shape[1], dtype=jnp.int32)[None, :]
        base = jnp.sum(jnp.where(match[None], order[:, None, :], 0), axis=2)
        return base * block_rows + (stored % block_rows)[None]

    frequency = jnp.power(ROPE_BASE, jnp.arange(HALF, dtype=F32) * (-2.0 / HEAD_DIM))

    def group_of(index):
        group = Plan()
        at = section * micros_all + index * micros
        group.name = "ab"[index]
        order = lax.dynamic_slice_in_dim(block_order, at, micros, axis=0)
        places_q = places_of(order, ctx)
        places_k = jnp.concatenate([places_of(order, ctx ^ k) for k in range(ctxs)], axis=1)
        group.place_q = places_q[:, :, None]
        group.place_k = places_k[:, None, :]
        group.places = places_q

        def make_tables(places):
            angles = places.reshape(rows, 1).astype(F32) * frequency
            cosine, sine = jnp.cos(angles), jnp.sin(angles)
            turned = 2 * (line_heads + k_width // HEAD_DIM)
            fixed = width - k_width
            group.cosine = jnp.concatenate(
                [cosine] * turned + [jnp.ones((rows, fixed), F32)], axis=1
            )
            group.sine = jnp.concatenate(
                [sine] * turned + [jnp.zeros((rows, fixed), F32)], axis=1
            )

        group.make_tables = make_tables

        def mine(value):
            part = lax.dynamic_slice_in_dim(value, at, micros, axis=0)
            return relative_columns(part, section, ctxs)

        group.x = mine(layer_input)
        group.cot = mine(out_cotangent)
        group.keep, group.d_in = {}, {}
        return group

    members = [group_of(index) for index in range(GROUPS)]
    tail = members[-1].name
    for group in members:
        group.firsts = send_rows(group.x)
        group.cot_pieces = [group.cot] * heads

    def exchange(shard, gate=None):
        def cut(which):
            return lax.dynamic_slice_in_dim(shard, which * d_half, d_half, axis=0)

        kept, given = cut(section), cut(1 - section)
        if gate is not None:
            given = after(given, gate)
        taken = swap(given, "section", 1)
        return pick(first, kept, taken), pick(first, taken, kept)

    gains = jnp.stack([gain_attn[0], gain_ffn[0]], axis=1)
    gains = jnp.pad(gains, ((0, 0), (0, LANES - 2)))
    early_shards = exchange(
        jnp.concatenate([w_query[0], w_key[0], w_value[0], gains], axis=1)
    )
    early0 = Fetch(early_shards[0])
    early0.send([group.firsts[1] for group in members])
    tables = after([group.places for group in members], early0.pieces[1])
    for group, places in zip(members, tables):
        group.make_tables(places)
    early0.settle([(group.cosine, group.sine, group.firsts) for group in members])
    landed = early0.pair[:1]
    w_late, w_o = after(((w_gate[0], w_up[0], w_down[0]), w_out[0]), landed)
    out_shards = exchange(w_o.T)
    late_shards = exchange(jnp.concatenate([w_late[0], w_late[1], w_late[2].T], axis=1))
    late0, late1 = Fetch(late_shards[0]), Fetch(late_shards[1])
    out0 = Fetch(out_shards[0])
    both1 = Fetch(jnp.concatenate([out_shards[1], early_shards[1]], axis=1))
    late0.first(landed)
    out0.send(landed)

    def views0(name):
        if name == "o":
            return [View(part, width, 0) for part in out0.pair]
        at = {"q": (width, 0), "kv": (width, 1), "g": (LANES, 2 * width // LANES)}[name]
        return [View(part, *at) for part in early0.pair]

    def views1(name):
        at = {
            "o": (width, 0),
            "q": (width, 1),
            "kv": (width, 2),
            "g": (LANES, 3 * width // LANES),
        }[name]
        return [View(part, *at) for part in both1.pair]

    token = [None]

    def enter(name, group, value):
        if token[0] is not None and GROUPS > 1:
            value = after(value, token[0])
        return chain.enter(name + group.name, value)

    def leave(name, group, value):
        token[0] = value
        chain.leave(name + group.name, value)

    def forward(label, group, layer_in, views, late_fetch):
        keep = Plan()
        keep.x = layer_in
        pieces = group.firsts if label == "0" else send_rows(layer_in)
        leave(label + "F0", group, layer_in)
        yield
        pieces = enter(label + "F1", group, pieces)
        keep.x_pieces = pieces
        keep.na, keep.query, kv, keep.gains = project(
            pieces, views("q"), views("kv"), views("g"), group.cosine, group.sine, turn
        )
        kv = kv.reshape(micros, span, width)
        pieces = send_blocks(kv)
        leave(label + "F1", group, kv)
        yield
        keep.kv = enter(label + "F2", group, pieces)
        keep.prob, keep.mix, *parts = attend(
            keep.query, keep.kv, group.place_q, group.place_k, pad, views("o"),
            heads, rows_dev, group_size,
        )
        terms = send_all(parts, "head")
        leave(label + "F2", group, parts[0])
        yield
        terms = enter(label + "F3", group, terms)
        keep.mid, own_nb = add_mid(layer_in, terms, keep.gains)
        pieces = send_rows(own_nb)
        leave(label + "F3", group, own_nb)
        yield
        pieces = enter(label + "F4", group, pieces)
        keep.late = late_fetch.pair
        keep.gate, keep.up, keep.hidden, keep.nb, packed, *parts = feed(
            pieces, keep.late, units, keep.na, keep.mix
        )
        keep.packed = swap(packed, "section", 1)
        group.parts = parts
        group.keep[label] = keep
        leave(label + "F4", group, parts[0])
        if label == "0":
            terms = send_all(parts, "head")
            yield
            terms = enter(label + "F5", group, terms)
            group.out = add_out(keep.mid, terms)

    def backward(label, group, pieces, grad, views):
        keep = group.keep[label]
        if label == "0":
            pieces = enter(label + "B1", group, pieces)
        keep.d_gate, keep.d_up, keep.gf, packed, *parts = feed_back(
            pieces, keep.late, keep.gate, keep.up
        )
        keep.packed_back = swap(packed, "section", 1)
        terms = send_all(parts, "head")
        leave(label + "B1", group, parts[0])
        yield
        terms = enter(label + "B2", group, terms)
        d_mid, own_ga, keep.gain_b = norm_back(terms, keep.mid, keep.gains, 1, grad)
        pieces = send_rows(own_ga)
        leave(label + "B2", group, own_ga)
        yield
        pieces = enter(label + "B3", group, pieces)
        keep.ga, ga_other, dq, *parts = attend_back(
            pieces, views("o"), keep.mix, keep.prob, keep.query, keep.kv, pad, turn,
            group.cosine, group.sine, group_size,
        )
        terms = send_all(parts, "ctx")
        keep.ga_other = swap(ga_other, "section", 1)
        leave(label + "B3", group, parts[0])
        yield
        terms = enter(label + "B4", group, terms)
        keep.d_line, keep.gain_a, *parts = project_back(
            terms, dq, views("q"), views("kv"), turn, group.cosine, group.sine, keep.x_pieces
        )
        terms = send_all(parts, "head")
        keep.d_line_other = swap(keep.d_line, "section", 1)
        leave(label + "B4", group, parts[0])
        leave(label + "B4z", group, terms[1])
        yield
        terms = enter(label + "B5", group, terms)
        d_input, d_low, _ = norm_back(terms, keep.x, keep.gains, 0, d_mid)
        if label == "1":
            group.d_in[label] = d_low
            group.pieces = send_rows(d_low)
        else:
            group.d_in[label] = d_input
        leave(label + "B5", group, group.d_in[label])
        yield

    def drive(*stages):
        waiting = list(stages)
        while waiting:
            waiting = [stage for stage in waiting if next(stage, stage) is not stage]

    def gather_cot(group, which):
        def task(gate):
            for k in which:
                if k < heads:
                    group.cot_pieces[k] = swap(after(group.cot, gate), "head", k)
            return group.cot_pieces[1:]

        return task

    for group in members:
        chain.plan("0F1" + group.name, "0F2" + group.name, gather_cot(group, [2, 1]))
        chain.plan("1F1" + group.name, "1F2" + group.name, gather_cot(group, range(3, heads)))

    def on_last(start, end, task):
        chain.plan(start + tail, end + tail if end else None, task)

    on_last("0F1", "0F2", out0.settle)
    on_last("0F3", None, late0.second)
    on_last("0F3", None, lambda gate: both1.first(late0.pair[0]))
    on_last("1F0", None, both1.second)
    on_last("1F0", None, lambda gate: late1.first(both1.pair[0]))
    on_last("1F3", None, late1.second)
    drive(*(forward("0", group, group.x, views0, late0) for group in members))

    def scatter_out(group, which):
        def task(gate):
            group.terms += [
                swap(after(group.parts[k], gate), "head", k) for k in which if k < heads
            ]
            return group.terms[1:]

        return task

    def finish_out(group):
        def task(gate):
            group.final = add_out(group.keep["1"].mid, group.terms)
            return group.final

        return task

    drive(*(forward("1", group, group.out, views1, late1) for group in members))
    for group in members:
        group.terms = [group.parts[0]]
        chain.plan("1B3" + group.name, "1B4" + group.name, scatter_out(group, [2, 1]))
        chain.plan("0B3" + group.name, "0B4" + group.name, scatter_out(group, range(3, heads)))
        chain.plan("0B5" + group.name, None, finish_out(group))

    _, mix_at = pack_places(d_model // 2, units, width)

    def rows_of(label, *names):
        def joined(name):
            parts = [getattr(group.keep[label], name) for group in members]
            return parts[0] if len(parts) == 1 else jnp.concatenate(parts, axis=0)

        return [joined(name) for name in names]

    def late_of(label, gate):
        names = ("nb", "gf", "d_gate", "d_up", "hidden", "packed", "packed_back")
        return late_grad(*after(rows_of(label, *names), gate))

    def out_group(ga, mix, ga_other, packed):
        return (
            (View(ga, d_model // 2, 0), View(mix)),
            (View(ga_other), View(packed, width, mix_at // width)),
        )

    def early_group(na, d_line, packed, d_line_other):
        return (
            (View(na, d_model // 2, 0), View(d_line)),
            (View(packed, d_model // 2, 0), View(d_line_other)),
        )

    out_names = ("ga", "mix", "ga_other", "packed")
    early_names = ("na", "d_line", "packed", "d_line_other")

    def out_of(label, gate):
        return weight_grad([out_group(*after(rows_of(label, *out_names), gate))])

    def early_of(label, gate):
        return weight_grad([early_group(*after(rows_of(label, *early_names), gate))])

    def both_of(label, gate):
        values = after(rows_of(label, *out_names, *early_names), gate)
        return weight_grad([out_group(*values[:4]), early_group(*values[4:])])

    late_1, both_1, late_0, both_0 = (Settle(s) for s in (0, 0, 1, 1))
    on_last("1B2", "1B3", lambda gate: late_1.first(late_of("1", gate)))
    on_last("1B5", "0B1", late_1.second)
    on_last("1B5", "0B1", lambda gate: both_1.first(both_of("1", (gate, late_1.kept))))
    on_last("0B2", "0B3", both_1.second)
    on_last("0B2", "0B3", lambda gate: late_0.first(late_of("0", (gate, both_1.kept))))
    on_last("0B5", None, late_0.second)
    late_done = []

    def finish(gate):
        late_done.append(finish_late(late_0.halves, late_1.halves, units))
        return late_done[0]

    on_last("0B5", None, finish)
    on_last("0B5", None, lambda gate: both_0.second(late_done[0]))
    last = []

    def last_grad(gate):
        last.append(both_0.first(both_of("0", gate)))
        return last[0]

    on_last("0B4z", "0B5", last_grad)

    gain_mine = []

    def sum_gains(gate):
        def gain_of(label, name):
            total = getattr(members[0].keep[label], name)
            for group in members[1:]:
                total = total + getattr(group.keep[label], name)
            return total[0]

        gain_rows = jnp.stack(
            [gain_of(label, name) for label in "01" for name in ("gain_a", "gain_b")]
        )
        gain_rows = after(gain_rows, gate)
        half = d_model // 2
        got = swap(pick(first, gain_rows[2:], gain_rows[:2]), "section", 1)
        got = jnp.concatenate([got[:, half:], got[:, :half]], axis=1)
        blocks = (pick(first, gain_rows[:2], gain_rows[2:]) + got).reshape(4, ctxs, d_half)

        def sum_over(values):
            total = values[0]
            for value in values[1:]:
                total = total + value
            return total

        mine = [
            lax.dynamic_index_in_dim(blocks, ctx ^ k, 1, keepdims=False) for k in range(ctxs)
        ]
        part = sum_over(send_all(mine, "ctx"))
        part = sum_over(send_all([part] * heads, "head")).reshape(2, 2, d_half)
        part = pick(first, part, part[:, ::-1])
        gain_mine.append(part.reshape(2, 2 * d_half))
        return gain_mine[0]

    def by_layer(lower, upper):
        lower = stored_columns(lower, section, ctxs)
        upper = stored_columns(upper, section, ctxs)
        kept_rows = pick(first, lower, upper)
        got_rows = swap(pick(first, upper, lower).astype(BF16), "section", 1).astype(lower.dtype)
        return jnp.concatenate(
            [pick(first, kept_rows, got_rows), pick(first, got_rows, kept_rows)], axis=0
        )[None]

    def all_rows(name):
        parts = [name(group) for group in members]
        return parts[0] if len(parts) == 1 else jnp.concatenate(parts, axis=0)

    layer_outs = []

    def out_rows(gate):
        lower, upper = after((all_rows(lambda g: g.out), all_rows(lambda g: g.final)), gate)
        layer_outs.append(by_layer(lower, upper))
        return layer_outs[0]

    on_last("0B5", None, out_rows)
    on_last("0B5", None, lambda gate: sum_gains((gate, last[0])))
    drive(*(backward("1", group, group.cot_pieces, group.cot, views1) for group in members))
    drive(*(backward("0", group, group.pieces, group.d_in["1"], views0) for group in members))

    g_query, g_key, g_value, g_out = finish_early(
        both_0.halves, both_1.halves, width, k_width
    )
    g_key, g_value = g_key.T, g_value.T
    g_gate, g_up, g_down = late_done[0]
    in_grad = by_layer(
        all_rows(lambda g: g.d_in["0"]), all_rows(lambda g: g.d_in["1"]).astype(F32)
    )
    return (
        layer_outs[0],
        in_grad,
        gain_mine[0][0][None],
        g_query[None],
        g_key[None],
        g_value[None],
        g_out[None],
        gain_mine[0][1][None],
        g_gate[None],
        g_up[None],
        g_down[None],
    )


def solution(mesh):
    row_spec = P(None, ("ctx", "head"), None)
    vector = P("section", "ctx")
    tall = P("section", "ctx", "head")
    wide = P("section", "head", "ctx")
    kept_rows = P("section", None, ("ctx", "head"), None)
    return jax.shard_map(
        local,
        mesh=mesh,
        in_specs=(row_spec, row_spec, P(), vector, tall, tall, tall, wide, vector, tall, tall, wide),
        out_specs=(kept_rows, kept_rows, vector, tall, tall, tall, wide, vector, tall, tall, wide),
        check_vma=False,
    )
```

```python
import jax
import jax.numpy as jnp
import numpy as np
from jax import lax
from jax.experimental import pallas as pl
from jax.experimental.pallas import tpu as pltpu
from jax.sharding import PartitionSpec as P

HEAD_DIM = 96
HALF = HEAD_DIM // 2
INV_ROOT = HEAD_DIM ** (-0.5)
EPSILON = 1e-05
ROPE_BASE = 100000.0
MASKED = -1e30
LANES = 128
UNIT_BLOCK = 512
F32 = jnp.float32
BF16 = jnp.bfloat16
GROUPS = 1
VMEM_LARGE = 60 * 1024 * 1024
VMEM_SMALL = 12 * 1024 * 1024


def swap(value, axis, step):
    count = lax.axis_size(axis)
    return lax.ppermute(value, axis, [(i, i ^ step) for i in range(count)])


def swap_from(value, source):
    return lax.ppermute(value, "section", [(source, 1 - source)])


def after(value, earlier):
    return lax.optimization_barrier((value, earlier))[0]


def dot(left, right):
    return jnp.dot(left, right, preferred_element_type=F32)


def dot_nt(left, right):
    return lax.dot_general(left, right, (((1,), (1,)), ((), ())), preferred_element_type=F32)


def dot_tn(left, right):
    return lax.dot_general(left, right, (((0,), (0,)), ((), ())), preferred_element_type=F32)


def split_terms(value):
    high = value.astype(BF16)
    return high, (value - high.astype(F32)).astype(BF16)


def shape(dims, dtype=BF16):
    return jax.ShapeDtypeStruct(dims, dtype)


def kept(dims, dtype=BF16):
    return pltpu.HBM(dims, dtype)


class View:
    def __init__(self, array, width=None, block=0):
        self.array = array
        self.width = array.shape[-1] if width is None else width
        self.block = block


def call(kernel, name, args, outs, scratch=(), flops=0, limit=VMEM_LARGE):
    specs, arrays = [], []
    size = 0
    for arg in args:
        if isinstance(arg, View):
            block = arg.block
            specs.append(
                pl.BlockSpec((arg.array.shape[0], arg.width), lambda i, block=block: (0, block))
            )
            arrays.append(arg.array)
            size += arg.array.shape[0] * arg.width * arg.array.dtype.itemsize
        else:
            zeros = (0,) * arg.ndim
            specs.append(pl.BlockSpec(arg.shape, lambda i, zeros=zeros: zeros))
            arrays.append(arg)
            size += arg.size * arg.dtype.itemsize
    out_specs = [
        pl.BlockSpec(out.shape, lambda i, zeros=(0,) * len(out.shape): zeros) for out in outs
    ]
    size += sum(int(np.prod(out.shape)) * jnp.dtype(out.dtype).itemsize for out in outs)
    return pl.pallas_call(
        kernel,
        grid=(1,),
        in_specs=specs,
        out_specs=out_specs,
        out_shape=outs,
        scratch_shapes=list(scratch),
        compiler_params=pltpu.CompilerParams(vmem_limit_bytes=limit),
        cost_estimate=pl.CostEstimate(flops=flops, bytes_accessed=size, transcendentals=0),
        name=name,
    )(*arrays)


def place(pieces, ctx):
    count = len(pieces)
    size, width = pieces[0].shape

    def kernel(*refs):
        whole = refs[count]
        mine = lax.axis_index("ctx")
        for k in range(count):
            at = pl.multiple_of((mine ^ k) * size, size)
            whole[pl.ds(at, size), :] = refs[k][...]

    return call(kernel, "place", pieces, [shape((count * size, width))])[0]


def write_pieces(outs, value, micros, start=0, width=None):
    heads = len(outs)
    piece = outs[0].shape[1]
    for m in range(micros):
        for k in range(heads):
            at = (m * heads + k) * piece
            outs[k][m] = value[at : at + piece].astype(BF16)


def read_pieces(whole, pieces, micros):
    heads = len(pieces)
    piece = pieces[0].shape[1]
    for m in range(micros):
        for k in range(heads):
            at = (m * heads + k) * piece
            whole[at : at + piece, :] = pieces[k][m]


def project(pieces, queries, kvs, gain_views, cosine, sine, turn):
    heads = len(pieces)
    micros, piece, d_model = pieces[0].shape
    rows = micros * heads * piece
    half = d_model // 2
    width = queries[0].width

    def kernel(*refs):
        xs = refs[:heads]
        q_own, q_other, kv_own, kv_other, g_own, g_other, cos, sin, turns, eye = refs[heads : heads + 10]
        na, q_out, kv_out, gains = refs[heads + 10 :]
        gains[:, :half] = dot_nt(eye[...], g_own[...])
        gains[:, half:] = dot_nt(eye[...], g_other[...])
        gain = gains[0:1, :]
        for m in range(micros):
            for k in range(heads):
                x = xs[k][m].astype(F32)
                scale = lax.rsqrt(jnp.mean(x * x, axis=-1, keepdims=True) + EPSILON)
                at = (m * heads + k) * piece
                na[at : at + piece, :] = (x * scale * gain).astype(BF16)
        low, high = na[:, :half], na[:, half:]
        for part, (own, other, out) in enumerate(
            ((q_own, q_other, q_out), (kv_own, kv_other, kv_out))
        ):
            lin = dot(low, own[...]) + dot(high, other[...])
            a, b = split_terms(lin)
            turned = dot(a, turns[part]) + dot(b, turns[part])
            at = part * width
            out[...] = (
                lin * cos[:, at : at + width] + turned * sin[:, at : at + width]
            ).astype(BF16)

    eye = jnp.asarray(np.eye(8, LANES), BF16)
    return call(
        kernel,
        "project",
        [*pieces, *queries, *kvs, *gain_views, cosine, sine, turn, eye],
        [kept((rows, d_model)), kept((rows, width)), shape((rows, width)), shape((8, d_model), F32)],
        flops=4 * rows * d_model * width,
    )


def attend(query, pieces, place_q, place_k, pad, outs_w, heads, piece, group):
    ctxs = len(pieces)
    micros, span, width = pieces[0].shape
    keys = ctxs * span
    rows = micros * span
    half = outs_w[0].array.shape[0]
    kv_heads = pad.shape[1] // LANES // 2

    def kernel(*refs):
        q_ref = refs[0]
        kvs = refs[1 : 1 + ctxs]
        pq, pk, pads, w_own, w_other = refs[1 + ctxs : 6 + ctxs]
        prob, mix = refs[6 + ctxs : 8 + ctxs]
        outs = refs[8 + ctxs : 8 + ctxs + heads]
        kv_rows, mixed = refs[8 + ctxs + heads :]
        for m in range(micros):
            for j in range(ctxs):
                kv_rows[j * span : (j + 1) * span, :] = kvs[j][m]
            kv = dot(kv_rows[...], pads[...]).astype(BF16)
            q = dot(q_ref[m * span : (m + 1) * span, :], pads[...]).astype(BF16)
            allowed = pk[m] <= pq[m]
            allowed = jnp.concatenate([allowed] * group, axis=0)
            for a in range(kv_heads):
                q2 = jnp.concatenate(
                    [q[:, (a * group + g) * LANES : (a * group + g + 1) * LANES] for g in range(group)],
                    axis=0,
                )
                key = kv[:, a * LANES : (a + 1) * LANES]
                value = kv[:, (kv_heads + a) * LANES : (kv_heads + a + 1) * LANES]
                scores = jnp.where(allowed, dot_nt(q2, key) * INV_ROOT, MASKED)
                top = jnp.max(scores, axis=-1, keepdims=True)
                weight = jnp.exp(scores - top)
                share = (weight / jnp.sum(weight, axis=-1, keepdims=True)).astype(BF16)
                prob[m * kv_heads + a] = share
                got = dot(share, value).astype(BF16)
                for g in range(group):
                    at = (a * group + g) * LANES
                    mixed[:, at : at + LANES] = got[g * span : (g + 1) * span]
            mix[m * span : (m + 1) * span, :] = dot_nt(mixed[...], pads[...]).astype(BF16)
        for t, w in enumerate((w_own, w_other)):
            branch = dot_nt(mix[...], w[...]).astype(BF16)
            for m in range(micros):
                for k in range(heads):
                    at = (m * heads + k) * piece
                    outs[k][m, :, t * half : (t + 1) * half] = branch[at : at + piece]

    return call(
        kernel,
        "attend",
        [query, *pieces, place_q, place_k, pad, *outs_w],
        [
            kept((micros * kv_heads, group * span, keys)),
            kept((rows, width)),
            *[shape((micros, piece, 2 * half)) for _ in range(heads)],
        ],
        [pltpu.VMEM((keys, width), BF16), pltpu.VMEM((span, pad.shape[1]), BF16)],
        flops=4 * rows * width * (keys + half),
    )


def add_mid(x, terms, gains):
    def kernel(*refs):
        x_ref, gain = refs[0], refs[1]
        parts = refs[2 : 2 + len(terms)]
        mid, nb = refs[2 + len(terms) :]
        total = x_ref[...].astype(F32)
        for part in parts:
            total = total + part[...].astype(F32)
        mid[...] = total
        scale = lax.rsqrt(jnp.mean(total * total, axis=-1, keepdims=True) + EPSILON)
        nb[...] = (total * scale * gain[1:2, :]).astype(BF16)

    return call(
        kernel,
        "add_mid",
        [x, gains, *terms],
        [shape(x.shape, F32), shape(x.shape)],
        limit=VMEM_SMALL,
    )


def add_out(mid, terms):
    def kernel(*refs):
        total = refs[0][...]
        for part in refs[1:-1]:
            total = total + part[...].astype(F32)
        refs[-1][...] = total.astype(BF16)

    return call(kernel, "add_out", [mid, *terms], [shape(mid.shape)], limit=VMEM_SMALL)[0]


def blocks_of(pair, units):
    specs, arrays = [], []
    count = units // UNIT_BLOCK
    for part in range(3):
        for array in pair:
            specs.append(
                pl.BlockSpec(
                    (array.shape[0], UNIT_BLOCK), lambda j, part=part: (0, part * count + j)
                )
            )
            arrays.append(array)
    return specs, arrays


def pack_places(half, units, width):
    hidden_at = -(-2 * half // UNIT_BLOCK) * UNIT_BLOCK
    mix_at = -(-(hidden_at + units) // width) * width
    return hidden_at, mix_at


def feed(pieces, pair, units, na, mix):
    heads = len(pieces)
    micros, piece, d_model = pieces[0].shape
    rows = micros * heads * piece
    half = d_model // 2
    count = units // UNIT_BLOCK
    width = mix.shape[1]
    hidden_at, mix_at = pack_places(half, units, width)

    def kernel(*refs):
        xs = refs[:heads]
        gate_w = refs[heads : heads + 2]
        up_w = refs[heads + 2 : heads + 4]
        down_w = refs[heads + 4 : heads + 6]
        na_in, mix_in = refs[heads + 6 : heads + 8]
        gate_out, up_out, hidden_out, nb, packed = refs[heads + 8 : heads + 13]
        outs = refs[heads + 13 : 2 * heads + 13]
        total = refs[-1]
        j = pl.program_id(0)

        @pl.when(j == 0)
        def _():
            read_pieces(nb, xs, micros)
            total[...] = jnp.zeros_like(total)
            packed[:, :half] = na_in[...]
            packed[:, half : 2 * half] = nb[:, half:]
            packed[:, mix_at : mix_at + width] = mix_in[...]

        low, high = nb[:, :half], nb[:, half:]
        gate = dot(low, gate_w[0][...]) + dot(high, gate_w[1][...])
        up = dot(low, up_w[0][...]) + dot(high, up_w[1][...])
        gate_out[...] = gate.astype(BF16)
        up_out[...] = up.astype(BF16)
        hidden = (gate * jax.nn.sigmoid(gate) * up).astype(BF16)
        hidden_out[...] = hidden
        at = pl.multiple_of(hidden_at + j * UNIT_BLOCK, UNIT_BLOCK)
        packed[:, pl.ds(at, UNIT_BLOCK)] = hidden
        total[:, :half] += dot_nt(hidden, down_w[0][...])
        total[:, half:] += dot_nt(hidden, down_w[1][...])

        @pl.when(j == count - 1)
        def _():
            write_pieces(outs, total, micros)

    specs, arrays = blocks_of(pair, units)
    whole = pl.BlockSpec((rows, d_model), lambda j: (0, 0))
    block = pl.BlockSpec((rows, UNIT_BLOCK), lambda j: (0, j))
    rows_spec = pl.BlockSpec((micros, piece, d_model), lambda j: (0, 0, 0))
    return pl.pallas_call(
        kernel,
        grid=(count,),
        in_specs=[rows_spec] * heads
        + specs
        + [pl.BlockSpec((rows, half), lambda j: (0, 1)), pl.BlockSpec(mix.shape, lambda j: (0, 0))],
        out_specs=[block, block, block, whole]
        + [pl.BlockSpec((rows, mix_at + width), lambda j: (0, 0))]
        + [rows_spec] * heads,
        out_shape=[
            kept((rows, units)),
            kept((rows, units)),
            kept((rows, units)),
            kept((rows, d_model)),
            kept((rows, mix_at + width)),
            *[shape((micros, piece, d_model)) for _ in range(heads)],
        ],
        scratch_shapes=[pltpu.VMEM((rows, d_model), F32)],
        compiler_params=pltpu.CompilerParams(vmem_limit_bytes=VMEM_LARGE),
        cost_estimate=pl.CostEstimate(
            flops=6 * rows * d_model * units, bytes_accessed=6 * d_model * units, transcendentals=0
        ),
        name="feed",
    )(*pieces, *arrays, na, mix)


def feed_back(pieces, pair, gate, up):
    heads = len(pieces)
    micros, piece, d_model = pieces[0].shape
    rows, units = gate.shape
    half = d_model // 2
    count = units // UNIT_BLOCK
    back_at = -(-half // UNIT_BLOCK) * UNIT_BLOCK

    def kernel(*refs):
        xs = refs[:heads]
        gate_w = refs[heads : heads + 2]
        up_w = refs[heads + 2 : heads + 4]
        down_w = refs[heads + 4 : heads + 6]
        gate_in, up_in = refs[heads + 6 : heads + 8]
        d_gate_out, d_up_out, gf, packed = refs[heads + 8 : heads + 12]
        outs = refs[heads + 12 : 2 * heads + 12]
        total = refs[-1]
        j = pl.program_id(0)

        @pl.when(j == 0)
        def _():
            read_pieces(gf, xs, micros)
            total[...] = jnp.zeros_like(total)
            packed[:, :half] = gf[:, half:]

        d_hidden = dot(gf[:, :half], down_w[0][...]) + dot(gf[:, half:], down_w[1][...])
        gate_v, up_v = gate_in[...].astype(F32), up_in[...].astype(F32)
        sigma = jax.nn.sigmoid(gate_v)
        d_gate = (d_hidden * up_v * sigma * (1.0 + gate_v * (1.0 - sigma))).astype(BF16)
        d_up = (d_hidden * gate_v * sigma).astype(BF16)
        d_gate_out[...] = d_gate
        d_up_out[...] = d_up
        at = pl.multiple_of(back_at + j * UNIT_BLOCK, UNIT_BLOCK)
        packed[:, pl.ds(at, UNIT_BLOCK)] = d_gate
        at = pl.multiple_of(back_at + units + j * UNIT_BLOCK, UNIT_BLOCK)
        packed[:, pl.ds(at, UNIT_BLOCK)] = d_up
        total[:, :half] += dot_nt(d_gate, gate_w[0][...]) + dot_nt(d_up, up_w[0][...])
        total[:, half:] += dot_nt(d_gate, gate_w[1][...]) + dot_nt(d_up, up_w[1][...])

        @pl.when(j == count - 1)
        def _():
            write_pieces(outs, total, micros)

    specs, arrays = blocks_of(pair, units)
    whole = pl.BlockSpec((rows, d_model), lambda j: (0, 0))
    block = pl.BlockSpec((rows, UNIT_BLOCK), lambda j: (0, j))
    rows_spec = pl.BlockSpec((micros, piece, d_model), lambda j: (0, 0, 0))
    return pl.pallas_call(
        kernel,
        grid=(count,),
        in_specs=[rows_spec] * heads + specs + [block, block],
        out_specs=[block, block, whole]
        + [pl.BlockSpec((rows, back_at + 2 * units), lambda j: (0, 0))]
        + [rows_spec] * heads,
        out_shape=[
            kept((rows, units)),
            kept((rows, units)),
            kept((rows, d_model)),
            kept((rows, back_at + 2 * units)),
            *[shape((micros, piece, d_model)) for _ in range(heads)],
        ],
        scratch_shapes=[pltpu.VMEM((rows, d_model), F32)],
        compiler_params=pltpu.CompilerParams(vmem_limit_bytes=VMEM_LARGE),
        cost_estimate=pl.CostEstimate(
            flops=6 * rows * d_model * units, bytes_accessed=6 * d_model * units, transcendentals=0
        ),
        name="feed_back",
    )(*pieces, *arrays, gate, up)


def norm_back(terms, residual, gains, row, carried):
    d_model = residual.shape[-1]

    def kernel(*refs):
        res, gain, carry = refs[:3]
        parts = refs[3 : 3 + len(terms)]
        d_out, d_low, d_gain = refs[3 + len(terms) :]
        d_normed = parts[0][...].astype(F32)
        for part in parts[1:]:
            d_normed = d_normed + part[...].astype(F32)
        rows = res[...].astype(F32)
        scale = lax.rsqrt(jnp.mean(rows * rows, axis=-1, keepdims=True) + EPSILON)
        unit = rows * scale
        d_gain[...] = jnp.sum(jnp.sum(d_normed * unit, axis=0), axis=0, keepdims=True)
        d_unit = d_normed * gain[row : row + 1, :]
        total = carry[...].astype(F32) + scale * (
            d_unit - unit * jnp.mean(d_unit * unit, axis=-1, keepdims=True)
        )
        d_out[...] = total
        d_low[...] = total.astype(BF16)

    return call(
        kernel,
        "norm_back",
        [residual, gains, carried, *terms],
        [shape(residual.shape, F32), shape(residual.shape), shape((1, d_model), F32)],
        limit=VMEM_SMALL,
    )


def attend_back(pieces, outs_w, mix, prob, query, kv_pieces, pad, turn, cosine, sine, group):
    heads = len(pieces)
    micros, piece, d_model = pieces[0].shape
    span = heads * piece
    rows = micros * span
    half = d_model // 2
    ctxs = len(kv_pieces)
    width = query.shape[1]
    keys = ctxs * span
    kv_heads = pad.shape[1] // LANES // 2

    def kernel(*refs):
        xs = refs[:heads]
        w_own, w_other, mix_in, prob_in, q_ref = refs[heads : heads + 5]
        kvs = refs[heads + 5 : heads + 5 + ctxs]
        pads, turns, cos, sin = refs[heads + 5 + ctxs : heads + 9 + ctxs]
        ga, ga_other, dq_out = refs[heads + 9 + ctxs : heads + 12 + ctxs]
        outs = refs[heads + 12 + ctxs : heads + 12 + 2 * ctxs]
        kv_rows, d_kv, d_q = refs[heads + 12 + 2 * ctxs :]
        read_pieces(ga, xs, micros)
        ga_other[...] = ga[:, half:]
        d_mix = (dot(ga[:, :half], w_own[...]) + dot(ga[:, half:], w_other[...])).astype(BF16)
        for m in range(micros):
            for j in range(ctxs):
                kv_rows[j * span : (j + 1) * span, :] = kvs[j][m]
            here = slice(m * span, (m + 1) * span)
            kv = dot(kv_rows[...], pads[...]).astype(BF16)
            q = dot(q_ref[here, :], pads[...]).astype(BF16)
            d = dot(d_mix[here], pads[...])
            product = d * dot(mix_in[here, :], pads[...])
            d = d.astype(BF16)
            for a in range(kv_heads):
                cuts = [slice((a * group + g) * LANES, (a * group + g + 1) * LANES) for g in range(group)]
                q2 = jnp.concatenate([q[:, cut] for cut in cuts], axis=0)
                d2 = jnp.concatenate([d[:, cut] for cut in cuts], axis=0)
                delta = jnp.concatenate(
                    [jnp.sum(product[:, cut], axis=-1, keepdims=True) for cut in cuts], axis=0
                )
                key = kv[:, a * LANES : (a + 1) * LANES]
                value = kv[:, (kv_heads + a) * LANES : (kv_heads + a + 1) * LANES]
                share = prob_in[m * kv_heads + a]
                d_prob = dot_nt(d2, value)
                d_score = (share.astype(F32) * (d_prob - delta)).astype(BF16)
                back = dot(d_score, key)
                for g, cut in enumerate(cuts):
                    d_q[:, cut] = back[g * span : (g + 1) * span]
                d_kv[:, a * LANES : (a + 1) * LANES] = dot_tn(d_score, q2).astype(BF16)
                d_kv[:, (kv_heads + a) * LANES : (kv_heads + a + 1) * LANES] = dot_tn(
                    share, d2
                ).astype(BF16)
            packed = dot_nt(d_kv[...], pads[...]).astype(BF16)
            for j in range(ctxs):
                outs[j][m] = packed[j * span : (j + 1) * span]
            high, low = split_terms(d_q[...])
            line = (dot_nt(high, pads[...]) + dot_nt(low, pads[...])) * INV_ROOT
            high, low = split_terms(line)
            turned = dot_nt(high, turns[0]) + dot_nt(low, turns[0])
            dq_out[here, :] = (line * cos[here, :width] + turned * sin[here, :width]).astype(BF16)

    return call(
        kernel,
        "attend_back",
        [*pieces, *outs_w, mix, prob, query, *kv_pieces, pad, turn, cosine, sine],
        [
            kept((rows, d_model)),
            shape((rows, half)),
            shape((rows, width)),
            *[shape((micros, span, width)) for _ in range(ctxs)],
        ],
        [
            pltpu.VMEM((keys, width), BF16),
            pltpu.VMEM((keys, pad.shape[1]), BF16),
            pltpu.VMEM((span, pad.shape[1]), F32),
        ],
        flops=10 * rows * width * keys,
    )


def project_back(terms, dq, queries, kvs, turn, cosine, sine, row_pieces):
    heads = len(row_pieces)
    micros, span, width = terms[0].shape
    rows = micros * span
    piece = span // heads
    half = queries[0].array.shape[0]
    count = len(terms)

    def kernel(*refs):
        parts = refs[:count]
        dq_in, q_own, q_other, kv_own, kv_other, turns, cos, sin = refs[count : count + 8]
        xs = refs[count + 8 : count + 8 + heads]
        d_line, d_gain = refs[count + 8 + heads : count + 10 + heads]
        outs = refs[count + 10 + heads : count + 10 + 2 * heads]
        unit = refs[-1]
        for m in range(micros):
            for k in range(heads):
                x = xs[k][m].astype(F32)
                scale = lax.rsqrt(jnp.mean(x * x, axis=-1, keepdims=True) + EPSILON)
                at = (m * heads + k) * piece
                unit[at : at + piece, :] = x * scale
        d_line[:, :width] = dq_in[...]
        lanes = lax.broadcasted_iota(jnp.int32, (span, width), 1)
        scaled = jnp.where(lanes < width // 2, INV_ROOT, 1.0)
        for m in range(micros):
            here = slice(m * span, (m + 1) * span)
            total = parts[0][m].astype(F32)
            for part in parts[1:]:
                total = total + part[m].astype(F32)
            total = total * scaled
            high, low = split_terms(total)
            turned = dot_nt(high, turns[1]) + dot_nt(low, turns[1])
            d_line[here, width:] = (
                total * cos[here, width:] + turned * sin[here, width:]
            ).astype(BF16)
        for t, (wq, wkv) in enumerate(((q_own, kv_own), (q_other, kv_other))):
            branch = dot_nt(d_line[:, :width], wq[...]) + dot_nt(d_line[:, width:], wkv[...])
            side = slice(t * half, (t + 1) * half)
            d_gain[:, side] = jnp.sum(branch * unit[:, side], axis=0, keepdims=True)
            branch = branch.astype(BF16)
            for m in range(micros):
                for k in range(heads):
                    at = (m * heads + k) * piece
                    outs[k][m, :, t * half : (t + 1) * half] = branch[at : at + piece]

    return call(
        kernel,
        "project_back",
        [*terms, dq, *queries, *kvs, turn, cosine, sine, *row_pieces],
        [
            kept((rows, 2 * width)),
            shape((1, 2 * half), F32),
            *[shape((micros, piece, 2 * half)) for _ in range(heads)],
        ],
        [pltpu.VMEM((rows, 2 * half), F32)],
        flops=8 * rows * half * width,
    )


def weight_grad(groups):
    half = groups[0][0][0].width
    total = sum(group[0][1].width for group in groups)
    args = [view for group in groups for pair in group for view in pair]

    def kernel(*refs):
        out = refs[-1]
        at = 0
        for g, group in enumerate(groups):
            n = group[0][1].width
            a, b, c, d = refs[4 * g : 4 * g + 4]
            out[:, at : at + n] = (dot_tn(a[...], b[...]) + dot_tn(c[...], d[...])).astype(BF16)
            at += n

    rows = groups[0][0][0].array.shape[0]
    return call(
        kernel, "weight_grad", args, [shape((half, total))], flops=4 * half * rows * total
    )[0]


def late_grad(nb, gf, d_gate, d_up, hidden, packed, packed_back):
    rows, d_model = nb.shape
    units = hidden.shape[1]
    half = d_model // 2
    count = units // UNIT_BLOCK
    hidden_at, _ = pack_places(half, units, LANES)
    back_at = -(-half // UNIT_BLOCK) * UNIT_BLOCK

    def kernel(*refs):
        sides = refs[:4]
        lines = refs[4:10]
        out = refs[10]
        turned, line = refs[11:13], refs[13]
        j = pl.program_id(0)

        @pl.when(j == 0)
        def _():
            for k, side in enumerate(sides):
                turned[k % 2][:, k // 2 * rows : (k // 2 + 1) * rows] = side[...].T

        for part in range(3):

            @pl.when(j // count == part)
            def _(part=part):
                line[:rows, :] = lines[part][...]
                line[rows:, :] = lines[3 + part][...]
                out[...] = dot(turned[(0, 0, 1)[part]][...], line[...]).astype(BF16)

    def side(block):
        return pl.BlockSpec((rows, half), lambda j: (0, block))

    def line(part, first):
        return pl.BlockSpec(
            (rows, UNIT_BLOCK),
            lambda j: (0, first // UNIT_BLOCK + jnp.clip(j - part * count, 0, count - 1)),
        )

    return pl.pallas_call(
        kernel,
        grid=(3 * count,),
        in_specs=[side(0), side(0), side(1), side(0)]
        + [line(part, 0) for part in range(3)]
        + [line(0, back_at), line(1, back_at + units), line(2, hidden_at)],
        out_specs=pl.BlockSpec((half, UNIT_BLOCK), lambda j: (0, j)),
        out_shape=kept((half, 3 * units)),
        scratch_shapes=[pltpu.VMEM((half, 2 * rows), BF16)] * 2
        + [pltpu.VMEM((2 * rows, UNIT_BLOCK), BF16)],
        compiler_params=pltpu.CompilerParams(vmem_limit_bytes=VMEM_LARGE),
        cost_estimate=pl.CostEstimate(
            flops=12 * half * rows * units, bytes_accessed=6 * half * units, transcendentals=0
        ),
        name="late_grad",
    )(nb, gf, packed, packed_back, d_gate, d_up, hidden, packed_back, packed_back, packed)


def finish_late(lower, upper, units):
    size, _ = lower[0].shape
    count = units // UNIT_BLOCK

    def kernel(*refs):
        parts, outs = refs[:12], refs[12:]
        first = lax.axis_index("section") == 0
        for which in range(3):
            a0, a1, b0, b1 = (parts[4 * which + k][...].astype(F32) for k in range(4))
            top, low = jnp.where(first, a0, b0), jnp.where(first, a1, b1)
            if which < 2:
                outs[which][:size, :] = top
                outs[which][size:, :] = low
            else:
                outs[2][:, :size] = top.T
                outs[2][:, size:] = low.T

    specs, arrays = [], []
    for which in range(3):
        for array in (*lower, *upper):
            specs.append(
                pl.BlockSpec((size, UNIT_BLOCK), lambda j, which=which: (0, which * count + j))
            )
            arrays.append(array)
    flat = pl.BlockSpec((2 * size, UNIT_BLOCK), lambda j: (0, j))
    return pl.pallas_call(
        kernel,
        grid=(count,),
        in_specs=specs,
        out_specs=[flat, flat, pl.BlockSpec((UNIT_BLOCK, 2 * size), lambda j: (j, 0))],
        out_shape=[
            kept((2 * size, units), F32),
            kept((2 * size, units), F32),
            kept((units, 2 * size), F32),
        ],
        compiler_params=pltpu.CompilerParams(vmem_limit_bytes=VMEM_LARGE),
        cost_estimate=pl.CostEstimate(
            flops=0, bytes_accessed=48 * size * units, transcendentals=0
        ),
        name="finish_late",
    )(*arrays)


def finish_early(lower, upper, width, k_width):
    size, lines = lower[0].shape

    def kernel(*refs):
        a0, a1, b0, b1, query, key, value, out = refs
        first = lax.axis_index("section") == 0
        for t, (a, b) in enumerate(((a0, b0), (a1, b1))):
            rows = slice(t * size, (t + 1) * size)
            both = jnp.where(first, a[...].astype(F32), b[...].astype(F32))
            line = both[:, width:]
            query[rows, :] = line[:, :width]
            key[:, rows] = line[:, width : width + k_width].T
            value[:, rows] = line[:, width + k_width :].T
            out[:, rows] = both[:, :width].T

    return call(
        kernel,
        "finish_early",
        [*lower, *upper],
        [
            kept((2 * size, width), F32),
            kept((k_width, 2 * size), F32),
            kept((k_width, 2 * size), F32),
            kept((width, 2 * size), F32),
        ],
    )


def relative_columns(value, section, ctxs):
    width = value.shape[-1] // (2 * ctxs)
    return jnp.concatenate(
        [
            lax.dynamic_slice_in_dim(
                value, (k * 2 + (section ^ t)) * width, width, axis=value.ndim - 1
            )
            for t in range(2)
            for k in range(ctxs)
        ],
        axis=-1,
    )


def stored_columns(value, section, ctxs):
    width = value.shape[-1] // (2 * ctxs)
    return jnp.concatenate(
        [
            lax.dynamic_slice_in_dim(
                value, ((section ^ t) * ctxs + k) * width, width, axis=value.ndim - 1
            )
            for k in range(ctxs)
            for t in range(2)
        ],
        axis=-1,
    )


def send_all(pieces, axis):
    return [pieces[0]] + [swap(piece, axis, k) for k, piece in enumerate(pieces[1:], 1)]


def send_rows(rows):
    return send_all([rows] * lax.axis_size("head"), "head")


def send_blocks(rows):
    return send_all([rows] * lax.axis_size("ctx"), "ctx")


class Fetch:
    def __init__(self, shard):
        self.shard = shard

    def send(self, gate=None):
        self.pieces = send_blocks(self.shard if gate is None else after(self.shard, gate))

    def settle(self, gate=None):
        own = place(after(self.pieces, gate), lax.axis_index("ctx"))
        self.pair = (own, swap(own, "section", 1))
        return self.pair

    def direct(self, gate=None, with_rows=None):
        shard = self.shard if gate is None else after(self.shard, gate)
        pieces = send_blocks(shard)
        if with_rows is not None:
            pieces = after(pieces, with_rows)
        own = place(pieces, lax.axis_index("ctx"))
        self.pair = (own, swap(own, "section", 1))
        return pieces[1:]

    def first(self, gate=None):
        shard = self.shard if gate is None else after(self.shard, gate)
        self.own = lax.all_gather(shard, "ctx", axis=0, tiled=True)
        return self.own

    def second(self, gate=None):
        own = self.own if gate is None else after(self.own, gate)
        self.pair = (own, swap(own, "section", 1))
        return self.pair[1]


class Settle:
    def __init__(self, source):
        self.source = source

    def first(self, whole):
        self.kept = lax.psum_scatter(whole, "ctx", scatter_dimension=0, tiled=True)
        return whole

    def direct(self, whole, gate=None):
        if gate is not None:
            whole = after(whole, gate)
        ctxs = lax.axis_size("ctx")
        ctx = lax.axis_index("ctx")
        size = whole.shape[0] // ctxs
        parts = [
            lax.dynamic_slice_in_dim(whole, (ctx ^ k) * size, size, axis=0) for k in range(ctxs)
        ]
        total = None
        for term in send_all(parts, "ctx"):
            term = term.astype(F32)
            total = term if total is None else total + term
        self.kept = total.astype(BF16)
        return whole

    def second(self, gate=None):
        kept = self.kept if gate is None else after(self.kept, gate)
        self.kept = kept
        sent = swap_from(kept, self.source)
        self.halves = (kept, sent) if self.source == 1 else (sent, kept)
        return sent


class Chain:
    def __init__(self):
        self.tasks = {}
        self.due = {}

    def plan(self, start, end, task):
        self.tasks.setdefault(start, []).append((end, task))

    def enter(self, name, value):
        done = self.due.pop(name, [])
        return after(value, done) if done else value

    def leave(self, name, value):
        for end, task in self.tasks.pop(name, []):
            result = task(value)
            if end is not None:
                self.due.setdefault(end, []).append(result)


class Plan:
    pass


def pick(first, a, b):
    return jnp.where(first, a, b)


def turning(heads_turned, heads):
    turn = np.zeros((heads * HEAD_DIM, heads * HEAD_DIM), np.float32)
    for h in range(heads_turned):
        for i in range(HALF):
            turn[h * HEAD_DIM + HALF + i, h * HEAD_DIM + i] = -1.0
            turn[h * HEAD_DIM + i, h * HEAD_DIM + HALF + i] = 1.0
    return turn


def padding(heads):
    pad = np.zeros((heads * HEAD_DIM, heads * LANES), np.float32)
    for h in range(heads):
        for i in range(HEAD_DIM):
            pad[h * HEAD_DIM + i, h * LANES + i] = 1.0
    return pad


def local(
    layer_input,
    out_cotangent,
    block_order,
    gain_attn,
    w_query,
    w_key,
    w_value,
    w_out,
    gain_ffn,
    w_gate,
    w_up,
    w_down,
):
    section = lax.axis_index("section")
    head = lax.axis_index("head")
    ctx = lax.axis_index("ctx")
    heads = lax.axis_size("head")
    ctxs = lax.axis_size("ctx")
    first = section == 0
    micros_all = layer_input.shape[0] // 2
    micros = micros_all // GROUPS
    rows_dev = layer_input.shape[1]
    d_model = layer_input.shape[2]
    span = heads * rows_dev
    rows = micros * span
    block_rows = ctxs * span // block_order.shape[1]
    d_half = d_model // ctxs // 2
    width = w_query.shape[2]
    k_width = w_key.shape[2]
    units = w_gate.shape[2]
    group_size = width // k_width
    line_heads = width // HEAD_DIM
    chain = Chain()

    turn = jnp.asarray(
        np.stack([turning(line_heads, line_heads), turning(k_width // HEAD_DIM, line_heads)]), BF16
    )
    pad = jnp.asarray(padding(line_heads), BF16)

    def places_of(order, ctx_index):
        piece = jnp.arange(span, dtype=jnp.int32)
        stored = (ctx_index * heads + (head ^ (piece // rows_dev))) * rows_dev + piece % rows_dev
        block = stored // block_rows
        match = block[:, None] == jnp.arange(order.shape[1], dtype=jnp.int32)[None, :]
        base = jnp.sum(jnp.where(match[None], order[:, None, :], 0), axis=2)
        return base * block_rows + (stored % block_rows)[None]

    frequency = jnp.power(ROPE_BASE, jnp.arange(HALF, dtype=F32) * (-2.0 / HEAD_DIM))

    def group_of(index):
        group = Plan()
        at = section * micros_all + index * micros
        group.name = "ab"[index]
        order = lax.dynamic_slice_in_dim(block_order, at, micros, axis=0)
        places_q = places_of(order, ctx)
        places_k = jnp.concatenate([places_of(order, ctx ^ k) for k in range(ctxs)], axis=1)
        group.place_q = places_q[:, :, None]
        group.place_k = places_k[:, None, :]
        group.places = places_q

        def make_tables(places):
            angles = places.reshape(rows, 1).astype(F32) * frequency
            cosine, sine = jnp.cos(angles), jnp.sin(angles)
            turned = 2 * (line_heads + k_width // HEAD_DIM)
            fixed = width - k_width
            group.cosine = jnp.concatenate(
                [cosine] * turned + [jnp.ones((rows, fixed), F32)], axis=1
            )
            group.sine = jnp.concatenate(
                [sine] * turned + [jnp.zeros((rows, fixed), F32)], axis=1
            )

        group.make_tables = make_tables

        def mine(value):
            part = lax.dynamic_slice_in_dim(value, at, micros, axis=0)
            return relative_columns(part, section, ctxs)

        group.x = mine(layer_input)
        group.cot = mine(out_cotangent)
        group.keep, group.d_in = {}, {}
        return group

    members = [group_of(index) for index in range(GROUPS)]
    tail = members[-1].name
    for group in members:
        group.firsts = send_rows(group.x)
        group.cot_pieces = [group.cot] * heads

    def exchange(shard, gate=None):
        def cut(which):
            return lax.dynamic_slice_in_dim(shard, which * d_half, d_half, axis=0)

        kept, given = cut(section), cut(1 - section)
        if gate is not None:
            given = after(given, gate)
        taken = swap(given, "section", 1)
        return pick(first, kept, taken), pick(first, taken, kept)

    gains = jnp.stack([gain_attn[0], gain_ffn[0]], axis=1)
    gains = jnp.pad(gains, ((0, 0), (0, LANES - 2)))
    early_shards = exchange(
        jnp.concatenate([w_query[0], w_key[0], w_value[0], gains], axis=1)
    )
    early0 = Fetch(early_shards[0])
    early0.send([group.firsts[1] for group in members])
    tables = after([group.places for group in members], early0.pieces[1])
    for group, places in zip(members, tables):
        group.make_tables(places)
    early0.settle([(group.cosine, group.sine, group.firsts) for group in members])
    landed = early0.pair[:1]
    w_late, w_o = after(((w_gate[0], w_up[0], w_down[0]), w_out[0]), landed)
    out_shards = exchange(w_o.T)
    late_shards = exchange(jnp.concatenate([w_late[0], w_late[1], w_late[2].T], axis=1))
    late0, late1 = Fetch(late_shards[0]), Fetch(late_shards[1])
    out0 = Fetch(out_shards[0])
    both1 = Fetch(jnp.concatenate([out_shards[1], early_shards[1]], axis=1))
    late0.first(landed)
    out0.send(landed)

    def views0(name):
        if name == "o":
            return [View(part, width, 0) for part in out0.pair]
        at = {"q": (width, 0), "kv": (width, 1), "g": (LANES, 2 * width // LANES)}[name]
        return [View(part, *at) for part in early0.pair]

    def views1(name):
        at = {
            "o": (width, 0),
            "q": (width, 1),
            "kv": (width, 2),
            "g": (LANES, 3 * width // LANES),
        }[name]
        return [View(part, *at) for part in both1.pair]

    token = [None]

    def enter(name, group, value):
        if token[0] is not None and GROUPS > 1:
            value = after(value, token[0])
        return chain.enter(name + group.name, value)

    def leave(name, group, value):
        token[0] = value
        chain.leave(name + group.name, value)

    def forward(label, group, layer_in, views, late_fetch):
        keep = Plan()
        keep.x = layer_in
        pieces = group.firsts if label == "0" else send_rows(layer_in)
        leave(label + "F0", group, layer_in)
        yield
        pieces = enter(label + "F1", group, pieces)
        keep.x_pieces = pieces
        keep.na, keep.query, kv, keep.gains = project(
            pieces, views("q"), views("kv"), views("g"), group.cosine, group.sine, turn
        )
        kv = kv.reshape(micros, span, width)
        pieces = send_blocks(kv)
        leave(label + "F1", group, kv)
        yield
        keep.kv = enter(label + "F2", group, pieces)
        keep.prob, keep.mix, *parts = attend(
            keep.query, keep.kv, group.place_q, group.place_k, pad, views("o"),
            heads, rows_dev, group_size,
        )
        terms = send_all(parts, "head")
        leave(label + "F2", group, parts[0])
        yield
        terms = enter(label + "F3", group, terms)
        keep.mid, own_nb = add_mid(layer_in, terms, keep.gains)
        pieces = send_rows(own_nb)
        leave(label + "F3", group, own_nb)
        yield
        pieces = enter(label + "F4", group, pieces)
        keep.late = late_fetch.pair
        keep.gate, keep.up, keep.hidden, keep.nb, packed, *parts = feed(
            pieces, keep.late, units, keep.na, keep.mix
        )
        keep.packed = swap(packed, "section", 1)
        group.parts = parts
        group.keep[label] = keep
        leave(label + "F4", group, parts[0])
        if label == "0":
            terms = send_all(parts, "head")
            yield
            terms = enter(label + "F5", group, terms)
            group.out = add_out(keep.mid, terms)

    def backward(label, group, pieces, grad, views):
        keep = group.keep[label]
        if label == "0":
            pieces = enter(label + "B1", group, pieces)
        keep.d_gate, keep.d_up, keep.gf, packed, *parts = feed_back(
            pieces, keep.late, keep.gate, keep.up
        )
        keep.packed_back = swap(packed, "section", 1)
        terms = send_all(parts, "head")
        leave(label + "B1", group, parts[0])
        yield
        terms = enter(label + "B2", group, terms)
        d_mid, own_ga, keep.gain_b = norm_back(terms, keep.mid, keep.gains, 1, grad)
        pieces = send_rows(own_ga)
        leave(label + "B2", group, own_ga)
        yield
        pieces = enter(label + "B3", group, pieces)
        keep.ga, ga_other, dq, *parts = attend_back(
            pieces, views("o"), keep.mix, keep.prob, keep.query, keep.kv, pad, turn,
            group.cosine, group.sine, group_size,
        )
        terms = send_all(parts, "ctx")
        keep.ga_other = swap(ga_other, "section", 1)
        leave(label + "B3", group, parts[0])
        yield
        terms = enter(label + "B4", group, terms)
        keep.d_line, keep.gain_a, *parts = project_back(
            terms, dq, views("q"), views("kv"), turn, group.cosine, group.sine, keep.x_pieces
        )
        terms = send_all(parts, "head")
        keep.d_line_other = swap(keep.d_line, "section", 1)
        leave(label + "B4", group, parts[0])
        leave(label + "B4z", group, terms[1])
        yield
        terms = enter(label + "B5", group, terms)
        d_input, d_low, _ = norm_back(terms, keep.x, keep.gains, 0, d_mid)
        if label == "1":
            group.d_in[label] = d_low
            group.pieces = send_rows(d_low)
        else:
            group.d_in[label] = d_input
        leave(label + "B5", group, group.d_in[label])
        yield

    def drive(*stages):
        waiting = list(stages)
        while waiting:
            waiting = [stage for stage in waiting if next(stage, stage) is not stage]

    def gather_cot(group, which):
        def task(gate):
            for k in which:
                if k < heads:
                    group.cot_pieces[k] = swap(after(group.cot, gate), "head", k)
            return group.cot_pieces[1:]

        return task

    for group in members:
        chain.plan("0F1" + group.name, "0F2" + group.name, gather_cot(group, [2, 1]))
        chain.plan("1F1" + group.name, "1F2" + group.name, gather_cot(group, range(3, heads)))

    def on_last(start, end, task):
        chain.plan(start + tail, end + tail if end else None, task)

    on_last("0F1", "0F2", out0.settle)
    on_last("0F3", None, late0.second)
    on_last("0F3", None, lambda gate: both1.first(late0.pair[0]))
    on_last("1F0", None, both1.second)
    on_last("1F0", None, lambda gate: late1.first(both1.pair[0]))
    on_last("1F3", None, late1.second)
    drive(*(forward("0", group, group.x, views0, late0) for group in members))

    def scatter_out(group, which):
        def task(gate):
            group.terms += [
                swap(after(group.parts[k], gate), "head", k) for k in which if k < heads
            ]
            return group.terms[1:]

        return task

    def finish_out(group):
        def task(gate):
            group.final = add_out(group.keep["1"].mid, group.terms)
            return group.final

        return task

    drive(*(forward("1", group, group.out, views1, late1) for group in members))
    for group in members:
        group.terms = [group.parts[0]]
        chain.plan("1B3" + group.name, "1B4" + group.name, scatter_out(group, [2, 1]))
        chain.plan("0B3" + group.name, "0B4" + group.name, scatter_out(group, range(3, heads)))
        chain.plan("0B5" + group.name, None, finish_out(group))

    _, mix_at = pack_places(d_model // 2, units, width)

    def rows_of(label, *names):
        def joined(name):
            parts = [getattr(group.keep[label], name) for group in members]
            return parts[0] if len(parts) == 1 else jnp.concatenate(parts, axis=0)

        return [joined(name) for name in names]

    def late_of(label, gate):
        names = ("nb", "gf", "d_gate", "d_up", "hidden", "packed", "packed_back")
        return late_grad(*after(rows_of(label, *names), gate))

    def out_group(ga, mix, ga_other, packed):
        return (
            (View(ga, d_model // 2, 0), View(mix)),
            (View(ga_other), View(packed, width, mix_at // width)),
        )

    def early_group(na, d_line, packed, d_line_other):
        return (
            (View(na, d_model // 2, 0), View(d_line)),
            (View(packed, d_model // 2, 0), View(d_line_other)),
        )

    out_names = ("ga", "mix", "ga_other", "packed")
    early_names = ("na", "d_line", "packed", "d_line_other")

    def out_of(label, gate):
        return weight_grad([out_group(*after(rows_of(label, *out_names), gate))])

    def early_of(label, gate):
        return weight_grad([early_group(*after(rows_of(label, *early_names), gate))])

    def both_of(label, gate):
        values = after(rows_of(label, *out_names, *early_names), gate)
        return weight_grad([out_group(*values[:4]), early_group(*values[4:])])

    late_1, both_1, late_0, both_0 = (Settle(s) for s in (0, 0, 1, 1))
    on_last("1B2", "1B3", lambda gate: late_1.first(late_of("1", gate)))
    on_last("1B5", "0B1", late_1.second)
    on_last("1B5", "0B1", lambda gate: both_1.first(both_of("1", (gate, late_1.kept))))
    on_last("0B2", "0B3", both_1.second)
    on_last("0B2", "0B3", lambda gate: late_0.first(late_of("0", (gate, both_1.kept))))
    on_last("0B5", None, late_0.second)
    late_done = []

    def finish(gate):
        late_done.append(finish_late(late_0.halves, late_1.halves, units))
        return late_done[0]

    on_last("0B5", None, finish)
    on_last("0B5", None, lambda gate: both_0.second(late_done[0]))
    last = []

    def last_grad(gate):
        last.append(both_0.first(both_of("0", gate)))
        return last[0]

    on_last("0B4", "0B5", last_grad)

    gain_mine = []

    def sum_gains(gate):
        def gain_of(label, name):
            total = getattr(members[0].keep[label], name)
            for group in members[1:]:
                total = total + getattr(group.keep[label], name)
            return total[0]

        gain_rows = jnp.stack(
            [gain_of(label, name) for label in "01" for name in ("gain_a", "gain_b")]
        )
        gain_rows = after(gain_rows, gate)
        half = d_model // 2
        got = swap(pick(first, gain_rows[2:], gain_rows[:2]), "section", 1)
        got = jnp.concatenate([got[:, half:], got[:, :half]], axis=1)
        blocks = (pick(first, gain_rows[:2], gain_rows[2:]) + got).reshape(4, ctxs, d_half)

        def sum_over(values):
            total = values[0]
            for value in values[1:]:
                total = total + value
            return total

        mine = [
            lax.dynamic_index_in_dim(blocks, ctx ^ k, 1, keepdims=False) for k in range(ctxs)
        ]
        part = sum_over(send_all(mine, "ctx"))
        part = sum_over(send_all([part] * heads, "head")).reshape(2, 2, d_half)
        part = pick(first, part, part[:, ::-1])
        gain_mine.append(part.reshape(2, 2 * d_half))
        return gain_mine[0]

    def by_layer(lower, upper):
        lower = stored_columns(lower, section, ctxs)
        upper = stored_columns(upper, section, ctxs)
        kept_rows = pick(first, lower, upper)
        got_rows = swap(pick(first, upper, lower).astype(BF16), "section", 1).astype(lower.dtype)
        return jnp.concatenate(
            [pick(first, kept_rows, got_rows), pick(first, got_rows, kept_rows)], axis=0
        )[None]

    def all_rows(name):
        parts = [name(group) for group in members]
        return parts[0] if len(parts) == 1 else jnp.concatenate(parts, axis=0)

    layer_outs = []

    def out_rows(gate):
        lower, upper = after((all_rows(lambda g: g.out), all_rows(lambda g: g.final)), gate)
        layer_outs.append(by_layer(lower, upper))
        return layer_outs[0]

    on_last("0B5", None, out_rows)
    on_last("0B5", None, lambda gate: sum_gains((gate, last[0])))
    drive(*(backward("1", group, group.cot_pieces, group.cot, views1) for group in members))
    drive(*(backward("0", group, group.pieces, group.d_in["1"], views0) for group in members))

    g_query, g_key, g_value, g_out = finish_early(
        both_0.halves, both_1.halves, width, k_width
    )
    g_key, g_value = g_key.T, g_value.T
    g_gate, g_up, g_down = late_done[0]
    in_grad = by_layer(
        all_rows(lambda g: g.d_in["0"]), all_rows(lambda g: g.d_in["1"]).astype(F32)
    )
    return (
        layer_outs[0],
        in_grad,
        gain_mine[0][0][None],
        g_query[None],
        g_key[None],
        g_value[None],
        g_out[None],
        gain_mine[0][1][None],
        g_gate[None],
        g_up[None],
        g_down[None],
    )


def solution(mesh):
    row_spec = P(None, ("ctx", "head"), None)
    vector = P("section", "ctx")
    tall = P("section", "ctx", "head")
    wide = P("section", "head", "ctx")
    kept_rows = P("section", None, ("ctx", "head"), None)
    return jax.shard_map(
        local,
        mesh=mesh,
        in_specs=(row_spec, row_spec, P(), vector, tall, tall, tall, wide, vector, tall, tall, wide),
        out_specs=(kept_rows, kept_rows, vector, tall, tall, tall, wide, vector, tall, tall, wide),
        check_vma=False,
    )
```
